128 devices in a mesh: row: 16 (over x, y), col: 8 (over z, core).
Axes of the slice: x: 4, y: 4, z: 4, core: 2. Of those that a mesh axis runs over, the one named last changes fastest.
Arguments:
- basis_in: bfloat16 [131072, 128], P(('row', 'col')), may hold values from -6 to 6
- tiles: bfloat16 [20480, 256, 256], P(('row', 'col'))
- tile_coords: int32 [20480, 2], P(('row', 'col')), may hold values from 0 to 511, as said below
- tile_count: int32 [128], P(('row', 'col')), may hold values from 40 to 160, as said below
Outputs:
- basis_out: float32 [131072, 128], P(('row', 'col'))
- factor: float32 [128, 128], replicated
The draws below stay inside these ranges and needn't reach their ends.
Inputs may be any that keep to these rules, and one draw needn't show every extreme that they name: `tile_coords`: slots d*160 to (d+1)*160 - 1 belong to device d of the row+col order (d = row index * 8 + col index). Pairs are distinct within a device; the block row lies in [r*8*4, (r+1)*8*4) for the device's row index r; the block column b satisfies (b // 4) mod 8 == the device's col index. Unused slots hold pairs of the same kind. `tile_count`: used slots are the leading ones of each device; 160 is reached by some devices in every draw.
All inputs are finite; a program needn't handle non-finite values.
Results may differ from the reference program's by a relative error of at most 0.0019.
Values may be sent and summed in bfloat16 or wider, within the bound.
No kernel may reach another device: no remote copies, remote signals or barrier semaphores. Data moves between devices by JAX's collectives and lax.ppermute only.
A program may use at most 192 MiB of HBM per device.

```python
import jax
import jax.numpy as jnp
from jax import lax

TILE = 256
RANK = 128
BPD = 4
TMAX = 160
ENT = 131072
N_ROW = 16
N_COL = 8
DEVICES = 128


def tile_layout(key):
    cells = N_COL * BPD * N_ROW * BPD
    keys = jax.random.split(key, DEVICES)
    picked = jax.vmap(lambda one: jax.random.permutation(one, cells)[:TMAX])(keys)
    local_row = picked // (N_ROW * BPD)
    local_col = picked % (N_ROW * BPD)
    device = jnp.arange(DEVICES, dtype=jnp.int32)
    row_group = (device // N_COL)[:, None]
    col_group = (device % N_COL)[:, None]
    block_row = row_group * (N_COL * BPD) + local_row
    block_col = (local_col // BPD * N_COL + col_group) * BPD + local_col % BPD
    return jnp.stack([block_row, block_col], axis=-1).reshape(DEVICES * TMAX, 2).astype(jnp.int32)


def draw_tile_coords(key, part):
    return tile_layout(key)


def draw_tiles(key, part):
    coords = tile_layout(key)
    key = jax.random.fold_in(key, 7)
    block_col = coords[:, 1]
    upper = block_col // (N_COL * BPD)
    lower = block_col // BPD % N_COL
    spread = (1.0 + 2.0 * lower.astype(jnp.float32) / (N_COL - 1)) * (1.0 + 2.0 * upper.astype(jnp.float32) / (N_ROW - 1)) / 4.0
    sigma = (2.5 * BPD / (TMAX * TILE)) ** 0.5
    shape = (DEVICES * TMAX, TILE, TILE)
    values = jax.random.normal(key, shape, jnp.float32)
    return (values * sigma * spread[:, None, None]).astype(jnp.bfloat16)


def draw_tile_count(key, part):
    key = jax.random.fold_in(key, 5)
    first, second = jax.random.split(key)
    counts = TMAX // 4 + jax.random.randint(first, (DEVICES,), 0, TMAX // 4 + 1)
    heavy = jax.random.permutation(second, DEVICES)[:4]
    return counts.at[heavy].set(TMAX).astype(jnp.int32)


def steps_of(key, extent, cuts, smallest, top_value):
    def one(axis_at, parts):
        steps = jax.random.uniform(jax.random.fold_in(jax.random.fold_in(key, 6), axis_at), (parts,), jnp.float32, smallest / len(cuts), top_value / len(cuts))
        return jnp.repeat(jnp.exp(steps), extent[axis_at] // parts).reshape((-1,) + (1,) * (len(extent) - axis_at - 1))

    factor_of = one(*cuts[0])
    for cut in cuts[1:]:
        factor_of = factor_of * one(*cut)
    return factor_of


def normal_values(stream_key, shape, scale, bound, cuts=(), kind=jnp.bfloat16):
    result = scale * jax.random.normal(stream_key, shape, jnp.float32)
    if cuts:
        result = result * steps_of(stream_key, shape, cuts, -0.22, 0.18)
    return jnp.clip(result, -bound, bound).astype(kind)


def setup_inputs(seed: int = 0) -> dict:
    splits = jax.random.split(jax.random.key(seed), 5)
    basis_in = normal_values(splits[0], (ENT, RANK), 1.0, 6.0, ((0, 128),))
    tiles = draw_tiles(jax.random.fold_in(splits[4], 71), 0)
    tile_coords = draw_tile_coords(jax.random.fold_in(splits[4], 71), 0)
    tile_count = draw_tile_count(jax.random.fold_in(splits[4], 71), 0)
    return {"basis_in": basis_in, "tiles": tiles, "tile_coords": tile_coords, "tile_count": tile_count}


def reference(basis_in, tiles, tile_coords, tile_count):
    ent = basis_in.shape[0]
    blocks = ent // TILE
    slots = jnp.arange(DEVICES * TMAX, dtype=jnp.int32)
    used = slots % TMAX < jnp.repeat(tile_count, TMAX)
    weight = used.astype(jnp.float32).reshape(DEVICES, TMAX)
    tile_sets = tiles.reshape(DEVICES, TMAX, TILE, TILE)
    rows_all = tile_coords[:, 0].reshape(DEVICES, TMAX)
    cols_all = tile_coords[:, 1].reshape(DEVICES, TMAX)
    source = basis_in.reshape(blocks, TILE, RANK).astype(jnp.float32)

    def forward(total, pieces):
        tile_set, rows_one, cols_one, mask = pieces
        chosen = source[cols_one]
        product = jnp.einsum('tab,tbk->tak', tile_set.astype(jnp.float32), chosen)
        return (total.at[rows_one].add(product * mask[:, None, None]), None)
    inner, _ = lax.scan(forward, jnp.zeros((blocks, TILE, RANK), jnp.float32), (tile_sets, rows_all, cols_all, weight))
    inner = inner.astype(jnp.bfloat16).astype(jnp.float32)

    def backward(total, pieces):
        tile_set, rows_one, cols_one, mask = pieces
        chosen = inner[rows_one]
        product = jnp.einsum('tab,tak->tbk', tile_set.astype(jnp.float32), chosen)
        return (total.at[cols_one].add(product * mask[:, None, None]), None)
    outer, _ = lax.scan(backward, jnp.zeros((blocks, TILE, RANK), jnp.float32), (tile_sets, rows_all, cols_all, weight))
    outer = outer.reshape(ent, RANK)
    gram_one = jnp.dot(outer.T, outer, precision=lax.Precision.HIGHEST)
    lower_one = jnp.linalg.cholesky(gram_one)
    first = jax.scipy.linalg.solve_triangular(lower_one, outer.T, lower=True).T
    scale = jnp.sqrt(jnp.float32(ent))
    factor = lower_one.T / scale
    return (first * scale, factor)
```

```python
import jax
import jax.numpy as jnp
from jax import lax
from jax.experimental import pallas as pl
from jax.experimental.pallas import tpu as pltpu
from jax.sharding import Mesh, PartitionSpec as P

AXES = ("x", "y", "z", "core")
SIZES = {"x": 4, "y": 4, "z": 4, "core": 2}
SIDE = 256
RANK = 128
CHUNK = 8
F32 = jnp.float32
BF16 = jnp.bfloat16


def send(array, axis, step):
    size = SIZES[axis]
    return lax.ppermute(array, axis, [(i, (i + step) % size) for i in range(size)])


def limits(mib):
    return pltpu.CompilerParams(vmem_limit_bytes=mib * 1024 * 1024)


def whole(count):
    return [pl.BlockSpec(memory_space=pltpu.VMEM)] * count


def load_pieces(pieces, held, sems):
    copies = []
    at = 0
    for i, piece in enumerate(pieces):
        rows = piece.shape[0]
        copies.append(pltpu.make_async_copy(piece, held.at[pl.ds(at, rows)], sems.at[i]))
        at += rows
    for copy in copies:
        copy.start()
    return copies


def forward_kernel(count, row_at, col_at, tiles, *rest):
    pieces, (keep, away, held, total, sems, out_sems) = rest[:8], rest[8:]
    step = pl.program_id(0)

    @pl.when(step == 0)
    def _():
        copies = load_pieces(pieces, held, sems)
        total[...] = jnp.zeros_like(total)
        for copy in copies:
            copy.wait()

    @pl.when(step * CHUNK < count[0])
    def _():
        for k in range(CHUNK):
            slot = step * CHUNK + k
            row = row_at[slot]
            col = col_at[slot]
            total[row] += jnp.dot(tiles[k], held[col], preferred_element_type=F32)

    @pl.when(step == pl.num_programs(0) - 1)
    def _():
        half = keep.shape[0]
        one = pltpu.make_async_copy(total.at[pl.ds(half, half)], away, out_sems.at[0])
        two = pltpu.make_async_copy(total.at[pl.ds(0, half)], keep, out_sems.at[1])
        one.start()
        two.start()
        one.wait()
        two.wait()


def tile_spec():
    def index(step, count, row_at, col_at):
        return (jnp.minimum(step, (count[0] - 1) // CHUNK), 0, 0)

    return pl.BlockSpec((CHUNK, SIDE, SIDE), index)


def forward(count, row_at, col_at, tiles, pieces):
    slots = tiles.shape[0]
    any_spec = pl.BlockSpec(memory_space=pl.ANY)
    half = jax.ShapeDtypeStruct((16, SIDE, RANK), F32)
    return pl.pallas_call(
        forward_kernel,
        out_shape=(half, half),
        grid_spec=pltpu.PrefetchScalarGridSpec(
            num_scalar_prefetch=3,
            grid=(slots // CHUNK,),
            in_specs=[tile_spec()] + [any_spec] * 8,
            out_specs=(any_spec, any_spec),
            scratch_shapes=[
                pltpu.VMEM((64, SIDE, RANK), BF16),
                pltpu.VMEM((33, SIDE, RANK), F32),
                pltpu.SemaphoreType.DMA((8,)),
                pltpu.SemaphoreType.DMA((2,)),
            ],
        ),
        compiler_params=limits(32),
        name="forward",
    )(count, row_at, col_at, tiles, *pieces)


def backward_kernel(count, row_at, col_at, tiles, *rest):
    pieces, keep, aways, (held, total, sems) = rest[:8], rest[8], rest[9:15], rest[15:]
    step = pl.program_id(0)

    @pl.when(step == 0)
    def _():
        copies = load_pieces(pieces, held, sems)
        total[...] = jnp.zeros_like(total)
        for copy in copies:
            copy.wait()

    @pl.when(step * CHUNK < count[0])
    def _():
        for k in range(CHUNK):
            slot = step * CHUNK + k
            row = row_at[slot]
            col = col_at[slot]
            total[col] += jnp.dot(held[row], tiles[k], preferred_element_type=F32)

    @pl.when(step == pl.num_programs(0) - 1)
    def _():
        for h in range(2):
            keep[h] = total[pl.ds(32 * h, 8)]
            for d in range(3):
                aways[3 * h + d][...] = total[pl.ds(32 * h + 8 * (d + 1), 8)].astype(BF16)


def backward(count, row_at, col_at, tiles, pieces):
    slots = tiles.shape[0]
    any_spec = pl.BlockSpec(memory_space=pl.ANY)
    part = jax.ShapeDtypeStruct((8, RANK, SIDE), BF16)
    return pl.pallas_call(
        backward_kernel,
        out_shape=(jax.ShapeDtypeStruct((2, 8, RANK, SIDE), F32),) + (part,) * 6,
        grid_spec=pltpu.PrefetchScalarGridSpec(
            num_scalar_prefetch=3,
            grid=(slots // CHUNK,),
            in_specs=[tile_spec()] + [any_spec] * 8,
            out_specs=tuple(whole(7)),
            scratch_shapes=[
                pltpu.VMEM((32, RANK, SIDE), BF16),
                pltpu.VMEM((65, RANK, SIDE), F32),
                pltpu.SemaphoreType.DMA((8,)),
            ],
        ),
        compiler_params=limits(40),
        name="backward",
    )(count, row_at, col_at, tiles, *pieces)


def core_sum_kernel(keep, came, *outs):
    for d in range(4):
        at = pl.ds(4 * d, 4)
        outs[d][...] = keep[at] + came[at]


def core_sum(keep, came):
    part = jax.ShapeDtypeStruct((4, SIDE, RANK), F32)
    return pl.pallas_call(
        core_sum_kernel,
        out_shape=(part,) * 4,
        in_specs=whole(2),
        out_specs=tuple(whole(4)),
        compiler_params=limits(16),
        name="core_sum",
    )(keep, came)


def inner_kernel(a, b, c, d, out):
    for i in range(out.shape[0]):
        summed = (a[i] + b[i]) + (c[i] + d[i])
        out[i] = summed.T.astype(BF16)


def inner_sum(parts):
    return pl.pallas_call(
        inner_kernel,
        out_shape=jax.ShapeDtypeStruct((4, RANK, SIDE), BF16),
        in_specs=whole(4),
        out_specs=whole(1)[0],
        compiler_params=limits(16),
        name="inner_sum",
    )(*parts)


def middle_kernel(keep, *rest):
    came, next_keep, aways = rest[:6], rest[6], rest[7:]
    for h in range(2):
        for d in range(4):
            at = pl.ds(2 * d, 2)
            total = keep[h, at]
            for one in came[3 * h : 3 * h + 3]:
                total += one[at].astype(F32)
            if d == 0:
                next_keep[h] = total
            else:
                aways[3 * h + d - 1][...] = total.astype(BF16)


def middle_sum(keep, came):
    part = jax.ShapeDtypeStruct((2, RANK, SIDE), BF16)
    return pl.pallas_call(
        middle_kernel,
        out_shape=(jax.ShapeDtypeStruct((2, 2, RANK, SIDE), F32),) + (part,) * 6,
        in_specs=whole(7),
        out_specs=tuple(whole(7)),
        compiler_params=limits(16),
        name="middle_sum",
    )(keep, *came)


def exact_dot(a, b, dims):
    return lax.dot_general(
        a, b, (dims, ((), ())), precision=lax.Precision.HIGHEST, preferred_element_type=F32
    )


def outer_kernel(keep, *rest):
    came, outer, gram = rest[:6], rest[6], rest[7]
    gram_total = jnp.zeros((RANK, RANK), F32)
    for h in range(2):
        for b in range(2):
            total = keep[h, b]
            for one in came[3 * h : 3 * h + 3]:
                total += one[b].astype(F32)
            outer[2 * h + b] = total
            gram_total += exact_dot(total, total, ((1,), (1,)))
    gram[...] = gram_total


def outer_sum(keep, came):
    return pl.pallas_call(
        outer_kernel,
        out_shape=(
            jax.ShapeDtypeStruct((4, RANK, SIDE), F32),
            jax.ShapeDtypeStruct((RANK, RANK), F32),
        ),
        in_specs=whole(7),
        out_specs=tuple(whole(2)),
        compiler_params=limits(16),
        name="outer_sum",
    )(keep, *came)


def finish_kernel(scale, gram, outer, basis, factor, work):
    rows = lax.broadcasted_iota(jnp.int32, (RANK, RANK), 0)
    cols = lax.broadcasted_iota(jnp.int32, (RANK, RANK), 1)
    work[:, :RANK] = gram[...]
    work[:, RANK:] = jnp.where(rows == cols, 1.0, 0.0)
    sub = lax.broadcasted_iota(jnp.int32, (8, 2 * RANK), 0)
    for j in range(0, RANK, 8):
        panel = work[j : j + 8, :]
        for i in range(8):
            column = panel[:, j + i : j + i + 1]
            pivot = panel[i : i + 1, j + i : j + i + 1]
            root = lax.rsqrt(pivot)
            root = root * (1.5 - 0.5 * pivot * root * root)
            row = panel[i : i + 1, :] * root
            panel = jnp.where(
                sub == i, row, jnp.where(sub > i, panel - (column * root) * row, panel)
            )
        work[j : j + 8, :] = panel
        if j + 8 < RANK:
            lower = panel[:, :RANK]
            update = exact_dot(lower, panel, ((0,), (0,)))
            work[j + 8 :, :] -= update[j + 8 :, :]
    factor[...] = jnp.where(cols >= rows, work[:, :RANK], 0.0) * (1.0 / scale)
    inverse = work[:, RANK:] * scale
    for b in range(outer.shape[0]):
        basis[pl.ds(b * SIDE, SIDE), :] = exact_dot(outer[b], inverse, ((0,), (1,)))


def finish(gram, outer, entities):
    scale = float(entities) ** 0.5

    def kernel(*refs):
        finish_kernel(scale, *refs)

    return pl.pallas_call(
        kernel,
        out_shape=(
            jax.ShapeDtypeStruct((4 * SIDE, RANK), F32),
            jax.ShapeDtypeStruct((RANK, RANK), F32),
        ),
        in_specs=whole(2),
        out_specs=tuple(whole(2)),
        scratch_shapes=[pltpu.VMEM((RANK, 2 * RANK), F32)],
        compiler_params=limits(16),
        name="finish",
    )(gram, outer)


def shards(basis_in, tiles, tile_coords, tile_count):
    x, y, z, core = (lax.axis_index(name) for name in AXES)
    slots = tiles.shape[0]
    used = jnp.arange(slots, dtype=jnp.int32) < tile_count[0]
    local_row = tile_coords[:, 0] - (x * 4 + y) * 32
    dz = (local_row // 8 - z) % 4
    dc = (local_row // 4 - core) % 2
    row_at = dc * 16 + dz * 4 + local_row % 4
    row_group = tile_coords[:, 1] // 32
    b = tile_coords[:, 1] % 4
    dx = (row_group // 4 - x) % 4
    dy = (row_group % 4 - y) % 4
    col_at = jnp.where(b < 2, dy * 8 + dx * 2 + b, 32 + dx * 8 + dy * 2 + b - 2)

    with jax.named_scope("gather_basis"):
        halves = (basis_in[: 2 * SIDE], basis_in[2 * SIDE :])
        orders = (("x", "y"), ("y", "x"))
        firsts = [
            jnp.concatenate([half] + [send(half, order[0], -d) for d in (1, 2, 3)], axis=0)
            for half, order in zip(halves, orders)
        ]
        pieces = []
        for first, order in zip(firsts, orders):
            pieces += [first] + [send(first, order[1], -d) for d in (1, 2, 3)]
        pieces = [piece.reshape(8, SIDE, RANK) for piece in pieces]

    keep, away = forward(tile_count, jnp.where(used, row_at, 32), col_at, tiles, pieces)

    with jax.named_scope("reduce_inner"):
        came = send(away, "core", 1)
        sums = core_sum(keep, came)
        inner = inner_sum([sums[0]] + [send(sums[d], "z", d) for d in (1, 2, 3)])

    with jax.named_scope("gather_inner"):
        mine = [inner] + [send(inner, "z", -d) for d in (1, 2, 3)]
        theirs = [send(one, "core", 1) for one in mine]

    keep, *aways = backward(
        tile_count, row_at, jnp.where(used, col_at, 64), tiles, mine + theirs
    )

    with jax.named_scope("reduce_outer"):
        back = ("y",) * 3 + ("x",) * 3
        steps = (1, 2, 3) * 2
        came = [send(a, axis, d) for a, axis, d in zip(aways, back, steps)]
        keep, *aways = middle_sum(keep, came)
        forth = ("x",) * 3 + ("y",) * 3
        came = [send(a, axis, d) for a, axis, d in zip(aways, forth, steps)]
        outer, gram = outer_sum(keep, came)

    with jax.named_scope("reduce_gram"):
        gram = gram + send(gram, "core", 1)
        for axis in ("z", "y", "x"):
            parts = [send(gram, axis, d) for d in (1, 2, 3)]
            gram = (gram + parts[1]) + (parts[0] + parts[2])

    entities = basis_in.shape[0] * 128
    return finish(gram, outer, entities)


def solution(mesh):
    split = Mesh(mesh.devices.reshape(4, 4, 4, 2), AXES)
    placed = (P(AXES, None), P(AXES, None, None), P(AXES, None), P(AXES))
    return jax.shard_map(
        shards,
        mesh=split,
        in_specs=placed,
        out_specs=(P(AXES, None), P()),
        check_vma=False,
    )
```

```python
import jax
import jax.numpy as jnp
from jax import lax
from jax.experimental import pallas as pl
from jax.experimental.pallas import tpu as pltpu
from jax.sharding import Mesh, PartitionSpec as P

AXES = ("x", "y", "z", "core")
SIZES = {"x": 4, "y": 4, "z": 4, "core": 2}
SIDE = 256
RANK = 128
CHUNK = 20
WINDOW = 3
F32 = jnp.float32
BF16 = jnp.bfloat16


def send(array, axis, step):
    size = SIZES[axis]
    return lax.ppermute(array, axis, [(i, (i + step) % size) for i in range(size)])


def limits(mib):
    return pltpu.CompilerParams(vmem_limit_bytes=mib * 1024 * 1024)


def whole(count):
    return [pl.BlockSpec(memory_space=pltpu.VMEM)] * count


def load_pieces(pieces, held, sems):
    copies = []
    at = 0
    for i, piece in enumerate(pieces):
        rows = piece.shape[0]
        copies.append(pltpu.make_async_copy(piece, held.at[pl.ds(at, rows)], sems.at[i]))
        at += rows
    for copy in copies:
        copy.start()
    return copies


def tile_window(count, tiles, window, sems):
    chunks = (count[0] + CHUNK - 1) // CHUNK

    def copy(i):
        at = pl.ds(i * CHUNK, CHUNK)
        return pltpu.make_async_copy(tiles.at[at], window.at[at], sems.at[i])

    def start(i):
        @pl.when(i < chunks)
        def _():
            copy(i).start()

    return chunks, copy, start


def forward_kernel(count, row_at, col_at, tiles, *rest):
    pieces, (keep, away, held, total, window, sems, tile_sems) = rest[:8], rest[8:]
    chunks, copy, start = tile_window(count, tiles, window, tile_sems)
    copies = load_pieces(pieces, held, sems)
    for i in range(WINDOW):
        start(i)
    total[...] = jnp.zeros_like(total)
    for one in copies:
        one.wait()

    def body(i, _):
        copy(i).wait()
        start(i + WINDOW)
        for k in range(CHUNK):
            slot = i * CHUNK + k
            total[row_at[slot]] += jnp.dot(
                window[slot], held[col_at[slot]], preferred_element_type=F32
            )
        return 0

    lax.fori_loop(0, chunks, body, 0)
    half = keep.shape[0]
    one = pltpu.make_async_copy(total.at[pl.ds(half, half)], away, sems.at[0])
    two = pltpu.make_async_copy(total.at[pl.ds(0, half)], keep, sems.at[1])
    one.start()
    two.start()
    one.wait()
    two.wait()


def forward(count, row_at, col_at, tiles, pieces):
    slots = tiles.shape[0]
    any_spec = pl.BlockSpec(memory_space=pl.ANY)
    half = jax.ShapeDtypeStruct((16, SIDE, RANK), F32)
    return pl.pallas_call(
        forward_kernel,
        out_shape=(half, half),
        in_specs=[pl.BlockSpec(memory_space=pltpu.SMEM)] * 3 + [any_spec] * 9,
        out_specs=(any_spec, any_spec),
        scratch_shapes=[
            pltpu.VMEM((64, SIDE, RANK), BF16),
            pltpu.VMEM((33, SIDE, RANK), F32),
            pltpu.VMEM((slots, SIDE, SIDE), BF16),
            pltpu.SemaphoreType.DMA((8,)),
            pltpu.SemaphoreType.DMA((slots // CHUNK,)),
        ],
        compiler_params=limits(36),
        name="forward",
    )(count, row_at, col_at, tiles, *pieces)


def backward_kernel(count, row_at, col_at, tiles, *rest):
    pieces, keep, aways = rest[:8], rest[8], rest[9:15]
    held, total, window, sems, tile_sems = rest[15:]
    chunks, copy, start = tile_window(count, tiles, window, tile_sems)
    copies = load_pieces(pieces, held, sems)
    for i in range(WINDOW):
        start(i)
    total[...] = jnp.zeros_like(total)
    for one in copies:
        one.wait()

    def body(i, _):
        copy(i).wait()
        start(i + WINDOW)
        for k in range(CHUNK):
            slot = i * CHUNK + k
            total[col_at[slot]] += jnp.dot(
                held[row_at[slot]], window[slot], preferred_element_type=F32
            )
        return 0

    lax.fori_loop(0, chunks, body, 0)
    for h in range(2):
        keep[h] = total[pl.ds(32 * h, 8)]
        for d in range(3):
            aways[3 * h + d][...] = total[pl.ds(32 * h + 8 * (d + 1), 8)].astype(BF16)


def backward(count, row_at, col_at, tiles, pieces):
    slots = tiles.shape[0]
    any_spec = pl.BlockSpec(memory_space=pl.ANY)
    part = jax.ShapeDtypeStruct((8, RANK, SIDE), BF16)
    return pl.pallas_call(
        backward_kernel,
        out_shape=(jax.ShapeDtypeStruct((2, 8, RANK, SIDE), F32),) + (part,) * 6,
        in_specs=[pl.BlockSpec(memory_space=pltpu.SMEM)] * 3 + [any_spec] * 9,
        out_specs=tuple(whole(7)),
        scratch_shapes=[
            pltpu.VMEM((32, RANK, SIDE), BF16),
            pltpu.VMEM((65, RANK, SIDE), F32),
            pltpu.VMEM((slots, SIDE, SIDE), BF16),
            pltpu.SemaphoreType.DMA((8,)),
            pltpu.SemaphoreType.DMA((slots // CHUNK,)),
        ],
        compiler_params=limits(44),
        name="backward",
    )(count, row_at, col_at, tiles, *pieces)


def core_sum_kernel(keep, came, *outs):
    for d in range(4):
        at = pl.ds(4 * d, 4)
        outs[d][...] = keep[at] + came[at]


def core_sum(keep, came):
    part = jax.ShapeDtypeStruct((4, SIDE, RANK), F32)
    return pl.pallas_call(
        core_sum_kernel,
        out_shape=(part,) * 4,
        in_specs=whole(2),
        out_specs=tuple(whole(4)),
        compiler_params=limits(16),
        name="core_sum",
    )(keep, came)


def inner_kernel(a, b, c, d, out):
    for i in range(out.shape[0]):
        summed = (a[i] + b[i]) + (c[i] + d[i])
        out[i] = summed.T.astype(BF16)


def inner_sum(parts):
    return pl.pallas_call(
        inner_kernel,
        out_shape=jax.ShapeDtypeStruct((4, RANK, SIDE), BF16),
        in_specs=whole(4),
        out_specs=whole(1)[0],
        compiler_params=limits(16),
        name="inner_sum",
    )(*parts)


def middle_kernel(keep, *rest):
    came, next_keep, aways = rest[:6], rest[6], rest[7:]
    for h in range(2):
        for d in range(4):
            at = pl.ds(2 * d, 2)
            total = keep[h, at]
            for one in came[3 * h : 3 * h + 3]:
                total += one[at].astype(F32)
            if d == 0:
                next_keep[h] = total
            else:
                aways[3 * h + d - 1][...] = total.astype(BF16)


def middle_sum(keep, came):
    part = jax.ShapeDtypeStruct((2, RANK, SIDE), BF16)
    return pl.pallas_call(
        middle_kernel,
        out_shape=(jax.ShapeDtypeStruct((2, 2, RANK, SIDE), F32),) + (part,) * 6,
        in_specs=whole(7),
        out_specs=tuple(whole(7)),
        compiler_params=limits(16),
        name="middle_sum",
    )(keep, *came)


def exact_dot(a, b, dims):
    return lax.dot_general(
        a, b, (dims, ((), ())), precision=lax.Precision.HIGHEST, preferred_element_type=F32
    )


def outer_kernel(keep, *rest):
    came, outer, gram = rest[:6], rest[6], rest[7]
    gram_total = jnp.zeros((RANK, RANK), F32)
    for h in range(2):
        for b in range(2):
            total = keep[h, b]
            for one in came[3 * h : 3 * h + 3]:
                total += one[b].astype(F32)
            outer[2 * h + b] = total
            gram_total += exact_dot(total, total, ((1,), (1,)))
    gram[...] = gram_total


def outer_sum(keep, came):
    return pl.pallas_call(
        outer_kernel,
        out_shape=(
            jax.ShapeDtypeStruct((4, RANK, SIDE), F32),
            jax.ShapeDtypeStruct((RANK, RANK), F32),
        ),
        in_specs=whole(7),
        out_specs=tuple(whole(2)),
        compiler_params=limits(16),
        name="outer_sum",
    )(keep, *came)


def wide(value):
    return jnp.broadcast_to(value, (8, RANK))


def finish_kernel(scale, gram, outer, basis, factor, work):
    rows = lax.broadcasted_iota(jnp.int32, (RANK, RANK), 0)
    cols = lax.broadcasted_iota(jnp.int32, (RANK, RANK), 1)
    sub = lax.broadcasted_iota(jnp.int32, (8, RANK), 0)
    work[:, :RANK] = gram[...]
    work[:, RANK:] = jnp.where(rows == cols, 1.0, 0.0)
    for j in range(0, RANK, 8):
        halves = [work[j : j + 8, :RANK], work[j : j + 8, RANK:]]
        diag = [
            [wide(halves[0][r : r + 1, j + s : j + s + 1]) for s in range(r + 1)]
            for r in range(8)
        ]
        upper = [[wide(half[r : r + 1, :]) for half in halves] for r in range(8)]
        lower = [[None] * 8 for _ in range(8)]
        root = [None] * 8
        for i in range(8):
            root[i] = lax.rsqrt(diag[i][i])
            for r in range(i + 1, 8):
                lower[r][i] = diag[r][i] * root[i]
            for r in range(i + 1, 8):
                for s in range(i + 1, r + 1):
                    diag[r][s] = diag[r][s] - lower[r][i] * lower[s][i]
            upper[i] = [one * root[i] for one in upper[i]]
            for r in range(i + 1, 8):
                upper[r] = [a - lower[r][i] * b for a, b in zip(upper[r], upper[i])]
        for h in range(2):
            panel = upper[0][h]
            for r in range(1, 8):
                panel = jnp.where(sub == r, upper[r][h], panel)
            work[j : j + 8, h * RANK : (h + 1) * RANK] = panel
        for g in range(j + 8, RANK, 8):
            halves = [work[g : g + 8, :RANK], work[g : g + 8, RANK:]]
            column = []
            for k in range(8):
                one = wide(halves[0][:, j + k : j + k + 1])
                for i in range(k):
                    one = one - column[i] * lower[k][i]
                column.append(one * root[k])
            for h in range(2):
                block = halves[h]
                for k in range(8):
                    block = block - column[k] * upper[k][h]
                work[g : g + 8, h * RANK : (h + 1) * RANK] = block
    factor[...] = jnp.where(cols >= rows, work[:, :RANK], 0.0) * (1.0 / scale)
    inverse = work[:, RANK:] * scale
    for b in range(outer.shape[0]):
        basis[pl.ds(b * SIDE, SIDE), :] = exact_dot(outer[b], inverse, ((0,), (1,)))


def finish(gram, outer, entities):
    scale = float(entities) ** 0.5

    def kernel(*refs):
        finish_kernel(scale, *refs)

    return pl.pallas_call(
        kernel,
        out_shape=(
            jax.ShapeDtypeStruct((4 * SIDE, RANK), F32),
            jax.ShapeDtypeStruct((RANK, RANK), F32),
        ),
        in_specs=whole(2),
        out_specs=tuple(whole(2)),
        scratch_shapes=[pltpu.VMEM((RANK, 2 * RANK), F32)],
        compiler_params=limits(16),
        name="finish",
    )(gram, outer)


def shards(basis_in, tiles, tile_coords, tile_count):
    x, y, z, core = (lax.axis_index(name) for name in AXES)
    slots = tiles.shape[0]
    used = jnp.arange(slots, dtype=jnp.int32) < tile_count[0]
    local_row = tile_coords[:, 0] - (x * 4 + y) * 32
    dz = (local_row // 8 - z) % 4
    dc = (local_row // 4 - core) % 2
    row_at = dc * 16 + dz * 4 + local_row % 4
    row_group = tile_coords[:, 1] // 32
    b = tile_coords[:, 1] % 4
    dx = (row_group // 4 - x) % 4
    dy = (row_group % 4 - y) % 4
    col_at = jnp.where(b < 2, dy * 8 + dx * 2 + b, 32 + dx * 8 + dy * 2 + b - 2)

    with jax.named_scope("gather_basis"):
        halves = (basis_in[: 2 * SIDE], basis_in[2 * SIDE :])
        orders = (("x", "y"), ("y", "x"))
        near = [
            [half] + [send(half, order[0], -d) for d in (1, 2, 3)]
            for half, order in zip(halves, orders)
        ]
        near = lax.optimization_barrier(near)
        firsts = [jnp.concatenate(four, axis=0) for four in near]
        pieces = []
        for first, order in zip(firsts, orders):
            pieces += [first] + [send(first, order[1], -d) for d in (1, 2, 3)]
        pieces = [piece.reshape(8, SIDE, RANK) for piece in pieces]

    keep, away = forward(tile_count, jnp.where(used, row_at, 32), col_at, tiles, pieces)

    with jax.named_scope("reduce_inner"):
        came = send(away, "core", 1)
        sums = core_sum(keep, came)
        inner = inner_sum([sums[0]] + [send(sums[d], "z", d) for d in (1, 2, 3)])

    with jax.named_scope("gather_inner"):
        mine = [inner] + [send(inner, "z", -d) for d in (1, 2, 3)]
        theirs = [send(one, "core", 1) for one in mine]

    keep, *aways = backward(
        tile_count, row_at, jnp.where(used, col_at, 64), tiles, mine + theirs
    )

    with jax.named_scope("reduce_outer"):
        back = ("y",) * 3 + ("x",) * 3
        steps = (1, 2, 3) * 2
        came = [send(a, axis, d) for a, axis, d in zip(aways, back, steps)]
        keep, *aways = middle_sum(keep, came)
        forth = ("x",) * 3 + ("y",) * 3
        came = [send(a, axis, d) for a, axis, d in zip(aways, forth, steps)]
        outer, gram = outer_sum(keep, came)

    with jax.named_scope("reduce_gram"):
        gram = gram + send(gram, "core", 1)
        for axis in ("z", "y", "x"):
            parts = [send(gram, axis, d) for d in (1, 2, 3)]
            gram = (gram + parts[1]) + (parts[0] + parts[2])

    entities = basis_in.shape[0] * 128
    return finish(gram, outer, entities)


def solution(mesh):
    split = Mesh(mesh.devices.reshape(4, 4, 4, 2), AXES)
    placed = (P(AXES, None), P(AXES, None, None), P(AXES, None), P(AXES))
    return jax.shard_map(
        shards,
        mesh=split,
        in_specs=placed,
        out_specs=(P(AXES, None), P()),
        check_vma=False,
    )
```

```python
import jax
import jax.numpy as jnp
from jax import lax
from jax.experimental import pallas as pl
from jax.experimental.pallas import tpu as pltpu
from jax.sharding import Mesh, PartitionSpec as P

AXES = ("x", "y", "z", "core")
SIZES = {"x": 4, "y": 4, "z": 4, "core": 2}
SIDE = 256
RANK = 128
CHUNK = 32
EXTRA = 16
F32 = jnp.float32
BF16 = jnp.bfloat16


def send(array, axis, step):
    size = SIZES[axis]
    return lax.ppermute(array, axis, [(i, (i + step) % size) for i in range(size)])


def limits(mib):
    return pltpu.CompilerParams(vmem_limit_bytes=mib * 1024 * 1024)


def whole(count):
    return [pl.BlockSpec(memory_space=pltpu.VMEM)] * count


def load_pieces(pieces, held, sems):
    copies = []
    at = 0
    for i, piece in enumerate(pieces):
        rows = piece.shape[0]
        copies.append(pltpu.make_async_copy(piece, held.at[pl.ds(at, rows)], sems.at[i]))
        at += rows
    for copy in copies:
        copy.start()
    return copies


def hold_kernel(count, tiles, held, sems):
    chunks = (count[0] + CHUNK - 1) // CHUNK

    def copy(i):
        at = pl.ds(i * CHUNK, CHUNK)
        return pltpu.make_async_copy(tiles.at[at], held.at[at], sems.at[i])

    def start(i, _):
        copy(i).start()
        return 0

    def wait(i, _):
        copy(i).wait()
        return 0

    lax.fori_loop(0, chunks, start, 0)
    lax.fori_loop(0, chunks, wait, 0)


def hold_tiles(count, tiles):
    return pl.pallas_call(
        hold_kernel,
        out_shape=jax.ShapeDtypeStruct(tiles.shape, tiles.dtype),
        in_specs=[pl.BlockSpec(memory_space=pltpu.SMEM), pl.BlockSpec(memory_space=pl.ANY)],
        out_specs=whole(1)[0],
        scratch_shapes=[pltpu.SemaphoreType.DMA((tiles.shape[0] // CHUNK,))],
        compiler_params=limits(27),
        cost_estimate=pl.CostEstimate(
            flops=0, bytes_accessed=2 * tiles.size * tiles.dtype.itemsize, transcendentals=0
        ),
        name="hold_tiles",
    )(count, tiles)


def forward_kernel(count, row_at, col_at, tiles, *rest):
    pieces, (keep, away, held, total, sems) = rest[:8], rest[8:]
    chunks = (count[0] + CHUNK - 1) // CHUNK
    copies = load_pieces(pieces, held, sems)
    total[...] = jnp.zeros_like(total)
    for one in copies:
        one.wait()

    def body(i, _):
        for k in range(CHUNK):
            slot = i * CHUNK + k
            total[row_at[slot]] += jnp.dot(
                tiles[slot], held[col_at[slot]], preferred_element_type=F32
            )
        return 0

    lax.fori_loop(0, chunks, body, 0)
    half = keep.shape[0]
    one = pltpu.make_async_copy(total.at[pl.ds(half, half)], away, sems.at[0])
    two = pltpu.make_async_copy(total.at[pl.ds(0, half)], keep, sems.at[1])
    one.start()
    two.start()
    one.wait()
    two.wait()


def forward(count, row_at, col_at, tiles, pieces):
    any_spec = pl.BlockSpec(memory_space=pl.ANY)
    half = jax.ShapeDtypeStruct((16, SIDE, RANK), F32)
    return pl.pallas_call(
        forward_kernel,
        out_shape=(half, half),
        in_specs=[pl.BlockSpec(memory_space=pltpu.SMEM)] * 3 + whole(1) + [any_spec] * 8,
        out_specs=(any_spec, any_spec),
        scratch_shapes=[
            pltpu.VMEM((64, SIDE, RANK), BF16),
            pltpu.VMEM((33, SIDE, RANK), F32),
            pltpu.SemaphoreType.DMA((8,)),
        ],
        compiler_params=limits(11),
        name="forward",
    )(count, row_at, col_at, tiles, *pieces)


def backward_kernel(count, row_at, col_at, tiles, *rest):
    pieces, keeps, aways = rest[:8], rest[8:10], rest[10:16]
    held, total, sems = rest[16:]
    chunks = (count[0] + CHUNK - 1) // CHUNK
    copies = load_pieces(pieces, held, sems)
    total[...] = jnp.zeros_like(total)
    for one in copies:
        one.wait()

    def body(i, _):
        for k in range(CHUNK):
            slot = i * CHUNK + k
            total[col_at[slot]] += jnp.dot(
                held[row_at[slot]], tiles[slot], preferred_element_type=F32
            )
        return 0

    lax.fori_loop(0, chunks, body, 0)
    for h in range(2):
        keeps[h][...] = total[pl.ds(32 * h, 8)]
        for d in range(3):
            aways[3 * h + d][...] = total[pl.ds(32 * h + 8 * (d + 1), 8)].astype(BF16)


def backward(count, row_at, col_at, tiles, pieces):
    any_spec = pl.BlockSpec(memory_space=pl.ANY)
    part = jax.ShapeDtypeStruct((8, RANK, SIDE), BF16)
    keep = jax.ShapeDtypeStruct((8, RANK, SIDE), F32)
    outs = pl.pallas_call(
        backward_kernel,
        out_shape=(keep,) * 2 + (part,) * 6,
        in_specs=[pl.BlockSpec(memory_space=pltpu.SMEM)] * 3 + whole(1) + [any_spec] * 8,
        out_specs=tuple(whole(8)),
        scratch_shapes=[
            pltpu.VMEM((32, RANK, SIDE), BF16),
            pltpu.VMEM((65, RANK, SIDE), F32),
            pltpu.SemaphoreType.DMA((8,)),
        ],
        compiler_params=limits(14),
        name="backward",
    )(count, row_at, col_at, tiles, *pieces)
    return outs[:2], (outs[2:5], outs[5:8])


def core_sum_kernel(keep, came, kept, *outs):
    kept[...] = keep[pl.ds(0, 4)] + came[pl.ds(0, 4)]
    for d, out in enumerate(outs):
        at = pl.ds(4 * (d + 1), 4)
        total = keep[at] + came[at]
        largest = jnp.max(jnp.abs(total), axis=0)
        largest = jnp.max(jnp.max(largest, axis=0, keepdims=True), axis=1, keepdims=True)
        power = jnp.floor(jnp.log2(jnp.maximum(largest, 1e-30))) - 13.0
        scale = jnp.exp2(-power)
        for i in range(4):
            out[pl.ds(SIDE * i, SIDE), :] = total[i] * scale
        out[pl.ds(4 * SIDE, EXTRA), :] = jnp.broadcast_to(power, (EXTRA, RANK))


def core_sum(keep, came):
    part = jax.ShapeDtypeStruct((4 * SIDE + EXTRA, RANK), F32)
    return pl.pallas_call(
        core_sum_kernel,
        out_shape=(jax.ShapeDtypeStruct((4, SIDE, RANK), F32),) + (part,) * 3,
        in_specs=whole(2),
        out_specs=tuple(whole(4)),
        compiler_params=limits(6),
        name="core_sum",
    )(keep, came)


def inner_kernel(kept, a, b, c, out):
    scales = [jnp.exp2(one[pl.ds(4 * SIDE, 1), :]) for one in (a, b, c)]
    for i in range(out.shape[0]):
        summed = kept[i]
        for one, scale in zip((a, b, c), scales):
            summed += one[pl.ds(SIDE * i, SIDE), :] * scale
        out[i] = summed.T.astype(BF16)


def inner_sum(kept, parts):
    return pl.pallas_call(
        inner_kernel,
        out_shape=jax.ShapeDtypeStruct((4, RANK, SIDE), BF16),
        in_specs=whole(4),
        out_specs=whole(1)[0],
        compiler_params=limits(6),
        name="inner_sum",
    )(kept, *parts)


def middle_kernel(keep, a, b, c, next_keep, *aways):
    for d in range(4):
        at = pl.ds(2 * d, 2)
        total = (keep[at] + a[at].astype(F32)) + (b[at].astype(F32) + c[at].astype(F32))
        if d == 0:
            next_keep[...] = total
        else:
            aways[d - 1][...] = total.astype(BF16)


def middle_sum(keep, came):
    part = jax.ShapeDtypeStruct((2, RANK, SIDE), BF16)
    keep, *aways = pl.pallas_call(
        middle_kernel,
        out_shape=(jax.ShapeDtypeStruct((2, RANK, SIDE), F32),) + (part,) * 3,
        in_specs=whole(4),
        out_specs=tuple(whole(4)),
        compiler_params=limits(6),
        name="middle_sum",
    )(keep, *came)
    return keep, aways


def exact_dot(a, b, dims):
    return lax.dot_general(
        a, b, (dims, ((), ())), precision=lax.Precision.HIGHEST, preferred_element_type=F32
    )


def outer_kernel(*refs):
    keeps, came, outer, gram = refs[:2], refs[2:8], refs[8], refs[9]
    gram_total = jnp.zeros((RANK, RANK), F32)
    for h in range(2):
        for b in range(2):
            total = keeps[h][b]
            for one in came[3 * h : 3 * h + 3]:
                total += one[b].astype(F32)
            outer[2 * h + b] = total
            gram_total += exact_dot(total, total, ((1,), (1,)))
    gram[...] = gram_total


def outer_sum(keeps, came):
    return pl.pallas_call(
        outer_kernel,
        out_shape=(
            jax.ShapeDtypeStruct((4, RANK, SIDE), F32),
            jax.ShapeDtypeStruct((RANK, RANK), F32),
        ),
        in_specs=whole(8),
        out_specs=tuple(whole(2)),
        compiler_params=limits(6),
        name="outer_sum",
    )(*keeps, *came)


def wide(value):
    return jnp.broadcast_to(value, (8, RANK))


def finish_kernel(scale, gram, outer, basis, factor, work):
    rows = lax.broadcasted_iota(jnp.int32, (RANK, RANK), 0)
    cols = lax.broadcasted_iota(jnp.int32, (RANK, RANK), 1)
    sub = lax.broadcasted_iota(jnp.int32, (8, RANK), 0)
    work[:, :RANK] = gram[...]
    work[:, RANK:] = jnp.where(rows == cols, 1.0, 0.0)
    for j in range(0, RANK, 8):
        halves = [work[j : j + 8, :RANK], work[j : j + 8, RANK:]]
        diag = [
            [wide(halves[0][r : r + 1, j + s : j + s + 1]) for s in range(r + 1)]
            for r in range(8)
        ]
        upper = [[wide(half[r : r + 1, :]) for half in halves] for r in range(8)]
        lower = [[None] * 8 for _ in range(8)]
        root = [None] * 8
        for i in range(8):
            root[i] = lax.rsqrt(diag[i][i])
            for r in range(i + 1, 8):
                lower[r][i] = diag[r][i] * root[i]
            for r in range(i + 1, 8):
                for s in range(i + 1, r + 1):
                    diag[r][s] = diag[r][s] - lower[r][i] * lower[s][i]
            upper[i] = [one * root[i] for one in upper[i]]
            for r in range(i + 1, 8):
                upper[r] = [a - lower[r][i] * b for a, b in zip(upper[r], upper[i])]
        for h in range(2):
            panel = upper[0][h]
            for r in range(1, 8):
                panel = jnp.where(sub == r, upper[r][h], panel)
            work[j : j + 8, h * RANK : (h + 1) * RANK] = panel
        for g in range(j + 8, RANK, 8):
            halves = [work[g : g + 8, :RANK], work[g : g + 8, RANK:]]
            column = []
            for k in range(8):
                one = wide(halves[0][:, j + k : j + k + 1])
                for i in range(k):
                    one = one - column[i] * lower[k][i]
                column.append(one * root[k])
            for h in range(2):
                block = halves[h]
                for k in range(8):
                    block = block - column[k] * upper[k][h]
                work[g : g + 8, h * RANK : (h + 1) * RANK] = block
    factor[...] = jnp.where(cols >= rows, work[:, :RANK], 0.0) * (1.0 / scale)
    inverse = work[:, RANK:] * scale
    for b in range(outer.shape[0]):
        basis[pl.ds(b * SIDE, SIDE), :] = exact_dot(outer[b], inverse, ((0,), (1,)))


def finish(gram, outer, entities):
    scale = float(entities) ** 0.5

    def kernel(*refs):
        finish_kernel(scale, *refs)

    return pl.pallas_call(
        kernel,
        out_shape=(
            jax.ShapeDtypeStruct((4 * SIDE, RANK), F32),
            jax.ShapeDtypeStruct((RANK, RANK), F32),
        ),
        in_specs=whole(2),
        out_specs=tuple(whole(2)),
        scratch_shapes=[pltpu.VMEM((RANK, 2 * RANK), F32)],
        compiler_params=limits(6),
        name="finish",
    )(gram, outer)


def shards(basis_in, tiles, tile_coords, tile_count):
    x, y, z, core = (lax.axis_index(name) for name in AXES)
    slots = tiles.shape[0]
    used = jnp.arange(slots, dtype=jnp.int32) < tile_count[0]
    local_row = tile_coords[:, 0] - (x * 4 + y) * 32
    dz = (local_row // 8 - z) % 4
    dc = (local_row // 4 - core) % 2
    row_at = dc * 16 + dz * 4 + local_row % 4
    row_group = tile_coords[:, 1] // 32
    b = tile_coords[:, 1] % 4
    dx = (row_group // 4 - x) % 4
    dy = (row_group % 4 - y) % 4
    col_at = jnp.where(b < 2, dy * 8 + dx * 2 + b, 32 + dx * 8 + dy * 2 + b - 2)

    with jax.named_scope("gather_basis"):
        halves = (basis_in[: 2 * SIDE], basis_in[2 * SIDE :])
        orders = (("x", "y"), ("y", "x"))
        near = [
            [half] + [send(half, order[0], -d) for d in (1, 2, 3)]
            for half, order in zip(halves, orders)
        ]
        near, first_tiles = lax.optimization_barrier((near, tiles))
        firsts = [jnp.concatenate(four, axis=0) for four in near]
        pieces = []
        for first, order in zip(firsts, orders):
            pieces += [first] + [send(first, order[1], -d) for d in (1, 2, 3)]
        pieces = [piece.reshape(8, SIDE, RANK) for piece in pieces]

    held = hold_tiles(tile_count, first_tiles)
    keep, away = forward(tile_count, jnp.where(used, row_at, 32), col_at, held, pieces)

    with jax.named_scope("reduce_inner"):
        came = send(away, "core", 1)
        kept, *sums = core_sum(keep, came)
        sums, second_tiles = lax.optimization_barrier((sums, tiles))
        held = hold_tiles(tile_count, second_tiles)
        sums = [send(one.astype(jnp.float16), "z", d) for d, one in zip((1, 2, 3), sums)]
        sums, held = lax.optimization_barrier((sums, held))
        inner = inner_sum(kept, [one.astype(F32) for one in sums])

    with jax.named_scope("gather_inner"):
        mine = [inner] + [send(inner, "z", -d) for d in (1, 2, 3)]
        theirs = [send(one, "core", 1) for one in mine]

    keeps, aways = backward(
        tile_count, row_at, jnp.where(used, col_at, 64), held, mine + theirs
    )

    with jax.named_scope("reduce_outer"):
        last_keeps, last_came = [], []
        for keep, away, (first, then) in zip(keeps, aways, (("y", "x"), ("x", "y"))):
            came = [send(one, first, d) for d, one in zip((1, 2, 3), away)]
            keep, away = middle_sum(keep, came)
            last_keeps.append(keep)
            last_came += [send(one, then, d) for d, one in zip((1, 2, 3), away)]
        outer, gram = outer_sum(last_keeps, last_came)

    with jax.named_scope("reduce_gram"):
        gram = gram + send(gram, "core", 1)
        for axis in ("z", "y", "x"):
            parts = [send(gram, axis, d) for d in (1, 2, 3)]
            gram = (gram + parts[1]) + (parts[0] + parts[2])

    entities = basis_in.shape[0] * 128
    return finish(gram, outer, entities)


def solution(mesh):
    split = Mesh(mesh.devices.reshape(4, 4, 4, 2), AXES)
    placed = (P(AXES, None), P(AXES, None, None), P(AXES, None), P(AXES))
    return jax.shard_map(
        shards,
        mesh=split,
        in_specs=placed,
        out_specs=(P(AXES, None), P()),
        check_vma=False,
    )
```

```python
import jax
import jax.numpy as jnp
from jax import lax
from jax.experimental import pallas as pl
from jax.experimental.pallas import tpu as pltpu
from jax.sharding import Mesh, PartitionSpec as P

AXES = ("x", "y", "z", "core")
SIZES = {"x": 4, "y": 4, "z": 4, "core": 2}
SIDE = 256
RANK = 128
CHUNK = 32
EXTRA = 16
F32 = jnp.float32
BF16 = jnp.bfloat16


def send(array, axis, step):
    size = SIZES[axis]
    return lax.ppermute(array, axis, [(i, (i + step) % size) for i in range(size)])


def limits(mib):
    return pltpu.CompilerParams(vmem_limit_bytes=mib * 1024 * 1024)


def whole(count):
    return [pl.BlockSpec(memory_space=pltpu.VMEM)] * count


def load_pieces(pieces, held, sems):
    copies = []
    at = 0
    for i, piece in enumerate(pieces):
        rows = piece.shape[0]
        copies.append(pltpu.make_async_copy(piece, held.at[pl.ds(at, rows)], sems.at[i]))
        at += rows
    for copy in copies:
        copy.start()
    return copies


def hold_kernel(count, tiles, held, sems):
    chunks = (count[0] + CHUNK - 1) // CHUNK

    def copy(i):
        at = pl.ds(i * CHUNK, CHUNK)
        return pltpu.make_async_copy(tiles.at[at], held.at[at], sems.at[i])

    def start(i, _):
        copy(i).start()
        return 0

    def wait(i, _):
        copy(i).wait()
        return 0

    lax.fori_loop(0, chunks, start, 0)
    lax.fori_loop(0, chunks, wait, 0)


def hold_tiles(count, tiles):
    return pl.pallas_call(
        hold_kernel,
        out_shape=jax.ShapeDtypeStruct(tiles.shape, tiles.dtype),
        in_specs=[pl.BlockSpec(memory_space=pltpu.SMEM), pl.BlockSpec(memory_space=pl.ANY)],
        out_specs=whole(1)[0],
        scratch_shapes=[pltpu.SemaphoreType.DMA((tiles.shape[0] // CHUNK,))],
        compiler_params=limits(27),
        cost_estimate=pl.CostEstimate(
            flops=0, bytes_accessed=2 * tiles.size * tiles.dtype.itemsize, transcendentals=0
        ),
        name="hold_tiles",
    )(count, tiles)


def forward_kernel(count, row_at, col_at, tiles, *rest):
    pieces, (total, away, held, sems) = rest[:-4], rest[-4:]
    chunks = (count[0] + CHUNK - 1) // CHUNK
    copies = load_pieces(pieces, held, sems)
    total[...] = jnp.zeros_like(total)
    for one in copies:
        one.wait()

    def body(i, _):
        for k in range(CHUNK):
            slot = i * CHUNK + k
            total[row_at[slot]] += jnp.dot(
                tiles[slot], held[col_at[slot]], preferred_element_type=F32
            )
        return 0

    lax.fori_loop(0, chunks, body, 0)
    away[...] = total[pl.ds(16, 16)]


def forward(count, row_at, col_at, tiles, pieces):
    any_spec = pl.BlockSpec(memory_space=pl.ANY)
    return pl.pallas_call(
        forward_kernel,
        out_shape=(
            jax.ShapeDtypeStruct((33, SIDE, RANK), F32),
            jax.ShapeDtypeStruct((16, SIDE, RANK), F32),
        ),
        in_specs=[pl.BlockSpec(memory_space=pltpu.SMEM)] * 3
        + whole(1)
        + [any_spec] * len(pieces),
        out_specs=tuple(whole(2)),
        scratch_shapes=[
            pltpu.VMEM((64, SIDE, RANK), BF16),
            pltpu.SemaphoreType.DMA((len(pieces),)),
        ],
        compiler_params=limits(8),
        name="forward",
    )(count, row_at, col_at, tiles, *pieces)


def backward_kernel(count, row_at, col_at, tiles, *rest):
    pieces, (total, *aways, held, sems) = rest[:8], rest[8:]
    chunks = (count[0] + CHUNK - 1) // CHUNK
    copies = load_pieces(pieces, held, sems)
    total[...] = jnp.zeros_like(total)
    for one in copies:
        one.wait()

    def body(i, _):
        for k in range(CHUNK):
            slot = i * CHUNK + k
            total[col_at[slot]] += jnp.dot(
                held[row_at[slot]], tiles[slot], preferred_element_type=F32
            )
        return 0

    lax.fori_loop(0, chunks, body, 0)
    for h in range(2):
        for half in range(2):
            at = pl.ds(32 * h + 16 + 4 * half, 4)
            aways[2 * h + half][...] = total[at].astype(BF16)


def backward(count, row_at, col_at, tiles, pieces):
    any_spec = pl.BlockSpec(memory_space=pl.ANY)
    part = jax.ShapeDtypeStruct((4, RANK, SIDE), BF16)
    total, *aways = pl.pallas_call(
        backward_kernel,
        out_shape=(jax.ShapeDtypeStruct((65, RANK, SIDE), F32),) + (part,) * 4,
        in_specs=[pl.BlockSpec(memory_space=pltpu.SMEM)] * 3 + whole(1) + [any_spec] * 8,
        out_specs=tuple(whole(5)),
        scratch_shapes=[
            pltpu.VMEM((32, RANK, SIDE), BF16),
            pltpu.SemaphoreType.DMA((8,)),
        ],
        compiler_params=limits(6),
        name="backward",
    )(count, row_at, col_at, tiles, *pieces)
    return total, (aways[:2], aways[2:])


def core_sum_kernel(keep, came, kept, *outs):
    kept[...] = keep[pl.ds(0, 4)] + came[pl.ds(0, 4)]
    for d, out in enumerate(outs):
        at = pl.ds(4 * (d + 1), 4)
        total = keep[at] + came[at]
        largest = jnp.max(jnp.abs(total), axis=0)
        largest = jnp.max(jnp.max(largest, axis=0, keepdims=True), axis=1, keepdims=True)
        power = jnp.floor(jnp.log2(jnp.maximum(largest, 1e-30))) - 13.0
        scale = jnp.exp2(-power)
        for i in range(4):
            out[pl.ds(SIDE * i, SIDE), :] = total[i] * scale
        out[pl.ds(4 * SIDE, EXTRA), :] = jnp.broadcast_to(power, (EXTRA, RANK))


def core_sum(keep, came):
    part = jax.ShapeDtypeStruct((4 * SIDE + EXTRA, RANK), F32)
    return pl.pallas_call(
        core_sum_kernel,
        out_shape=(jax.ShapeDtypeStruct((4, SIDE, RANK), F32),) + (part,) * 3,
        in_specs=whole(2),
        out_specs=tuple(whole(4)),
        compiler_params=limits(6),
        name="core_sum",
    )(keep, came)


def inner_kernel(kept, a, b, c, out):
    scales = [jnp.exp2(one[pl.ds(4 * SIDE, 1), :]) for one in (a, b, c)]
    for i in range(out.shape[0]):
        summed = kept[i]
        for one, scale in zip((a, b, c), scales):
            summed += one[pl.ds(SIDE * i, SIDE), :] * scale
        out[i] = summed.T.astype(BF16)


def inner_sum(kept, parts):
    return pl.pallas_call(
        inner_kernel,
        out_shape=jax.ShapeDtypeStruct((4, RANK, SIDE), BF16),
        in_specs=whole(4),
        out_specs=whole(1)[0],
        compiler_params=limits(6),
        name="inner_sum",
    )(kept, *parts)


def relay_sum(total, came, half):
    part = jax.ShapeDtypeStruct((8, RANK, SIDE), BF16)

    def kernel(total, a, b, right, left):
        low, high = pl.ds(0, 4), pl.ds(4, 4)
        at = 32 * half + 8
        right[low] = (total[pl.ds(at, 4)] + a[...].astype(F32)).astype(BF16)
        right[high] = total[pl.ds(at + 4, 4)].astype(BF16)
        at = 32 * half + 24
        left[low] = total[pl.ds(at, 4)].astype(BF16)
        left[high] = (total[pl.ds(at + 4, 4)] + b[...].astype(F32)).astype(BF16)

    return pl.pallas_call(
        kernel,
        out_shape=(part, part),
        in_specs=whole(3),
        out_specs=tuple(whole(2)),
        compiler_params=limits(6),
        name="relay_sum",
    )(total, *came)


def middle_sum(total, came, half):
    part = jax.ShapeDtypeStruct((2, RANK, SIDE), BF16)

    def kernel(total, a, b, keep, *aways):
        for d in range(4):
            at = pl.ds(2 * d, 2)
            one = total[pl.ds(32 * half + 2 * d, 2)] + (a[at].astype(F32) + b[at].astype(F32))
            if d == 0:
                keep[...] = one
            else:
                aways[d - 1][...] = one.astype(BF16)

    keep, *aways = pl.pallas_call(
        kernel,
        out_shape=(jax.ShapeDtypeStruct((2, RANK, SIDE), F32),) + (part,) * 3,
        in_specs=whole(3),
        out_specs=tuple(whole(4)),
        compiler_params=limits(6),
        name="middle_sum",
    )(total, *came)
    return keep, aways


def exact_dot(a, b, dims):
    return lax.dot_general(
        a, b, (dims, ((), ())), precision=lax.Precision.HIGHEST, preferred_element_type=F32
    )


def outer_kernel(*refs):
    keeps, came, outer, gram = refs[:2], refs[2:8], refs[8], refs[9]
    gram_total = jnp.zeros((RANK, RANK), F32)
    for h in range(2):
        for b in range(2):
            total = keeps[h][b]
            for one in came[3 * h : 3 * h + 3]:
                total += one[b].astype(F32)
            outer[2 * h + b] = total
            gram_total += exact_dot(total, total, ((1,), (1,)))
    gram[...] = gram_total


def outer_sum(keeps, came):
    return pl.pallas_call(
        outer_kernel,
        out_shape=(
            jax.ShapeDtypeStruct((4, RANK, SIDE), F32),
            jax.ShapeDtypeStruct((RANK, RANK), F32),
        ),
        in_specs=whole(8),
        out_specs=tuple(whole(2)),
        compiler_params=limits(6),
        name="outer_sum",
    )(*keeps, *came)


def wide(value):
    return jnp.broadcast_to(value, (8, RANK))


def finish_kernel(scale, gram, outer, basis, factor, work):
    rows = lax.broadcasted_iota(jnp.int32, (RANK, RANK), 0)
    cols = lax.broadcasted_iota(jnp.int32, (RANK, RANK), 1)
    sub = lax.broadcasted_iota(jnp.int32, (8, RANK), 0)
    work[:, :RANK] = gram[...]
    work[:, RANK:] = jnp.where(rows == cols, 1.0, 0.0)
    for j in range(0, RANK, 8):
        halves = [work[j : j + 8, :RANK], work[j : j + 8, RANK:]]
        diag = [
            [wide(halves[0][r : r + 1, j + s : j + s + 1]) for s in range(r + 1)]
            for r in range(8)
        ]
        upper = [[wide(half[r : r + 1, :]) for half in halves] for r in range(8)]
        lower = [[None] * 8 for _ in range(8)]
        root = [None] * 8
        for i in range(8):
            root[i] = lax.rsqrt(diag[i][i])
            for r in range(i + 1, 8):
                lower[r][i] = diag[r][i] * root[i]
            for r in range(i + 1, 8):
                for s in range(i + 1, r + 1):
                    diag[r][s] = diag[r][s] - lower[r][i] * lower[s][i]
            upper[i] = [one * root[i] for one in upper[i]]
            for r in range(i + 1, 8):
                upper[r] = [a - lower[r][i] * b for a, b in zip(upper[r], upper[i])]
        for h in range(2):
            panel = upper[0][h]
            for r in range(1, 8):
                panel = jnp.where(sub == r, upper[r][h], panel)
            work[j : j + 8, h * RANK : (h + 1) * RANK] = panel
        for g in range(j + 8, RANK, 8):
            halves = [work[g : g + 8, :RANK], work[g : g + 8, RANK:]]
            column = []
            for k in range(8):
                one = wide(halves[0][:, j + k : j + k + 1])
                for i in range(k):
                    one = one - column[i] * lower[k][i]
                column.append(one * root[k])
            for h in range(2):
                block = halves[h]
                for k in range(8):
                    block = block - column[k] * upper[k][h]
                work[g : g + 8, h * RANK : (h + 1) * RANK] = block
    factor[...] = jnp.where(cols >= rows, work[:, :RANK], 0.0) * (1.0 / scale)
    inverse = work[:, RANK:] * scale
    for b in range(outer.shape[0]):
        basis[pl.ds(b * SIDE, SIDE), :] = exact_dot(outer[b], inverse, ((0,), (1,)))


def finish(gram, outer, entities):
    scale = float(entities) ** 0.5

    def kernel(*refs):
        finish_kernel(scale, *refs)

    return pl.pallas_call(
        kernel,
        out_shape=(
            jax.ShapeDtypeStruct((4 * SIDE, RANK), F32),
            jax.ShapeDtypeStruct((RANK, RANK), F32),
        ),
        in_specs=whole(2),
        out_specs=tuple(whole(2)),
        scratch_shapes=[pltpu.VMEM((RANK, 2 * RANK), F32)],
        compiler_params=limits(6),
        name="finish",
    )(gram, outer)


def shards(basis_in, tiles, tile_coords, tile_count):
    x, y, z, core = (lax.axis_index(name) for name in AXES)
    slots = tiles.shape[0]
    used = jnp.arange(slots, dtype=jnp.int32) < tile_count[0]
    local_row = tile_coords[:, 0] - (x * 4 + y) * 32
    dz = (local_row // 8 - z) % 4
    dc = (local_row // 4 - core) % 2
    row_at = dc * 16 + dz * 4 + local_row % 4
    row_group = tile_coords[:, 1] // 32
    b = tile_coords[:, 1] % 4
    dx = (row_group // 4 - x) % 4
    dy = (row_group % 4 - y) % 4
    col_at = jnp.where(b < 2, dy * 8 + dx * 2 + b, 32 + dx * 8 + dy * 2 + b - 2)

    with jax.named_scope("gather_basis"):
        halves = (basis_in[: 2 * SIDE], basis_in[2 * SIDE :])
        orders = (("x", "y"), ("y", "x"))
        near = [
            [half] + [send(half, order[0], -d) for d in (1, 2, 3)]
            for half, order in zip(halves, orders)
        ]
        near, first_tiles = lax.optimization_barrier((near, tiles))
        firsts = [jnp.concatenate(four, axis=0) for four in near]
        pieces = []
        for first, (_, axis) in zip(firsts, orders):
            first = first.reshape(8, SIDE, RANK)
            right, left = send(first, axis, 1), send(first, axis, -1)
            over = (send(right[:4], axis, 1), send(left[4:], axis, -1))
            pieces += [first, left, *over, right]

    held = hold_tiles(tile_count, first_tiles)
    keep, away = forward(tile_count, jnp.where(used, row_at, 32), col_at, held, pieces)

    with jax.named_scope("reduce_inner"):
        came = send(away, "core", 1)
        kept, *sums = core_sum(keep, came)
        sums, second_tiles = lax.optimization_barrier((sums, tiles))
        held = hold_tiles(tile_count, second_tiles)
        sums = [send(one.astype(jnp.float16), "z", d) for d, one in zip((1, 2, 3), sums)]
        sums, held = lax.optimization_barrier((sums, held))
        inner = inner_sum(kept, [one.astype(F32) for one in sums])

    with jax.named_scope("gather_inner"):
        mine = [inner] + [send(inner, "z", -d) for d in (1, 2, 3)]
        theirs = [send(one, "core", 1) for one in mine]

    total, aways = backward(
        tile_count, row_at, jnp.where(used, col_at, 64), held, mine + theirs
    )

    with jax.named_scope("reduce_outer"):
        last_keeps, last_came = [], []
        for half, (first, then) in enumerate((("y", "x"), ("x", "y"))):
            over = aways[half]
            came = (send(over[0], first, 1), send(over[1], first, -1))
            right, left = relay_sum(total, came, half)
            came = (send(right, first, 1), send(left, first, -1))
            keep, away = middle_sum(total, came, half)
            last_keeps.append(keep)
            last_came += [send(one, then, d) for d, one in zip((1, 2, 3), away)]
        outer, gram = outer_sum(last_keeps, last_came)

    with jax.named_scope("reduce_gram"):
        gram = gram + send(gram, "core", 1)
        for axis in ("z", "y", "x"):
            parts = [send(gram, axis, d) for d in (1, 2, 3)]
            gram = (gram + parts[1]) + (parts[0] + parts[2])

    entities = basis_in.shape[0] * 128
    return finish(gram, outer, entities)


def solution(mesh):
    split = Mesh(mesh.devices.reshape(4, 4, 4, 2), AXES)
    placed = (P(AXES, None), P(AXES, None, None), P(AXES, None), P(AXES))
    return jax.shard_map(
        shards,
        mesh=split,
        in_specs=placed,
        out_specs=(P(AXES, None), P()),
        check_vma=False,
    )
```

```python
import itertools

import jax
import jax.numpy as jnp
from jax import lax
from jax.experimental import pallas as pl
from jax.experimental.pallas import tpu as pltpu
from jax.sharding import Mesh, PartitionSpec as P

AXES = ("x", "y", "z", "core")
SIZES = {"x": 4, "y": 4, "z": 4, "core": 2}
SIDE = 256
RANK = 128
CHUNK = 32
EXTRA = 16
F32 = jnp.float32
BF16 = jnp.bfloat16


def send(array, axis, step):
    size = SIZES[axis]
    return lax.ppermute(array, axis, [(i, (i + step) % size) for i in range(size)])


def cross(array, axes, step):
    names = AXES[:3]
    pairs = []
    for place in itertools.product(*(range(SIZES[name]) for name in AXES)):
        there = list(place)
        at = names.index(axes[place[3]])
        there[at] = (there[at] + step) % SIZES[names[at]]
        pairs.append((linear(place), linear(there)))
    return lax.ppermute(array, AXES, pairs)


def linear(place):
    index = 0
    for name, one in zip(AXES, place):
        index = index * SIZES[name] + one
    return index


def limits(mib):
    return pltpu.CompilerParams(vmem_limit_bytes=mib * 1024 * 1024)


def whole(count):
    return [pl.BlockSpec(memory_space=pltpu.VMEM)] * count


def load_pieces(pieces, held, sems):
    copies = []
    at = 0
    for i, piece in enumerate(pieces):
        rows = piece.shape[0]
        copies.append(pltpu.make_async_copy(piece, held.at[pl.ds(at, rows)], sems.at[i]))
        at += rows
    for copy in copies:
        copy.start()
    return copies


def hold_kernel(count, tiles, held, sems):
    chunks = (count[0] + CHUNK - 1) // CHUNK

    def copy(i):
        at = pl.ds(i * CHUNK, CHUNK)
        return pltpu.make_async_copy(tiles.at[at], held.at[at], sems.at[i])

    def start(i, _):
        copy(i).start()
        return 0

    def wait(i, _):
        copy(i).wait()
        return 0

    lax.fori_loop(0, chunks, start, 0)
    lax.fori_loop(0, chunks, wait, 0)


def hold_tiles(count, tiles):
    return pl.pallas_call(
        hold_kernel,
        out_shape=jax.ShapeDtypeStruct(tiles.shape, tiles.dtype),
        in_specs=[pl.BlockSpec(memory_space=pltpu.SMEM), pl.BlockSpec(memory_space=pl.ANY)],
        out_specs=whole(1)[0],
        scratch_shapes=[pltpu.SemaphoreType.DMA((tiles.shape[0] // CHUNK,))],
        compiler_params=limits(27),
        cost_estimate=pl.CostEstimate(
            flops=0, bytes_accessed=2 * tiles.size * tiles.dtype.itemsize, transcendentals=0
        ),
        name="hold_tiles",
    )(count, tiles)


def forward_kernel(count, row_at, col_at, tiles, *rest):
    pieces, (total, away, held, sems) = rest[:-4], rest[-4:]
    chunks = (count[0] + CHUNK - 1) // CHUNK
    copies = load_pieces(pieces, held, sems)
    total[...] = jnp.zeros_like(total)
    for one in copies:
        one.wait()

    def body(i, _):
        for k in range(CHUNK):
            slot = i * CHUNK + k
            total[row_at[slot]] += jnp.dot(
                tiles[slot], held[col_at[slot]], preferred_element_type=F32
            )
        return 0

    lax.fori_loop(0, chunks, body, 0)
    away[...] = total[pl.ds(16, 16)]


def forward(count, row_at, col_at, tiles, pieces):
    any_spec = pl.BlockSpec(memory_space=pl.ANY)
    return pl.pallas_call(
        forward_kernel,
        out_shape=(
            jax.ShapeDtypeStruct((33, SIDE, RANK), F32),
            jax.ShapeDtypeStruct((16, SIDE, RANK), F32),
        ),
        in_specs=[pl.BlockSpec(memory_space=pltpu.SMEM)] * 3
        + whole(1)
        + [any_spec] * len(pieces),
        out_specs=tuple(whole(2)),
        scratch_shapes=[
            pltpu.VMEM((64, SIDE, RANK), BF16),
            pltpu.SemaphoreType.DMA((len(pieces),)),
        ],
        compiler_params=limits(8),
        name="forward",
    )(count, row_at, col_at, tiles, *pieces)


def backward_kernel(count, row_at, col_at, tiles, *rest):
    pieces, (total, *aways, held, sems) = rest[:8], rest[8:]
    chunks = (count[0] + CHUNK - 1) // CHUNK
    copies = load_pieces(pieces, held, sems)
    total[...] = jnp.zeros_like(total)
    for one in copies:
        one.wait()

    def body(i, _):
        for k in range(CHUNK):
            slot = i * CHUNK + k
            total[col_at[slot]] += jnp.dot(
                held[row_at[slot]], tiles[slot], preferred_element_type=F32
            )
        return 0

    lax.fori_loop(0, chunks, body, 0)
    for half in range(2):
        aways[half][...] = total[pl.ds(32 + 8 * half, 8)].astype(BF16)


def backward(count, row_at, col_at, tiles, pieces):
    any_spec = pl.BlockSpec(memory_space=pl.ANY)
    part = jax.ShapeDtypeStruct((8, RANK, SIDE), BF16)
    total, *aways = pl.pallas_call(
        backward_kernel,
        out_shape=(jax.ShapeDtypeStruct((65, RANK, SIDE), F32),) + (part,) * 2,
        in_specs=[pl.BlockSpec(memory_space=pltpu.SMEM)] * 3 + whole(1) + [any_spec] * 8,
        out_specs=tuple(whole(3)),
        scratch_shapes=[
            pltpu.VMEM((32, RANK, SIDE), BF16),
            pltpu.SemaphoreType.DMA((8,)),
        ],
        compiler_params=limits(6),
        name="backward",
    )(count, row_at, col_at, tiles, *pieces)
    return total, aways


def core_sum_kernel(keep, came, kept, *outs):
    kept[...] = keep[pl.ds(0, 4)] + came[pl.ds(0, 4)]
    for d, out in enumerate(outs):
        at = pl.ds(4 * (d + 1), 4)
        total = keep[at] + came[at]
        largest = jnp.max(jnp.abs(total), axis=0)
        largest = jnp.max(jnp.max(largest, axis=0, keepdims=True), axis=1, keepdims=True)
        power = jnp.floor(jnp.log2(jnp.maximum(largest, 1e-30))) - 13.0
        scale = jnp.exp2(-power)
        for i in range(4):
            out[pl.ds(SIDE * i, SIDE), :] = total[i] * scale
        out[pl.ds(4 * SIDE, EXTRA), :] = jnp.broadcast_to(power, (EXTRA, RANK))


def core_sum(keep, came):
    part = jax.ShapeDtypeStruct((4 * SIDE + EXTRA, RANK), F32)
    return pl.pallas_call(
        core_sum_kernel,
        out_shape=(jax.ShapeDtypeStruct((4, SIDE, RANK), F32),) + (part,) * 3,
        in_specs=whole(2),
        out_specs=tuple(whole(4)),
        compiler_params=limits(6),
        name="core_sum",
    )(keep, came)


def inner_kernel(kept, a, b, c, out):
    scales = [jnp.exp2(one[pl.ds(4 * SIDE, 1), :]) for one in (a, b, c)]
    for i in range(out.shape[0]):
        summed = kept[i]
        for one, scale in zip((a, b, c), scales):
            summed += one[pl.ds(SIDE * i, SIDE), :] * scale
        out[i] = summed.T.astype(BF16)


def inner_sum(kept, parts):
    return pl.pallas_call(
        inner_kernel,
        out_shape=jax.ShapeDtypeStruct((4, RANK, SIDE), BF16),
        in_specs=whole(4),
        out_specs=whole(1)[0],
        compiler_params=limits(6),
        name="inner_sum",
    )(kept, *parts)


def relay_kernel(total, a, b, right, left):
    low, high = pl.ds(0, 8), pl.ds(8, 8)
    right[low] = (total[pl.ds(16, 8)] + a[...].astype(F32)).astype(BF16)
    right[high] = total[pl.ds(24, 8)].astype(BF16)
    left[low] = total[pl.ds(48, 8)].astype(BF16)
    left[high] = (total[pl.ds(56, 8)] + b[...].astype(F32)).astype(BF16)


def relay_sum(total, came):
    part = jax.ShapeDtypeStruct((16, RANK, SIDE), BF16)
    return pl.pallas_call(
        relay_kernel,
        out_shape=(part, part),
        in_specs=whole(3),
        out_specs=tuple(whole(2)),
        compiler_params=limits(6),
        name="relay_sum",
    )(total, *came)


def middle_kernel(total, a, b, keep, *aways):
    for d in range(4):
        at = pl.ds(4 * d, 4)
        one = total[at] + (a[at].astype(F32) + b[at].astype(F32))
        if d == 0:
            keep[...] = one
        else:
            aways[d - 1][...] = one.astype(BF16)


def middle_sum(total, came):
    part = jax.ShapeDtypeStruct((4, RANK, SIDE), BF16)
    keep, *aways = pl.pallas_call(
        middle_kernel,
        out_shape=(jax.ShapeDtypeStruct((4, RANK, SIDE), F32),) + (part,) * 3,
        in_specs=whole(3),
        out_specs=tuple(whole(4)),
        compiler_params=limits(6),
        name="middle_sum",
    )(total, *came)
    return keep, aways


def exact_dot(a, b, dims):
    return lax.dot_general(
        a, b, (dims, ((), ())), precision=lax.Precision.HIGHEST, preferred_element_type=F32
    )


def outer_kernel(keep, a, b, c, outer, gram):
    gram_total = jnp.zeros((RANK, RANK), F32)
    for i in range(outer.shape[0]):
        total = (keep[i] + a[i].astype(F32)) + (b[i].astype(F32) + c[i].astype(F32))
        outer[i] = total
        gram_total += exact_dot(total, total, ((1,), (1,)))
    gram[...] = gram_total


def outer_sum(keep, came):
    return pl.pallas_call(
        outer_kernel,
        out_shape=(
            jax.ShapeDtypeStruct((4, RANK, SIDE), F32),
            jax.ShapeDtypeStruct((RANK, RANK), F32),
        ),
        in_specs=whole(4),
        out_specs=tuple(whole(2)),
        compiler_params=limits(6),
        name="outer_sum",
    )(keep, *came)


def wide(value):
    return jnp.broadcast_to(value, (8, RANK))


def finish_kernel(scale, gram, outer, basis, factor, work):
    rows = lax.broadcasted_iota(jnp.int32, (RANK, RANK), 0)
    cols = lax.broadcasted_iota(jnp.int32, (RANK, RANK), 1)
    sub = lax.broadcasted_iota(jnp.int32, (8, RANK), 0)
    work[:, :RANK] = gram[...]
    work[:, RANK:] = jnp.where(rows == cols, 1.0, 0.0)
    for j in range(0, RANK, 8):
        halves = [work[j : j + 8, :RANK], work[j : j + 8, RANK:]]
        diag = [
            [wide(halves[0][r : r + 1, j + s : j + s + 1]) for s in range(r + 1)]
            for r in range(8)
        ]
        upper = [[wide(half[r : r + 1, :]) for half in halves] for r in range(8)]
        lower = [[None] * 8 for _ in range(8)]
        root = [None] * 8
        for i in range(8):
            root[i] = lax.rsqrt(diag[i][i])
            for r in range(i + 1, 8):
                lower[r][i] = diag[r][i] * root[i]
            for r in range(i + 1, 8):
                for s in range(i + 1, r + 1):
                    diag[r][s] = diag[r][s] - lower[r][i] * lower[s][i]
            upper[i] = [one * root[i] for one in upper[i]]
            for r in range(i + 1, 8):
                upper[r] = [a - lower[r][i] * b for a, b in zip(upper[r], upper[i])]
        for h in range(2):
            panel = upper[0][h]
            for r in range(1, 8):
                panel = jnp.where(sub == r, upper[r][h], panel)
            work[j : j + 8, h * RANK : (h + 1) * RANK] = panel
        for g in range(j + 8, RANK, 8):
            halves = [work[g : g + 8, :RANK], work[g : g + 8, RANK:]]
            column = []
            for k in range(8):
                one = wide(halves[0][:, j + k : j + k + 1])
                for i in range(k):
                    one = one - column[i] * lower[k][i]
                column.append(one * root[k])
            for h in range(2):
                block = halves[h]
                for k in range(8):
                    block = block - column[k] * upper[k][h]
                work[g : g + 8, h * RANK : (h + 1) * RANK] = block
    factor[...] = jnp.where(cols >= rows, work[:, :RANK], 0.0) * (1.0 / scale)
    inverse = work[:, RANK:] * scale
    for b in range(outer.shape[0]):
        basis[pl.ds(b * SIDE, SIDE), :] = exact_dot(outer[b], inverse, ((0,), (1,)))


def finish(gram, outer, entities):
    scale = float(entities) ** 0.5

    def kernel(*refs):
        finish_kernel(scale, *refs)

    return pl.pallas_call(
        kernel,
        out_shape=(
            jax.ShapeDtypeStruct((4 * SIDE, RANK), F32),
            jax.ShapeDtypeStruct((RANK, RANK), F32),
        ),
        in_specs=whole(2),
        out_specs=tuple(whole(2)),
        scratch_shapes=[pltpu.VMEM((RANK, 2 * RANK), F32)],
        compiler_params=limits(6),
        name="finish",
    )(gram, outer)


def shards(basis_in, tiles, tile_coords, tile_count):
    x, y, z, core = (lax.axis_index(name) for name in AXES)
    slots = tiles.shape[0]
    used = jnp.arange(slots, dtype=jnp.int32) < tile_count[0]
    local_row = tile_coords[:, 0] - (x * 4 + y) * 32
    dz = (local_row // 8 - z) % 4
    dc = (local_row // 4 - core) % 2
    row_at = dc * 16 + dz * 4 + local_row % 4
    row_group = tile_coords[:, 1] // 32
    b = tile_coords[:, 1] % 4
    dx = (row_group // 4 - x) % 4
    dy = (row_group % 4 - y) % 4
    near_axes, far_axes = ("x", "y"), ("y", "x")
    near_at = jnp.where(core == 0, dx, dy)
    far_at = jnp.where(core == 0, dy, dx)
    col_at = far_at * 16 + near_at * 4 + b

    with jax.named_scope("gather_basis"):
        near = [basis_in] + [cross(basis_in, near_axes, -d) for d in (1, 2, 3)]
        near, first_tiles = lax.optimization_barrier((near, tiles))
        first = jnp.concatenate(near, axis=0).reshape(16, SIDE, RANK)
        right, left = cross(first, far_axes, 1), cross(first, far_axes, -1)
        held = hold_tiles(tile_count, first_tiles)
        right, left, held = lax.optimization_barrier((right, left, held))
        over = (cross(right[:8], far_axes, 1), cross(left[8:], far_axes, -1))
        pieces = [first, left, *over, right]

    keep, away = forward(tile_count, jnp.where(used, row_at, 32), col_at, held, pieces)

    with jax.named_scope("reduce_inner"):
        came = send(away, "core", 1)
        kept, *sums = core_sum(keep, came)
        sums, second_tiles = lax.optimization_barrier((sums, tiles))
        held = hold_tiles(tile_count, second_tiles)
        sums = [send(one.astype(jnp.float16), "z", d) for d, one in zip((1, 2, 3), sums)]
        sums, held = lax.optimization_barrier((sums, held))
        inner = inner_sum(kept, [one.astype(F32) for one in sums])

    with jax.named_scope("gather_inner"):
        mine = [inner] + [send(inner, "z", -d) for d in (1, 2, 3)]
        theirs = [send(one, "core", 1) for one in mine]

    total, aways = backward(
        tile_count, row_at, jnp.where(used, col_at, 64), held, mine + theirs
    )

    with jax.named_scope("reduce_outer"):
        came = (cross(aways[0], far_axes, 1), cross(aways[1], far_axes, -1))
        right, left = relay_sum(total, came)
        came = (cross(right, far_axes, 1), cross(left, far_axes, -1))
        keep, aways = middle_sum(total, came)
        came = [cross(one, near_axes, d) for d, one in zip((1, 2, 3), aways)]
        outer, gram = outer_sum(keep, came)

    with jax.named_scope("reduce_gram"):
        gram = gram + send(gram, "core", 1)
        for axis in ("z", "y", "x"):
            parts = [send(gram, axis, d) for d in (1, 2, 3)]
            gram = (gram + parts[1]) + (parts[0] + parts[2])

    entities = basis_in.shape[0] * 128
    return finish(gram, outer, entities)


def solution(mesh):
    split = Mesh(mesh.devices.reshape(4, 4, 4, 2), AXES)
    placed = (P(AXES, None), P(AXES, None, None), P(AXES, None), P(AXES))
    return jax.shard_map(
        shards,
        mesh=split,
        in_specs=placed,
        out_specs=(P(AXES, None), P()),
        check_vma=False,
    )
```

```python
import itertools

import jax
import jax.numpy as jnp
from jax import lax
from jax.experimental import pallas as pl
from jax.experimental.pallas import tpu as pltpu
from jax.sharding import Mesh, PartitionSpec as P

AXES = ("x", "y", "z", "core")
SIZES = {"x": 4, "y": 4, "z": 4, "core": 2}
SIDE = 256
RANK = 128
CHUNK = 32
EXTRA = 16
SPARE = 32 * 256 + 64 * 65536
F32 = jnp.float32
BF16 = jnp.bfloat16


def send(array, axis, step):
    size = SIZES[axis]
    return lax.ppermute(array, axis, [(i, (i + step) % size) for i in range(size)])


def cross(array, axes, step):
    names = AXES[:3]
    pairs = []
    for place in itertools.product(*(range(SIZES[name]) for name in AXES)):
        there = list(place)
        at = names.index(axes[place[3]])
        there[at] = (there[at] + step) % SIZES[names[at]]
        pairs.append((linear(place), linear(there)))
    return lax.ppermute(array, AXES, pairs)


def linear(place):
    index = 0
    for name, one in zip(AXES, place):
        index = index * SIZES[name] + one
    return index


def limits(mib):
    return pltpu.CompilerParams(vmem_limit_bytes=mib * 1024 * 1024)


def whole(count):
    return [pl.BlockSpec(memory_space=pltpu.VMEM)] * count


def load_pieces(pieces, held, sems):
    copies = []
    at = 0
    for i, piece in enumerate(pieces):
        rows = piece.shape[0]
        copies.append(pltpu.make_async_copy(piece, held.at[pl.ds(at, rows)], sems.at[i]))
        at += rows
    for copy in copies:
        copy.start()
    return copies


def hold_copies(count, tiles, held, sems):
    chunks = (count[0] + CHUNK - 1) // CHUNK

    def copy(i):
        at = pl.ds(i * CHUNK, CHUNK)
        return pltpu.make_async_copy(tiles.at[at], held.at[at], sems.at[i])

    def start(i, _):
        copy(i).start()
        return 0

    def wait(i, _):
        copy(i).wait()
        return 0

    return (lambda: lax.fori_loop(0, chunks, start, 0)), (
        lambda: lax.fori_loop(0, chunks, wait, 0)
    )


def hold_kernel(count, tiles, held, sems):
    start, wait = hold_copies(count, tiles, held, sems)
    start()
    wait()


def plan_kernel(count, row_at, col_at, tiles, held, counts, near, far, sems):
    start, wait = hold_copies(count, tiles, held, sems)
    start()

    def place(slot, ends):
        near_end, far_end = ends
        col = col_at[slot]
        entry = slot + row_at[slot] * 256 + col * 65536
        near[near_end] = entry
        far[far_end] = entry
        over = (col >> 4 == 2).astype(jnp.int32)
        return near_end + 1 - over, far_end + over

    zero = jnp.int32(0)
    near_end, far_end = lax.fori_loop(0, count[0], place, (zero, zero))
    for k in range(CHUNK):
        near[near_end + k] = SPARE
        far[far_end + k] = SPARE
    counts[0] = near_end
    counts[1] = far_end
    wait()


def hold_parameters(tiles):
    return dict(
        scratch_shapes=[pltpu.SemaphoreType.DMA((tiles.shape[0] // CHUNK,))],
        compiler_params=limits(22),
        cost_estimate=pl.CostEstimate(
            flops=0, bytes_accessed=2 * tiles.size * tiles.dtype.itemsize, transcendentals=0
        ),
    )


def scalars(count):
    return [pl.BlockSpec(memory_space=pltpu.SMEM)] * count


def anywhere(count):
    return [pl.BlockSpec(memory_space=pl.ANY)] * count


def hold_tiles(count, tiles):
    return pl.pallas_call(
        hold_kernel,
        out_shape=jax.ShapeDtypeStruct(tiles.shape, tiles.dtype),
        in_specs=scalars(1) + anywhere(1),
        out_specs=whole(1)[0],
        name="hold_tiles",
        **hold_parameters(tiles),
    )(count, tiles)


def plan_tiles(count, row_at, col_at, tiles):
    entries = jax.ShapeDtypeStruct((tiles.shape[0] + CHUNK,), jnp.int32)
    return pl.pallas_call(
        plan_kernel,
        out_shape=(
            jax.ShapeDtypeStruct(tiles.shape, tiles.dtype),
            jax.ShapeDtypeStruct((2,), jnp.int32),
            entries,
            entries,
        ),
        in_specs=scalars(3) + anywhere(1),
        out_specs=tuple(whole(1) + scalars(3)),
        name="plan_tiles",
        **hold_parameters(tiles),
    )(count, row_at, col_at, tiles)


def listed(total, entries, chunk, body):
    def step(i, _):
        for k in range(chunk):
            entry = entries[i * chunk + k]
            body(entry & 255, (entry >> 8) & 255, entry >> 16)
        return 0

    lax.fori_loop(0, (total + chunk - 1) // chunk, step, 0)


def dot(a, b):
    return jnp.dot(a, b, preferred_element_type=F32)


def product_cost(share):
    return pl.CostEstimate(
        flops=int(share * 160 * 2 * SIDE * SIDE * RANK), bytes_accessed=1 << 20, transcendentals=0
    )


def forward_near_kernel(counts, near, tiles, first, left, right, total, held, sems):
    copies = load_pieces([first, left], held, sems)
    last = pltpu.make_async_copy(right, held.at[pl.ds(48, 16)], sems.at[2])
    last.start()
    total[...] = jnp.zeros_like(total)
    for one in copies + [last]:
        one.wait()

    def body(slot, row, col):
        total[row] += dot(tiles[slot], held[col])

    listed(counts[0], near, 32, body)


def forward_near(counts, near, tiles, pieces):
    return pl.pallas_call(
        forward_near_kernel,
        out_shape=jax.ShapeDtypeStruct((33, SIDE, RANK), F32),
        in_specs=scalars(2) + whole(1) + anywhere(3),
        out_specs=whole(1)[0],
        scratch_shapes=[
            pltpu.VMEM((65, SIDE, RANK), BF16),
            pltpu.SemaphoreType.DMA((3,)),
        ],
        compiler_params=limits(8),
        cost_estimate=product_cost(0.75),
        name="forward_near",
    )(counts, near, tiles, *pieces)


def forward_far_kernel(counts, far, tiles, a, b, before, total, away, held, sems):
    copies = load_pieces([a, b], held, sems)
    for one in copies:
        one.wait()

    def body(slot, row, col):
        total[row] += dot(tiles[slot], held[jnp.minimum(col - 32, 16)])

    listed(counts[1], far, 16, body)
    away[...] = total[pl.ds(16, 16)]


def forward_far(counts, far, tiles, pieces, before):
    return pl.pallas_call(
        forward_far_kernel,
        out_shape=(
            jax.ShapeDtypeStruct((33, SIDE, RANK), F32),
            jax.ShapeDtypeStruct((16, SIDE, RANK), F32),
        ),
        in_specs=scalars(2) + whole(1) + anywhere(2) + whole(1),
        out_specs=tuple(whole(2)),
        scratch_shapes=[
            pltpu.VMEM((17, SIDE, RANK), BF16),
            pltpu.SemaphoreType.DMA((2,)),
        ],
        input_output_aliases={5: 0},
        compiler_params=limits(4),
        name="forward_far",
    )(counts, far, tiles, *pieces, before)


def backward_far_kernel(counts, far, tiles, *rest):
    pieces, (a, b, held, total, sems) = rest[:8], rest[8:]
    copies = load_pieces(pieces, held, sems)
    total[...] = jnp.zeros_like(total)
    for one in copies:
        one.wait()

    def body(slot, row, col):
        total[jnp.minimum(col - 32, 16)] += dot(held[row], tiles[slot])

    listed(counts[1], far, 16, body)
    a[...] = total[pl.ds(0, 8)].astype(BF16)
    b[...] = total[pl.ds(8, 8)].astype(BF16)


def backward_far(counts, far, tiles, pieces):
    part = jax.ShapeDtypeStruct((8, RANK, SIDE), BF16)
    return pl.pallas_call(
        backward_far_kernel,
        out_shape=(part, part),
        in_specs=scalars(2) + whole(1) + anywhere(8),
        out_specs=tuple(whole(2)),
        scratch_shapes=[
            pltpu.VMEM((33, RANK, SIDE), BF16),
            pltpu.VMEM((17, RANK, SIDE), F32),
            pltpu.SemaphoreType.DMA((8,)),
        ],
        compiler_params=limits(8),
        name="backward_far",
    )(counts, far, tiles, *pieces)


def backward_near_kernel(counts, near, tiles, *rest):
    pieces, (total, held, sems) = rest[:8], rest[8:]
    copies = load_pieces(pieces, held, sems)
    total[...] = jnp.zeros_like(total)
    for one in copies:
        one.wait()

    def body(slot, row, col):
        total[col] += dot(held[row], tiles[slot])

    listed(counts[0], near, 32, body)


def backward_near(counts, near, tiles, pieces):
    return pl.pallas_call(
        backward_near_kernel,
        out_shape=jax.ShapeDtypeStruct((65, RANK, SIDE), F32),
        in_specs=scalars(2) + whole(1) + anywhere(8),
        out_specs=whole(1)[0],
        scratch_shapes=[
            pltpu.VMEM((33, RANK, SIDE), BF16),
            pltpu.SemaphoreType.DMA((8,)),
        ],
        compiler_params=limits(6),
        cost_estimate=product_cost(0.75),
        name="backward_near",
    )(counts, near, tiles, *pieces)


def core_sum_kernel(keep, came, kept, *outs):
    kept[...] = keep[pl.ds(0, 4)] + came[pl.ds(0, 4)]
    for d, out in enumerate(outs):
        at = pl.ds(4 * (d + 1), 4)
        total = keep[at] + came[at]
        largest = jnp.max(jnp.abs(total), axis=0)
        largest = jnp.max(jnp.max(largest, axis=0, keepdims=True), axis=1, keepdims=True)
        power = jnp.floor(jnp.log2(jnp.maximum(largest, 1e-30))) - 13.0
        scale = jnp.exp2(-power)
        for i in range(4):
            out[pl.ds(SIDE * i, SIDE), :] = total[i] * scale
        out[pl.ds(4 * SIDE, EXTRA), :] = jnp.broadcast_to(power, (EXTRA, RANK))


def core_sum(keep, came):
    part = jax.ShapeDtypeStruct((4 * SIDE + EXTRA, RANK), F32)
    return pl.pallas_call(
        core_sum_kernel,
        out_shape=(jax.ShapeDtypeStruct((4, SIDE, RANK), F32),) + (part,) * 3,
        in_specs=whole(2),
        out_specs=tuple(whole(4)),
        compiler_params=limits(6),
        name="core_sum",
    )(keep, came)


def inner_kernel(kept, a, b, c, out):
    scales = [jnp.exp2(one[pl.ds(4 * SIDE, 1), :]) for one in (a, b, c)]
    for i in range(out.shape[0]):
        summed = kept[i]
        for one, scale in zip((a, b, c), scales):
            summed += one[pl.ds(SIDE * i, SIDE), :] * scale
        out[i] = summed.T.astype(BF16)


def inner_sum(kept, parts):
    return pl.pallas_call(
        inner_kernel,
        out_shape=jax.ShapeDtypeStruct((4, RANK, SIDE), BF16),
        in_specs=whole(4),
        out_specs=whole(1)[0],
        compiler_params=limits(6),
        name="inner_sum",
    )(kept, *parts)


def relay_kernel(total, a, b, right, left):
    low, high = pl.ds(0, 8), pl.ds(8, 8)
    right[low] = (total[pl.ds(16, 8)] + a[...].astype(F32)).astype(BF16)
    right[high] = total[pl.ds(24, 8)].astype(BF16)
    left[low] = total[pl.ds(48, 8)].astype(BF16)
    left[high] = (total[pl.ds(56, 8)] + b[...].astype(F32)).astype(BF16)


def relay_sum(total, came):
    part = jax.ShapeDtypeStruct((16, RANK, SIDE), BF16)
    return pl.pallas_call(
        relay_kernel,
        out_shape=(part, part),
        in_specs=whole(3),
        out_specs=tuple(whole(2)),
        compiler_params=limits(6),
        name="relay_sum",
    )(total, *came)


def middle_kernel(total, a, b, keep, *aways):
    for d in range(4):
        at = pl.ds(4 * d, 4)
        one = total[at] + (a[at].astype(F32) + b[at].astype(F32))
        if d == 0:
            keep[...] = one
        else:
            aways[d - 1][...] = one.astype(BF16)


def middle_sum(total, came):
    part = jax.ShapeDtypeStruct((4, RANK, SIDE), BF16)
    keep, *aways = pl.pallas_call(
        middle_kernel,
        out_shape=(jax.ShapeDtypeStruct((4, RANK, SIDE), F32),) + (part,) * 3,
        in_specs=whole(3),
        out_specs=tuple(whole(4)),
        compiler_params=limits(6),
        name="middle_sum",
    )(total, *came)
    return keep, aways


def exact_dot(a, b, dims):
    return lax.dot_general(
        a, b, (dims, ((), ())), precision=lax.Precision.HIGHEST, preferred_element_type=F32
    )


def outer_kernel(keep, a, b, c, outer, gram):
    gram_total = jnp.zeros((RANK, RANK), F32)
    for i in range(outer.shape[0]):
        total = (keep[i] + a[i].astype(F32)) + (b[i].astype(F32) + c[i].astype(F32))
        outer[i] = total
        gram_total += exact_dot(total, total, ((1,), (1,)))
    gram[...] = gram_total


def outer_sum(keep, came):
    return pl.pallas_call(
        outer_kernel,
        out_shape=(
            jax.ShapeDtypeStruct((4, RANK, SIDE), F32),
            jax.ShapeDtypeStruct((RANK, RANK), F32),
        ),
        in_specs=whole(4),
        out_specs=tuple(whole(2)),
        compiler_params=limits(6),
        name="outer_sum",
    )(keep, *came)


def wide(value):
    return jnp.broadcast_to(value, (8, RANK))


def finish_kernel(scale, gram, outer, basis, factor, work):
    rows = lax.broadcasted_iota(jnp.int32, (RANK, RANK), 0)
    cols = lax.broadcasted_iota(jnp.int32, (RANK, RANK), 1)
    sub = lax.broadcasted_iota(jnp.int32, (8, RANK), 0)
    work[:, :RANK] = gram[...]
    work[:, RANK:] = jnp.where(rows == cols, 1.0, 0.0)
    for j in range(0, RANK, 8):
        halves = [work[j : j + 8, :RANK], work[j : j + 8, RANK:]]
        diag = [
            [wide(halves[0][r : r + 1, j + s : j + s + 1]) for s in range(r + 1)]
            for r in range(8)
        ]
        upper = [[wide(half[r : r + 1, :]) for half in halves] for r in range(8)]
        lower = [[None] * 8 for _ in range(8)]
        root = [None] * 8
        for i in range(8):
            root[i] = lax.rsqrt(diag[i][i])
            for r in range(i + 1, 8):
                lower[r][i] = diag[r][i] * root[i]
            for r in range(i + 1, 8):
                for s in range(i + 1, r + 1):
                    diag[r][s] = diag[r][s] - lower[r][i] * lower[s][i]
            upper[i] = [one * root[i] for one in upper[i]]
            for r in range(i + 1, 8):
                upper[r] = [a - lower[r][i] * b for a, b in zip(upper[r], upper[i])]
        for h in range(2):
            panel = upper[0][h]
            for r in range(1, 8):
                panel = jnp.where(sub == r, upper[r][h], panel)
            work[j : j + 8, h * RANK : (h + 1) * RANK] = panel
        for g in range(j + 8, RANK, 8):
            halves = [work[g : g + 8, :RANK], work[g : g + 8, RANK:]]
            column = []
            for k in range(8):
                one = wide(halves[0][:, j + k : j + k + 1])
                for i in range(k):
                    one = one - column[i] * lower[k][i]
                column.append(one * root[k])
            for h in range(2):
                block = halves[h]
                for k in range(8):
                    block = block - column[k] * upper[k][h]
                work[g : g + 8, h * RANK : (h + 1) * RANK] = block
    factor[...] = jnp.where(cols >= rows, work[:, :RANK], 0.0) * (1.0 / scale)
    inverse = work[:, RANK:] * scale
    for b in range(outer.shape[0]):
        basis[pl.ds(b * SIDE, SIDE), :] = exact_dot(outer[b], inverse, ((0,), (1,)))


def finish(gram, outer, entities):
    scale = float(entities) ** 0.5

    def kernel(*refs):
        finish_kernel(scale, *refs)

    return pl.pallas_call(
        kernel,
        out_shape=(
            jax.ShapeDtypeStruct((4 * SIDE, RANK), F32),
            jax.ShapeDtypeStruct((RANK, RANK), F32),
        ),
        in_specs=whole(2),
        out_specs=tuple(whole(2)),
        scratch_shapes=[pltpu.VMEM((RANK, 2 * RANK), F32)],
        compiler_params=limits(6),
        name="finish",
    )(gram, outer)


def shards(basis_in, tiles, tile_coords, tile_count):
    x, y, z, core = (lax.axis_index(name) for name in AXES)
    local_row = tile_coords[:, 0] - (x * 4 + y) * 32
    dz = (local_row // 8 - z) % 4
    dc = (local_row // 4 - core) % 2
    row_at = dc * 16 + dz * 4 + local_row % 4
    row_group = tile_coords[:, 1] // 32
    b = tile_coords[:, 1] % 4
    dx = (row_group // 4 - x) % 4
    dy = (row_group % 4 - y) % 4
    near_axes, far_axes = ("x", "y"), ("y", "x")
    near_at = jnp.where(core == 0, dx, dy)
    far_at = jnp.where(core == 0, dy, dx)
    col_at = far_at * 16 + near_at * 4 + b

    with jax.named_scope("gather_basis"):
        near = [basis_in] + [cross(basis_in, near_axes, -d) for d in (1, 2, 3)]
        near, first_tiles, row_at, col_at = lax.optimization_barrier((near, tiles, row_at, col_at))
        first = jnp.concatenate(near, axis=0).reshape(16, SIDE, RANK)
        right, left = cross(first, far_axes, 1), cross(first, far_axes, -1)
        held, counts, near_list, far_list = plan_tiles(tile_count, row_at, col_at, first_tiles)
        right, left, held = lax.optimization_barrier((right, left, held))
        over = (cross(right[:8], far_axes, 1), cross(left[8:], far_axes, -1))

    keep = forward_near(counts, near_list, held, (first, left, right))
    keep, away = forward_far(counts, far_list, held, over, keep)

    with jax.named_scope("reduce_inner"):
        came = send(away, "core", 1)
        kept, *sums = core_sum(keep, came)
        sums, second_tiles = lax.optimization_barrier((sums, tiles))
        held = hold_tiles(tile_count, second_tiles)
        sums = [send(one.astype(jnp.float16), "z", d) for d, one in zip((1, 2, 3), sums)]
        sums, held = lax.optimization_barrier((sums, held))
        inner = inner_sum(kept, [one.astype(F32) for one in sums])

    with jax.named_scope("gather_inner"):
        mine = [inner] + [send(inner, "z", -d) for d in (1, 2, 3)]
        theirs = [send(one, "core", 1) for one in mine]

    aways = backward_far(counts, far_list, held, mine + theirs)

    with jax.named_scope("reduce_outer"):
        came = (cross(aways[0], far_axes, 1), cross(aways[1], far_axes, -1))
        total = backward_near(counts, near_list, held, mine + theirs)
        right, left = relay_sum(total, came)
        came = (cross(right, far_axes, 1), cross(left, far_axes, -1))
        keep, aways = middle_sum(total, came)
        came = [cross(one, near_axes, d) for d, one in zip((1, 2, 3), aways)]
        outer, gram = outer_sum(keep, came)

    with jax.named_scope("reduce_gram"):
        gram = gram + send(gram, "core", 1)
        for axis in ("z", "y", "x"):
            parts = [send(gram, axis, d) for d in (1, 2, 3)]
            gram = (gram + parts[1]) + (parts[0] + parts[2])

    entities = basis_in.shape[0] * 128
    return finish(gram, outer, entities)


def solution(mesh):
    split = Mesh(mesh.devices.reshape(4, 4, 4, 2), AXES)
    placed = (P(AXES, None), P(AXES, None, None), P(AXES, None), P(AXES))
    return jax.shard_map(
        shards,
        mesh=split,
        in_specs=placed,
        out_specs=(P(AXES, None), P()),
        check_vma=False,
    )
```

```python
import itertools

import jax
import jax.numpy as jnp
from jax import lax
from jax.experimental import pallas as pl
from jax.experimental.pallas import tpu as pltpu
from jax.sharding import Mesh, PartitionSpec as P

AXES = ("x", "y", "z", "core")
SIZES = {"x": 4, "y": 4, "z": 4, "core": 2}
SIDE = 256
RANK = 128
CHUNK = 32
EXTRA = 16
SPARE = 32 * 256 + 64 * 65536
F32 = jnp.float32
BF16 = jnp.bfloat16


def send(array, axis, step):
    size = SIZES[axis]
    return lax.ppermute(array, axis, [(i, (i + step) % size) for i in range(size)])


def cross(array, axes, step):
    names = AXES[:3]
    pairs = []
    for place in itertools.product(*(range(SIZES[name]) for name in AXES)):
        there = list(place)
        at = names.index(axes[place[3]])
        there[at] = (there[at] + step) % SIZES[names[at]]
        pairs.append((linear(place), linear(there)))
    return lax.ppermute(array, AXES, pairs)


def linear(place):
    index = 0
    for name, one in zip(AXES, place):
        index = index * SIZES[name] + one
    return index


def limits(mib):
    return pltpu.CompilerParams(vmem_limit_bytes=mib * 1024 * 1024)


def whole(count):
    return [pl.BlockSpec(memory_space=pltpu.VMEM)] * count


def load_pieces(pieces, held, sems):
    copies = []
    at = 0
    for i, piece in enumerate(pieces):
        rows = piece.shape[0]
        copies.append(pltpu.make_async_copy(piece, held.at[pl.ds(at, rows)], sems.at[i]))
        at += rows
    for copy in copies:
        copy.start()
    return copies


def hold_copies(count, tiles, held, sems):
    chunks = (count[0] + CHUNK - 1) // CHUNK

    def copy(i):
        at = pl.ds(i * CHUNK, CHUNK)
        return pltpu.make_async_copy(tiles.at[at], held.at[at], sems.at[i])

    def start(i, _):
        copy(i).start()
        return 0

    def wait(i, _):
        copy(i).wait()
        return 0

    return (lambda: lax.fori_loop(0, chunks, start, 0)), (
        lambda: lax.fori_loop(0, chunks, wait, 0)
    )


def plan_kernel(count, row_at, col_at, tiles, held, counts, near, far, sems):
    start, wait = hold_copies(count, tiles, held, sems)
    start()

    def place(slot, ends):
        near_end, far_end = ends
        col = col_at[slot]
        entry = slot + row_at[slot] * 256 + col * 65536
        near[near_end] = entry
        far[far_end] = entry
        over = (col >> 4 == 2).astype(jnp.int32)
        return near_end + 1 - over, far_end + over

    zero = jnp.int32(0)
    near_end, far_end = lax.fori_loop(0, count[0], place, (zero, zero))
    for k in range(CHUNK):
        near[near_end + k] = SPARE
        far[far_end + k] = SPARE
    counts[0] = near_end
    counts[1] = far_end
    wait()


def hold_parameters(tiles):
    return dict(
        scratch_shapes=[pltpu.SemaphoreType.DMA((tiles.shape[0] // CHUNK,))],
        compiler_params=limits(22),
        cost_estimate=pl.CostEstimate(
            flops=0, bytes_accessed=2 * tiles.size * tiles.dtype.itemsize, transcendentals=0
        ),
    )


def scalars(count):
    return [pl.BlockSpec(memory_space=pltpu.SMEM)] * count


def anywhere(count):
    return [pl.BlockSpec(memory_space=pl.ANY)] * count


def plan_tiles(count, row_at, col_at, tiles):
    entries = jax.ShapeDtypeStruct((tiles.shape[0] + CHUNK,), jnp.int32)
    return pl.pallas_call(
        plan_kernel,
        out_shape=(
            jax.ShapeDtypeStruct(tiles.shape, tiles.dtype),
            jax.ShapeDtypeStruct((2,), jnp.int32),
            entries,
            entries,
        ),
        in_specs=scalars(3) + anywhere(1),
        out_specs=tuple(whole(1) + scalars(3)),
        name="plan_tiles",
        **hold_parameters(tiles),
    )(count, row_at, col_at, tiles)


def listed(total, entries, chunk, body):
    def step(i, _):
        for k in range(chunk):
            entry = entries[i * chunk + k]
            body(entry & 255, (entry >> 8) & 255, entry >> 16)
        return 0

    lax.fori_loop(0, (total + chunk - 1) // chunk, step, 0)


def dot(a, b):
    return jnp.dot(a, b, preferred_element_type=F32)


def product_cost(share):
    return pl.CostEstimate(
        flops=int(share * 160 * 2 * SIDE * SIDE * RANK), bytes_accessed=1 << 20, transcendentals=0
    )


def forward_near_kernel(counts, near, tiles, first, left, right, total, held, sems):
    copies = load_pieces([first, left], held, sems)
    last = pltpu.make_async_copy(right, held.at[pl.ds(48, 16)], sems.at[2])
    last.start()
    total[...] = jnp.zeros_like(total)
    for one in copies + [last]:
        one.wait()

    def body(slot, row, col):
        total[row] += dot(tiles[slot], held[col])

    listed(counts[0], near, 32, body)


def forward_near(counts, near, tiles, pieces):
    return pl.pallas_call(
        forward_near_kernel,
        out_shape=jax.ShapeDtypeStruct((33, SIDE, RANK), F32),
        in_specs=scalars(2) + whole(1) + anywhere(3),
        out_specs=whole(1)[0],
        scratch_shapes=[
            pltpu.VMEM((65, SIDE, RANK), BF16),
            pltpu.SemaphoreType.DMA((3,)),
        ],
        compiler_params=limits(8),
        cost_estimate=product_cost(0.75),
        name="forward_near",
    )(counts, near, tiles, *pieces)


def forward_far_kernel(counts, far, tiles, a, b, before, total, *rest):
    *aways, held, sems = rest
    copies = load_pieces([a, b], held, sems)
    for one in copies:
        one.wait()

    def body(slot, row, col):
        total[row] += dot(tiles[slot], held[jnp.minimum(col - 32, 16)])

    listed(counts[1], far, 16, body)
    for d, away in enumerate(aways):
        away[...] = total[pl.ds(16 + 4 * d, 4)]


def forward_far(counts, far, tiles, pieces, before):
    return pl.pallas_call(
        forward_far_kernel,
        out_shape=(jax.ShapeDtypeStruct((33, SIDE, RANK), F32),)
        + (jax.ShapeDtypeStruct((4, SIDE, RANK), F32),) * 4,
        in_specs=scalars(2) + whole(1) + anywhere(2) + whole(1),
        out_specs=tuple(whole(5)),
        scratch_shapes=[
            pltpu.VMEM((17, SIDE, RANK), BF16),
            pltpu.SemaphoreType.DMA((2,)),
        ],
        input_output_aliases={5: 0},
        compiler_params=limits(4),
        name="forward_far",
    )(counts, far, tiles, *pieces, before)


def backward_far_kernel(counts, far, tiles, *rest):
    pieces, (a, b, held, total, sems) = rest[:8], rest[8:]
    copies = load_pieces(pieces, held, sems)
    total[...] = jnp.zeros_like(total)
    for one in copies:
        one.wait()

    def body(slot, row, col):
        total[jnp.minimum(col - 32, 16)] += dot(held[row], tiles[slot])

    listed(counts[1], far, 16, body)
    a[...] = total[pl.ds(0, 8)].astype(BF16)
    b[...] = total[pl.ds(8, 8)].astype(BF16)


def backward_far(counts, far, tiles, pieces):
    part = jax.ShapeDtypeStruct((8, RANK, SIDE), BF16)
    return pl.pallas_call(
        backward_far_kernel,
        out_shape=(part, part),
        in_specs=scalars(2) + whole(1) + anywhere(8),
        out_specs=tuple(whole(2)),
        scratch_shapes=[
            pltpu.VMEM((33, RANK, SIDE), BF16),
            pltpu.VMEM((17, RANK, SIDE), F32),
            pltpu.SemaphoreType.DMA((8,)),
        ],
        compiler_params=limits(8),
        name="backward_far",
    )(counts, far, tiles, *pieces)


def backward_near_kernel(counts, near, tiles, *rest):
    pieces, (total, held, sems) = rest[:8], rest[8:]
    copies = load_pieces(pieces, held, sems)
    total[...] = jnp.zeros_like(total)
    for one in copies:
        one.wait()

    def body(slot, row, col):
        total[col] += dot(held[row], tiles[slot])

    listed(counts[0], near, 32, body)


def backward_near(counts, near, tiles, pieces):
    return pl.pallas_call(
        backward_near_kernel,
        out_shape=jax.ShapeDtypeStruct((65, RANK, SIDE), F32),
        in_specs=scalars(2) + whole(1) + anywhere(8),
        out_specs=whole(1)[0],
        scratch_shapes=[
            pltpu.VMEM((33, RANK, SIDE), BF16),
            pltpu.SemaphoreType.DMA((8,)),
        ],
        compiler_params=limits(6),
        cost_estimate=product_cost(0.75),
        name="backward_near",
    )(counts, near, tiles, *pieces)


def core_sum(keep, came, d):
    def kernel(keep, came, out):
        total = keep[pl.ds(4 * d, 4)] + came[...]
        largest = jnp.max(jnp.abs(total), axis=0)
        largest = jnp.max(jnp.max(largest, axis=0, keepdims=True), axis=1, keepdims=True)
        power = jnp.floor(jnp.log2(jnp.maximum(largest, 1e-30))) - 13.0
        scale = jnp.exp2(-power)
        for i in range(4):
            out[pl.ds(SIDE * i, SIDE), :] = total[i] * scale
        out[pl.ds(4 * SIDE, EXTRA), :] = jnp.broadcast_to(power, (EXTRA, RANK))

    return pl.pallas_call(
        kernel,
        out_shape=jax.ShapeDtypeStruct((4 * SIDE + EXTRA, RANK), F32),
        in_specs=whole(2),
        out_specs=whole(1)[0],
        compiler_params=limits(6),
        name="core_sum",
    )(keep, came)


def inner_kernel(keep, came, a, b, c, out):
    scales = [jnp.exp2(one[pl.ds(4 * SIDE, 1), :]) for one in (a, b, c)]
    for i in range(out.shape[0]):
        summed = keep[i] + came[i]
        for one, scale in zip((a, b, c), scales):
            summed += one[pl.ds(SIDE * i, SIDE), :] * scale
        out[i] = summed.T.astype(BF16)


def inner_sum(keep, came, parts):
    return pl.pallas_call(
        inner_kernel,
        out_shape=jax.ShapeDtypeStruct((4, RANK, SIDE), BF16),
        in_specs=whole(5),
        out_specs=whole(1)[0],
        compiler_params=limits(6),
        name="inner_sum",
    )(keep, came, *parts)


def relay_kernel(total, a, b, right, left):
    low, high = pl.ds(0, 8), pl.ds(8, 8)
    right[low] = (total[pl.ds(16, 8)] + a[...].astype(F32)).astype(BF16)
    right[high] = total[pl.ds(24, 8)].astype(BF16)
    left[low] = total[pl.ds(48, 8)].astype(BF16)
    left[high] = (total[pl.ds(56, 8)] + b[...].astype(F32)).astype(BF16)


def relay_sum(total, came):
    part = jax.ShapeDtypeStruct((16, RANK, SIDE), BF16)
    return pl.pallas_call(
        relay_kernel,
        out_shape=(part, part),
        in_specs=whole(3),
        out_specs=tuple(whole(2)),
        compiler_params=limits(6),
        name="relay_sum",
    )(total, *came)


def middle_kernel(total, a, b, keep, *aways):
    for d in range(4):
        at = pl.ds(4 * d, 4)
        one = total[at] + (a[at].astype(F32) + b[at].astype(F32))
        if d == 0:
            keep[...] = one
        else:
            aways[d - 1][...] = one.astype(BF16)


def middle_sum(total, came):
    part = jax.ShapeDtypeStruct((4, RANK, SIDE), BF16)
    keep, *aways = pl.pallas_call(
        middle_kernel,
        out_shape=(jax.ShapeDtypeStruct((4, RANK, SIDE), F32),) + (part,) * 3,
        in_specs=whole(3),
        out_specs=tuple(whole(4)),
        compiler_params=limits(6),
        name="middle_sum",
    )(total, *came)
    return keep, aways


def exact_dot(a, b, dims):
    return lax.dot_general(
        a, b, (dims, ((), ())), precision=lax.Precision.HIGHEST, preferred_element_type=F32
    )


def outer_kernel(keep, a, b, c, outer, gram):
    gram_total = jnp.zeros((RANK, RANK), F32)
    for i in range(outer.shape[0]):
        total = (keep[i] + a[i].astype(F32)) + (b[i].astype(F32) + c[i].astype(F32))
        outer[i] = total
        gram_total += exact_dot(total, total, ((1,), (1,)))
    gram[...] = gram_total


def outer_sum(keep, came):
    return pl.pallas_call(
        outer_kernel,
        out_shape=(
            jax.ShapeDtypeStruct((4, RANK, SIDE), F32),
            jax.ShapeDtypeStruct((RANK, RANK), F32),
        ),
        in_specs=whole(4),
        out_specs=tuple(whole(2)),
        compiler_params=limits(6),
        name="outer_sum",
    )(keep, *came)


def halved(value):
    large = value.astype(BF16)
    return large, (value - large.astype(F32)).astype(BF16)


def wide(value):
    return jnp.broadcast_to(value, (8, RANK))


def finish_kernel(scale, gram, outer, basis, factor, work):
    rows = lax.broadcasted_iota(jnp.int32, (RANK, RANK), 0)
    cols = lax.broadcasted_iota(jnp.int32, (RANK, RANK), 1)
    sub = lax.broadcasted_iota(jnp.int32, (8, RANK), 0)
    work[:, :RANK] = gram[...]
    work[:, RANK:] = jnp.where(rows == cols, 1.0, 0.0)
    for j in range(0, RANK, 8):
        halves = [work[j : j + 8, :RANK], work[j : j + 8, RANK:]]
        diag = [
            [wide(halves[0][r : r + 1, j + s : j + s + 1]) for s in range(r + 1)]
            for r in range(8)
        ]
        upper = [[wide(half[r : r + 1, :]) for half in halves] for r in range(8)]
        lower = [[None] * 8 for _ in range(8)]
        root = [None] * 8
        for i in range(8):
            root[i] = lax.rsqrt(diag[i][i])
            for r in range(i + 1, 8):
                lower[r][i] = diag[r][i] * root[i]
            for r in range(i + 1, 8):
                for s in range(i + 1, r + 1):
                    diag[r][s] = diag[r][s] - lower[r][i] * lower[s][i]
            upper[i] = [one * root[i] for one in upper[i]]
            for r in range(i + 1, 8):
                upper[r] = [a - lower[r][i] * b for a, b in zip(upper[r], upper[i])]
        for h in range(2):
            panel = upper[0][h]
            for r in range(1, 8):
                panel = jnp.where(sub == r, upper[r][h], panel)
            work[j : j + 8, h * RANK : (h + 1) * RANK] = panel
        for g in range(j + 8, RANK, 8):
            halves = [work[g : g + 8, :RANK], work[g : g + 8, RANK:]]
            column = []
            for k in range(8):
                one = wide(halves[0][:, j + k : j + k + 1])
                for i in range(k):
                    one = one - column[i] * lower[k][i]
                column.append(one * root[k])
            for h in range(2):
                block = halves[h]
                for k in range(8):
                    block = block - column[k] * upper[k][h]
                work[g : g + 8, h * RANK : (h + 1) * RANK] = block
    factor[...] = jnp.where(cols >= rows, work[:, :RANK], 0.0) * (1.0 / scale)
    inverse, rest = halved(work[:, RANK:] * scale)
    for b in range(outer.shape[0]):
        large, small = halved(outer[b])
        product = dot(inverse, large) + (dot(rest, large) + dot(inverse, small))
        basis[pl.ds(b * SIDE, SIDE), :] = product.T


def finish(gram, outer, entities):
    scale = float(entities) ** 0.5

    def kernel(*refs):
        finish_kernel(scale, *refs)

    return pl.pallas_call(
        kernel,
        out_shape=(
            jax.ShapeDtypeStruct((4 * SIDE, RANK), F32),
            jax.ShapeDtypeStruct((RANK, RANK), F32),
        ),
        in_specs=whole(2),
        out_specs=tuple(whole(2)),
        scratch_shapes=[pltpu.VMEM((RANK, 2 * RANK), F32)],
        compiler_params=limits(6),
        name="finish",
    )(gram, outer)


def shards(basis_in, tiles, tile_coords, tile_count):
    x, y, z, core = (lax.axis_index(name) for name in AXES)
    local_row = tile_coords[:, 0] - (x * 4 + y) * 32
    dz = (local_row // 8 - z) % 4
    dc = (local_row // 4 - core) % 2
    row_at = dc * 16 + dz * 4 + local_row % 4
    row_group = tile_coords[:, 1] // 32
    b = tile_coords[:, 1] % 4
    dx = (row_group // 4 - x) % 4
    dy = (row_group % 4 - y) % 4
    near_axes, far_axes = ("x", "y"), ("y", "x")
    near_at = jnp.where(core == 0, dx, dy)
    far_at = jnp.where(core == 0, dy, dx)
    col_at = far_at * 16 + near_at * 4 + b

    with jax.named_scope("gather_basis"):
        near = [basis_in] + [cross(basis_in, near_axes, -d) for d in (1, 2, 3)]
        near, first_tiles, row_at, col_at = lax.optimization_barrier((near, tiles, row_at, col_at))
        first = jnp.concatenate(near, axis=0).reshape(16, SIDE, RANK)
        right, left = cross(first, far_axes, 1), cross(first, far_axes, -1)
        held, counts, near_list, far_list = plan_tiles(tile_count, row_at, col_at, first_tiles)
        right, left, held = lax.optimization_barrier((right, left, held))
        over = (cross(right[:8], far_axes, 1), cross(left[8:], far_axes, -1))

    keep = forward_near(counts, near_list, held, (first, left, right))
    keep, *aways = forward_far(counts, far_list, held, over, keep)

    with jax.named_scope("reduce_inner"):
        parts = []
        for d in (2, 1, 3):
            one = core_sum(keep, send(aways[d], "core", 1), d)
            parts.append(send(one.astype(jnp.float16), "z", d).astype(F32))
        inner = inner_sum(keep, send(aways[0], "core", 1), parts)

    with jax.named_scope("gather_inner"):
        mine = [inner] + [send(inner, "z", -d) for d in (1, 2, 3)]
        theirs = [send(one, "core", 1) for one in mine]

    aways = backward_far(counts, far_list, held, mine + theirs)

    with jax.named_scope("reduce_outer"):
        came = (cross(aways[0], far_axes, 1), cross(aways[1], far_axes, -1))
        total = backward_near(counts, near_list, held, mine + theirs)
        right, left = relay_sum(total, came)
        came = (cross(right, far_axes, 1), cross(left, far_axes, -1))
        keep, aways = middle_sum(total, came)
        came = [cross(one, near_axes, d) for d, one in zip((1, 2, 3), aways)]
        outer, gram = outer_sum(keep, came)

    with jax.named_scope("reduce_gram"):
        gram = gram + send(gram, "core", 1)
        for axis in ("z", "y", "x"):
            parts = [send(gram, axis, d) for d in (1, 2, 3)]
            gram = (gram + parts[1]) + (parts[0] + parts[2])

    entities = basis_in.shape[0] * 128
    return finish(gram, outer, entities)


def solution(mesh):
    split = Mesh(mesh.devices.reshape(4, 4, 4, 2), AXES)
    placed = (P(AXES, None), P(AXES, None, None), P(AXES, None), P(AXES))
    return jax.shard_map(
        shards,
        mesh=split,
        in_specs=placed,
        out_specs=(P(AXES, None), P()),
        check_vma=False,
    )
```

```python
import itertools

import jax
import jax.numpy as jnp
from jax import lax
from jax.experimental import pallas as pl
from jax.experimental.pallas import tpu as pltpu
from jax.sharding import Mesh, PartitionSpec as P

AXES = ("x", "y", "z", "core")
SIZES = {"x": 4, "y": 4, "z": 4, "core": 2}
SIDE = 256
RANK = 128
CHUNK = 32
EXTRA = 16
SPARE = 32 * 256 + 64 * 65536
F32 = jnp.float32
BF16 = jnp.bfloat16


def send(array, axis, step):
    size = SIZES[axis]
    return lax.ppermute(array, axis, [(i, (i + step) % size) for i in range(size)])


def cross(array, axes, step):
    names = AXES[:3]
    pairs = []
    for place in itertools.product(*(range(SIZES[name]) for name in AXES)):
        if axes[place[3]] is None:
            continue
        there = list(place)
        at = names.index(axes[place[3]])
        there[at] = (there[at] + step) % SIZES[names[at]]
        pairs.append((linear(place), linear(there)))
    return lax.ppermute(array, AXES, pairs)


def linear(place):
    index = 0
    for name, one in zip(AXES, place):
        index = index * SIZES[name] + one
    return index


def limits(mib):
    return pltpu.CompilerParams(vmem_limit_bytes=mib * 1024 * 1024)


def whole(count):
    return [pl.BlockSpec(memory_space=pltpu.VMEM)] * count


def load_pieces(pieces, held, sems):
    copies = []
    at = 0
    for i, piece in enumerate(pieces):
        rows = piece.shape[0]
        copies.append(pltpu.make_async_copy(piece, held.at[pl.ds(at, rows)], sems.at[i]))
        at += rows
    for copy in copies:
        copy.start()
    return copies


def hold_copies(count, tiles, held, sems):
    chunks = (count[0] + CHUNK - 1) // CHUNK

    def copy(i):
        at = pl.ds(i * CHUNK, CHUNK)
        return pltpu.make_async_copy(tiles.at[at], held.at[at], sems.at[i])

    def start(i, _):
        copy(i).start()
        return 0

    def wait(i, _):
        copy(i).wait()
        return 0

    return (lambda: lax.fori_loop(0, chunks, start, 0)), (
        lambda: lax.fori_loop(0, chunks, wait, 0)
    )


def plan_kernel(count, row_at, col_at, tiles, held, counts, near, far, sems):
    start, wait = hold_copies(count, tiles, held, sems)
    start()

    def place(slot, ends):
        near_end, far_end = ends
        col = col_at[slot]
        entry = slot + row_at[slot] * 256 + col * 65536
        near[near_end] = entry
        far[far_end] = entry
        over = (col >> 4 == 2).astype(jnp.int32)
        return near_end + 1 - over, far_end + over

    zero = jnp.int32(0)
    near_end, far_end = lax.fori_loop(0, count[0], place, (zero, zero))
    for k in range(CHUNK):
        near[near_end + k] = SPARE
        far[far_end + k] = SPARE
    counts[0] = near_end
    counts[1] = far_end
    wait()


def hold_parameters(tiles):
    return dict(
        scratch_shapes=[pltpu.SemaphoreType.DMA((tiles.shape[0] // CHUNK,))],
        compiler_params=limits(22),
        cost_estimate=pl.CostEstimate(
            flops=0, bytes_accessed=2 * tiles.size * tiles.dtype.itemsize, transcendentals=0
        ),
    )


def scalars(count):
    return [pl.BlockSpec(memory_space=pltpu.SMEM)] * count


def anywhere(count):
    return [pl.BlockSpec(memory_space=pl.ANY)] * count


def plan_tiles(count, row_at, col_at, tiles):
    entries = jax.ShapeDtypeStruct((tiles.shape[0] + CHUNK,), jnp.int32)
    return pl.pallas_call(
        plan_kernel,
        out_shape=(
            jax.ShapeDtypeStruct(tiles.shape, tiles.dtype),
            jax.ShapeDtypeStruct((2,), jnp.int32),
            entries,
            entries,
        ),
        in_specs=scalars(3) + anywhere(1),
        out_specs=tuple(whole(1) + scalars(3)),
        name="plan_tiles",
        **hold_parameters(tiles),
    )(count, row_at, col_at, tiles)


def listed(total, entries, chunk, body):
    def step(i, _):
        for k in range(chunk):
            entry = entries[i * chunk + k]
            body(entry & 255, (entry >> 8) & 255, entry >> 16)
        return 0

    lax.fori_loop(0, (total + chunk - 1) // chunk, step, 0)


def dot(a, b):
    return jnp.dot(a, b, preferred_element_type=F32)


def product_cost(share):
    return pl.CostEstimate(
        flops=int(share * 160 * 2 * SIDE * SIDE * RANK), bytes_accessed=1 << 20, transcendentals=0
    )


def forward_near_kernel(counts, near, tiles, *rest):
    pieces, (total, held, sems) = rest[:6], rest[6:]
    copies = []
    for i, at in enumerate((0, 8, 16, 24, 48, 56)):
        copies.append(pltpu.make_async_copy(pieces[i], held.at[pl.ds(at, 8)], sems.at[i]))
    for one in copies:
        one.start()
    total[...] = jnp.zeros_like(total)
    for one in copies:
        one.wait()

    def body(slot, row, col):
        total[row] += dot(tiles[slot], held[col])

    listed(counts[0], near, 32, body)


def forward_near(counts, near, tiles, pieces):
    return pl.pallas_call(
        forward_near_kernel,
        out_shape=jax.ShapeDtypeStruct((33, SIDE, RANK), F32),
        in_specs=scalars(2) + whole(1) + anywhere(6),
        out_specs=whole(1)[0],
        scratch_shapes=[
            pltpu.VMEM((65, SIDE, RANK), BF16),
            pltpu.SemaphoreType.DMA((6,)),
        ],
        compiler_params=limits(8),
        cost_estimate=product_cost(0.75),
        name="forward_near",
    )(counts, near, tiles, *pieces)


def forward_far_kernel(counts, far, tiles, a, b, before, total, *rest):
    *aways, held, sems = rest
    copies = load_pieces([a, b], held, sems)
    for one in copies:
        one.wait()

    def body(slot, row, col):
        total[row] += dot(tiles[slot], held[jnp.minimum(col - 32, 16)])

    listed(counts[1], far, 16, body)
    for d, away in enumerate(aways):
        away[...] = total[pl.ds(16 + 4 * d, 4)]


def forward_far(counts, far, tiles, pieces, before):
    return pl.pallas_call(
        forward_far_kernel,
        out_shape=(jax.ShapeDtypeStruct((33, SIDE, RANK), F32),)
        + (jax.ShapeDtypeStruct((4, SIDE, RANK), F32),) * 4,
        in_specs=scalars(2) + whole(1) + anywhere(2) + whole(1),
        out_specs=tuple(whole(5)),
        scratch_shapes=[
            pltpu.VMEM((17, SIDE, RANK), BF16),
            pltpu.SemaphoreType.DMA((2,)),
        ],
        input_output_aliases={5: 0},
        compiler_params=limits(4),
        name="forward_far",
    )(counts, far, tiles, *pieces, before)


def backward_far_kernel(counts, far, tiles, *rest):
    pieces, (a, b, held, total, sems) = rest[:8], rest[8:]
    copies = load_pieces(pieces, held, sems)
    total[...] = jnp.zeros_like(total)
    for one in copies:
        one.wait()

    def body(slot, row, col):
        total[jnp.minimum(col - 32, 16)] += dot(held[row], tiles[slot])

    listed(counts[1], far, 16, body)
    a[...] = total[pl.ds(0, 8)].astype(BF16)
    b[...] = total[pl.ds(8, 8)].astype(BF16)


def backward_far(counts, far, tiles, pieces):
    part = jax.ShapeDtypeStruct((8, RANK, SIDE), BF16)
    return pl.pallas_call(
        backward_far_kernel,
        out_shape=(part, part),
        in_specs=scalars(2) + whole(1) + anywhere(8),
        out_specs=tuple(whole(2)),
        scratch_shapes=[
            pltpu.VMEM((33, RANK, SIDE), BF16),
            pltpu.VMEM((17, RANK, SIDE), F32),
            pltpu.SemaphoreType.DMA((8,)),
        ],
        compiler_params=limits(8),
        name="backward_far",
    )(counts, far, tiles, *pieces)


def backward_near_kernel(counts, near, tiles, *rest):
    pieces, (total, right, left, held, sems) = rest[:8], rest[8:]
    copies = load_pieces(pieces, held, sems)
    total[...] = jnp.zeros_like(total)
    for one in copies:
        one.wait()

    def body(slot, row, col):
        total[col] += dot(held[row], tiles[slot])

    listed(counts[0], near, 32, body)
    right[...] = total[pl.ds(24, 8)].astype(BF16)
    left[...] = total[pl.ds(48, 8)].astype(BF16)


def backward_near(counts, near, tiles, pieces):
    part = jax.ShapeDtypeStruct((8, RANK, SIDE), BF16)
    return pl.pallas_call(
        backward_near_kernel,
        out_shape=(jax.ShapeDtypeStruct((65, RANK, SIDE), F32), part, part),
        in_specs=scalars(2) + whole(1) + anywhere(8),
        out_specs=tuple(whole(3)),
        scratch_shapes=[
            pltpu.VMEM((33, RANK, SIDE), BF16),
            pltpu.SemaphoreType.DMA((8,)),
        ],
        compiler_params=limits(6),
        cost_estimate=product_cost(0.75),
        name="backward_near",
    )(counts, near, tiles, *pieces)


def core_sum(keep, came, d):
    def kernel(keep, came, out):
        total = keep[pl.ds(4 * d, 4)] + came[...]
        largest = jnp.max(jnp.abs(total), axis=0)
        largest = jnp.max(jnp.max(largest, axis=0, keepdims=True), axis=1, keepdims=True)
        power = jnp.floor(jnp.log2(jnp.maximum(largest, 1e-30))) - 13.0
        scale = jnp.exp2(-power)
        for i in range(4):
            out[pl.ds(SIDE * i, SIDE), :] = total[i] * scale
        out[pl.ds(4 * SIDE, EXTRA), :] = jnp.broadcast_to(power, (EXTRA, RANK))

    return pl.pallas_call(
        kernel,
        out_shape=jax.ShapeDtypeStruct((4 * SIDE + EXTRA, RANK), F32),
        in_specs=whole(2),
        out_specs=whole(1)[0],
        compiler_params=limits(6),
        name="core_sum",
    )(keep, came)


def inner_kernel(keep, came, a, b, c, out):
    scales = [jnp.exp2(one[pl.ds(4 * SIDE, 1), :]) for one in (a, b, c)]
    for i in range(out.shape[0]):
        summed = keep[i] + came[i]
        for one, scale in zip((a, b, c), scales):
            summed += one[pl.ds(SIDE * i, SIDE), :] * scale
        out[i] = summed.T.astype(BF16)


def inner_sum(keep, came, parts):
    return pl.pallas_call(
        inner_kernel,
        out_shape=jax.ShapeDtypeStruct((4, RANK, SIDE), BF16),
        in_specs=whole(5),
        out_specs=whole(1)[0],
        compiler_params=limits(6),
        name="inner_sum",
    )(keep, came, *parts)


def relay_sum(total, came, at):
    def kernel(total, came, out):
        out[...] = (total[pl.ds(at, 8)] + came[...].astype(F32)).astype(BF16)

    return pl.pallas_call(
        kernel,
        out_shape=jax.ShapeDtypeStruct((8, RANK, SIDE), BF16),
        in_specs=whole(2),
        out_specs=whole(1)[0],
        compiler_params=limits(6),
        name="relay_sum",
    )(total, came)


def middle_sum(total, came, at):
    def kernel(total, a, b, *outs):
        for d, out in enumerate(outs):
            here = pl.ds(4 * d, 4)
            one = total[pl.ds(at + 4 * d, 4)] + (a[here].astype(F32) + b[here].astype(F32))
            out[...] = one.astype(out.dtype)

    return pl.pallas_call(
        kernel,
        out_shape=tuple(
            jax.ShapeDtypeStruct((4, RANK, SIDE), F32 if at + d == 0 else BF16) for d in range(2)
        ),
        in_specs=whole(3),
        out_specs=tuple(whole(2)),
        compiler_params=limits(6),
        name="middle_sum",
    )(total, *came)


def exact_dot(a, b, dims):
    return lax.dot_general(
        a, b, (dims, ((), ())), precision=lax.Precision.HIGHEST, preferred_element_type=F32
    )


def outer_kernel(keep, a, b, c, outer, gram):
    gram_total = jnp.zeros((RANK, RANK), F32)
    for i in range(outer.shape[0]):
        total = (keep[i] + a[i].astype(F32)) + (b[i].astype(F32) + c[i].astype(F32))
        outer[i] = total
        gram_total += exact_dot(total, total, ((1,), (1,)))
    gram[...] = gram_total


def outer_sum(keep, came):
    return pl.pallas_call(
        outer_kernel,
        out_shape=(
            jax.ShapeDtypeStruct((4, RANK, SIDE), F32),
            jax.ShapeDtypeStruct((RANK, RANK), F32),
        ),
        in_specs=whole(4),
        out_specs=tuple(whole(2)),
        compiler_params=limits(6),
        name="outer_sum",
    )(keep, *came)


def halved(value):
    large = value.astype(BF16)
    return large, (value - large.astype(F32)).astype(BF16)


def wide(value):
    return jnp.broadcast_to(value, (8, RANK))


def finish_kernel(scale, gram, outer, basis, factor, work):
    rows = lax.broadcasted_iota(jnp.int32, (RANK, RANK), 0)
    cols = lax.broadcasted_iota(jnp.int32, (RANK, RANK), 1)
    sub = lax.broadcasted_iota(jnp.int32, (8, RANK), 0)
    work[:, :RANK] = gram[...]
    work[:, RANK:] = jnp.where(rows == cols, 1.0, 0.0)
    for j in range(0, RANK, 8):
        halves = [work[j : j + 8, :RANK], work[j : j + 8, RANK:]]
        diag = [
            [wide(halves[0][r : r + 1, j + s : j + s + 1]) for s in range(r + 1)]
            for r in range(8)
        ]
        upper = [[wide(half[r : r + 1, :]) for half in halves] for r in range(8)]
        lower = [[None] * 8 for _ in range(8)]
        root = [None] * 8
        for i in range(8):
            root[i] = lax.rsqrt(diag[i][i])
            for r in range(i + 1, 8):
                lower[r][i] = diag[r][i] * root[i]
            for r in range(i + 1, 8):
                for s in range(i + 1, r + 1):
                    diag[r][s] = diag[r][s] - lower[r][i] * lower[s][i]
            upper[i] = [one * root[i] for one in upper[i]]
            for r in range(i + 1, 8):
                upper[r] = [a - lower[r][i] * b for a, b in zip(upper[r], upper[i])]
        for h in range(2):
            panel = upper[0][h]
            for r in range(1, 8):
                panel = jnp.where(sub == r, upper[r][h], panel)
            work[j : j + 8, h * RANK : (h + 1) * RANK] = panel
        for g in range(j + 8, RANK, 8):
            halves = [work[g : g + 8, :RANK], work[g : g + 8, RANK:]]
            column = []
            for k in range(8):
                one = wide(halves[0][:, j + k : j + k + 1])
                for i in range(k):
                    one = one - column[i] * lower[k][i]
                column.append(one * root[k])
            for h in range(2):
                block = halves[h]
                for k in range(8):
                    block = block - column[k] * upper[k][h]
                work[g : g + 8, h * RANK : (h + 1) * RANK] = block
    factor[...] = jnp.where(cols >= rows, work[:, :RANK], 0.0) * (1.0 / scale)
    inverse, rest = halved(work[:, RANK:] * scale)
    for b in range(outer.shape[0]):
        large, small = halved(outer[b])
        product = dot(inverse, large) + (dot(rest, large) + dot(inverse, small))
        basis[pl.ds(b * SIDE, SIDE), :] = product.T


def finish(gram, outer, entities):
    scale = float(entities) ** 0.5

    def kernel(*refs):
        finish_kernel(scale, *refs)

    return pl.pallas_call(
        kernel,
        out_shape=(
            jax.ShapeDtypeStruct((4 * SIDE, RANK), F32),
            jax.ShapeDtypeStruct((RANK, RANK), F32),
        ),
        in_specs=whole(2),
        out_specs=tuple(whole(2)),
        scratch_shapes=[pltpu.VMEM((RANK, 2 * RANK), F32)],
        compiler_params=limits(6),
        name="finish",
    )(gram, outer)


def shards(basis_in, tiles, tile_coords, tile_count):
    x, y, z, core = (lax.axis_index(name) for name in AXES)
    local_row = tile_coords[:, 0] - (x * 4 + y) * 32
    dz = (local_row // 8 - z) % 4
    dc = (local_row // 4 - core) % 2
    row_at = dc * 16 + dz * 4 + local_row % 4
    row_group = tile_coords[:, 1] // 32
    b = tile_coords[:, 1] % 4
    dx = (row_group // 4 - x) % 4
    dy = (row_group % 4 - y) % 4
    near_axes, far_axes = ("x", "y"), ("y", "x")
    near_at = jnp.where(core == 0, dx, dy)
    far_at = jnp.where(core == 0, dy, dx)
    col_at = far_at * 16 + near_at * 4 + b

    with jax.named_scope("gather_basis"):
        near = [basis_in] + [cross(basis_in, near_axes, -d) for d in (1, 2, 3)]
        held, counts, near_list, far_list = plan_tiles(tile_count, row_at, col_at, tiles)
        near, held = lax.optimization_barrier((near, held))
        low, high = (
            jnp.concatenate(pair, axis=0).reshape(8, SIDE, RANK) for pair in (near[:2], near[2:])
        )
        right_low, left_high = cross(low, far_axes, 1), cross(high, far_axes, -1)
        left_low, right_high = cross(low, far_axes, -1), cross(high, far_axes, 1)
        over = (cross(right_low, far_axes, 1), cross(left_high, far_axes, -1))

    keep = forward_near(
        counts, near_list, held, (low, high, left_low, left_high, right_low, right_high)
    )
    keep, *aways = forward_far(counts, far_list, held, over, keep)

    with jax.named_scope("reduce_inner"):
        parts = []
        for d in (2, 1, 3):
            one = core_sum(keep, send(aways[d], "core", 1), d)
            parts.append(send(one.astype(jnp.float16), "z", d).astype(F32))
        inner = inner_sum(keep, send(aways[0], "core", 1), parts)

    with jax.named_scope("gather_inner"):
        mine = [inner] + [send(inner, "z", -d) for d in (1, 2, 3)]
        theirs = [send(one, "core", 1) for one in mine]

    aways = backward_far(counts, far_list, held, mine + theirs)

    with jax.named_scope("reduce_outer"):
        over = (cross(aways[0], far_axes, 1), cross(aways[1], far_axes, -1))
        total, right_high, left_low = backward_near(counts, near_list, held, mine + theirs)
        right_high, left_low = cross(right_high, far_axes, 1), cross(left_low, far_axes, -1)
        right_low = cross(relay_sum(total, over[0], 16), far_axes, 1)
        left_high = cross(relay_sum(total, over[1], 56), far_axes, -1)
        keep, one = middle_sum(total, (right_low, left_low), 0)
        two, three = middle_sum(total, (right_high, left_high), 8)
        came = [cross(part, near_axes, d) for d, part in ((1, one), (2, two), (3, three))]
        outer, gram = outer_sum(keep, came)

    with jax.named_scope("reduce_gram"):
        gram = gram + lax.ppermute(gram, "core", [(0, 1)])
        for axis in ("z", "y", "x"):
            parts = [cross(gram, (None, axis), d) for d in (1, 2, 3)]
            gram = (gram + parts[1]) + (parts[0] + parts[2])
        gram = jnp.where(core == 1, gram, lax.ppermute(gram, "core", [(1, 0)]))

    entities = basis_in.shape[0] * 128
    return finish(gram, outer, entities)


def solution(mesh):
    split = Mesh(mesh.devices.reshape(4, 4, 4, 2), AXES)
    placed = (P(AXES, None), P(AXES, None, None), P(AXES, None), P(AXES))
    return jax.shard_map(
        shards,
        mesh=split,
        in_specs=placed,
        out_specs=(P(AXES, None), P()),
        check_vma=False,
    )
```

```python
import itertools

import jax
import jax.numpy as jnp
from jax import lax
from jax.experimental import pallas as pl
from jax.experimental.pallas import tpu as pltpu
from jax.sharding import Mesh, PartitionSpec as P

AXES = ("x", "y", "z", "core")
SIZES = {"x": 4, "y": 4, "z": 4, "core": 2}
SIDE = 256
RANK = 128
CHUNK = 32
EXTRA = 16
SPARE = 32 * 256 + 64 * 65536
F32 = jnp.float32
BF16 = jnp.bfloat16


def send(array, axis, step):
    size = SIZES[axis]
    return lax.ppermute(array, axis, [(i, (i + step) % size) for i in range(size)])


def cross(array, axes, step):
    names = AXES[:3]
    pairs = []
    for place in itertools.product(*(range(SIZES[name]) for name in AXES)):
        there = list(place)
        at = names.index(axes[place[3]])
        there[at] = (there[at] + step) % SIZES[names[at]]
        pairs.append((linear(place), linear(there)))
    return lax.ppermute(array, AXES, pairs)


def linear(place):
    index = 0
    for name, one in zip(AXES, place):
        index = index * SIZES[name] + one
    return index


def limits(mib):
    return pltpu.CompilerParams(vmem_limit_bytes=mib * 1024 * 1024)


def whole(count):
    return [pl.BlockSpec(memory_space=pltpu.VMEM)] * count


def load_pieces(pieces, held, sems):
    copies = []
    at = 0
    for i, piece in enumerate(pieces):
        rows = piece.shape[0]
        copies.append(pltpu.make_async_copy(piece, held.at[pl.ds(at, rows)], sems.at[i]))
        at += rows
    for copy in copies:
        copy.start()
    return copies


def hold_copies(count, tiles, held, sems):
    chunks = (count[0] + CHUNK - 1) // CHUNK

    def copy(i):
        at = pl.ds(i * CHUNK, CHUNK)
        return pltpu.make_async_copy(tiles.at[at], held.at[at], sems.at[i])

    def start(i, _):
        copy(i).start()
        return 0

    def wait(i, _):
        copy(i).wait()
        return 0

    return (lambda: lax.fori_loop(0, chunks, start, 0)), (
        lambda: lax.fori_loop(0, chunks, wait, 0)
    )


def plan_kernel(count, row_at, col_at, tiles, held, counts, near, far, sems):
    start, wait = hold_copies(count, tiles, held, sems)
    start()

    def place(slot, ends):
        near_end, far_end = ends
        col = col_at[slot]
        entry = slot + row_at[slot] * 256 + col * 65536
        near[near_end] = entry
        far[far_end] = entry
        over = (col >> 4 == 2).astype(jnp.int32)
        return near_end + 1 - over, far_end + over

    zero = jnp.int32(0)
    near_end, far_end = lax.fori_loop(0, count[0], place, (zero, zero))
    for k in range(CHUNK):
        near[near_end + k] = SPARE
        far[far_end + k] = SPARE
    counts[0] = near_end
    counts[1] = far_end
    wait()


def hold_parameters(tiles):
    return dict(
        scratch_shapes=[pltpu.SemaphoreType.DMA((tiles.shape[0] // CHUNK,))],
        compiler_params=limits(22),
        cost_estimate=pl.CostEstimate(
            flops=0, bytes_accessed=2 * tiles.size * tiles.dtype.itemsize, transcendentals=0
        ),
    )


def scalars(count):
    return [pl.BlockSpec(memory_space=pltpu.SMEM)] * count


def anywhere(count):
    return [pl.BlockSpec(memory_space=pl.ANY)] * count


def plan_tiles(count, row_at, col_at, tiles):
    entries = jax.ShapeDtypeStruct((tiles.shape[0] + CHUNK,), jnp.int32)
    return pl.pallas_call(
        plan_kernel,
        out_shape=(
            jax.ShapeDtypeStruct(tiles.shape, tiles.dtype),
            jax.ShapeDtypeStruct((2,), jnp.int32),
            entries,
            entries,
        ),
        in_specs=scalars(3) + anywhere(1),
        out_specs=tuple(whole(1) + scalars(3)),
        name="plan_tiles",
        **hold_parameters(tiles),
    )(count, row_at, col_at, tiles)


def listed(total, entries, chunk, body):
    def step(i, _):
        for k in range(chunk):
            entry = entries[i * chunk + k]
            body(entry & 255, (entry >> 8) & 255, entry >> 16)
        return 0

    lax.fori_loop(0, (total + chunk - 1) // chunk, step, 0)


def dot(a, b):
    return jnp.dot(a, b, preferred_element_type=F32)


def product_cost(share):
    return pl.CostEstimate(
        flops=int(share * 160 * 2 * SIDE * SIDE * RANK), bytes_accessed=1 << 20, transcendentals=0
    )


def forward_near_kernel(counts, near, tiles, *rest):
    pieces, (total, held, sems) = rest[:6], rest[6:]
    copies = []
    for i, at in enumerate((0, 8, 16, 24, 48, 56)):
        copies.append(pltpu.make_async_copy(pieces[i], held.at[pl.ds(at, 8)], sems.at[i]))
    for one in copies:
        one.start()
    total[...] = jnp.zeros_like(total)
    for one in copies:
        one.wait()

    def body(slot, row, col):
        total[row] += dot(tiles[slot], held[col])

    listed(counts[0], near, 32, body)


def forward_near(counts, near, tiles, pieces):
    return pl.pallas_call(
        forward_near_kernel,
        out_shape=jax.ShapeDtypeStruct((33, SIDE, RANK), F32),
        in_specs=scalars(2) + whole(1) + anywhere(6),
        out_specs=whole(1)[0],
        scratch_shapes=[
            pltpu.VMEM((65, SIDE, RANK), BF16),
            pltpu.SemaphoreType.DMA((6,)),
        ],
        compiler_params=limits(8),
        cost_estimate=product_cost(0.75),
        name="forward_near",
    )(counts, near, tiles, *pieces)


def forward_far_kernel(counts, far, tiles, a, b, before, total, *rest):
    *aways, held, sems = rest
    copies = load_pieces([a, b], held, sems)
    for one in copies:
        one.wait()

    def body(slot, row, col):
        total[row] += dot(tiles[slot], held[jnp.minimum(col - 32, 16)])

    listed(counts[1], far, 16, body)
    for d, away in enumerate(aways):
        away[...] = total[pl.ds(16 + 4 * d, 4)]


def forward_far(counts, far, tiles, pieces, before):
    return pl.pallas_call(
        forward_far_kernel,
        out_shape=(jax.ShapeDtypeStruct((33, SIDE, RANK), F32),)
        + (jax.ShapeDtypeStruct((4, SIDE, RANK), F32),) * 4,
        in_specs=scalars(2) + whole(1) + anywhere(2) + whole(1),
        out_specs=tuple(whole(5)),
        scratch_shapes=[
            pltpu.VMEM((17, SIDE, RANK), BF16),
            pltpu.SemaphoreType.DMA((2,)),
        ],
        input_output_aliases={5: 0},
        compiler_params=limits(4),
        name="forward_far",
    )(counts, far, tiles, *pieces, before)


def backward_far_kernel(counts, far, tiles, *rest):
    pieces, (a, b, held, total, sems) = rest[:8], rest[8:]
    copies = load_pieces(pieces, held, sems)
    total[...] = jnp.zeros_like(total)
    for one in copies:
        one.wait()

    def body(slot, row, col):
        total[jnp.minimum(col - 32, 16)] += dot(held[row], tiles[slot])

    listed(counts[1], far, 16, body)
    a[...] = total[pl.ds(0, 8)].astype(BF16)
    b[...] = total[pl.ds(8, 8)].astype(BF16)


def backward_far(counts, far, tiles, pieces):
    part = jax.ShapeDtypeStruct((8, RANK, SIDE), BF16)
    return pl.pallas_call(
        backward_far_kernel,
        out_shape=(part, part),
        in_specs=scalars(2) + whole(1) + anywhere(8),
        out_specs=tuple(whole(2)),
        scratch_shapes=[
            pltpu.VMEM((33, RANK, SIDE), BF16),
            pltpu.VMEM((17, RANK, SIDE), F32),
            pltpu.SemaphoreType.DMA((8,)),
        ],
        compiler_params=limits(8),
        name="backward_far",
    )(counts, far, tiles, *pieces)


def backward_near_kernel(counts, near, tiles, *rest):
    pieces, (total, held, sems) = rest[:8], rest[8:]
    copies = load_pieces(pieces, held, sems)
    total[...] = jnp.zeros_like(total)
    for one in copies:
        one.wait()

    def body(slot, row, col):
        total[col] += dot(held[row], tiles[slot])

    listed(counts[0], near, 32, body)


def backward_near(counts, near, tiles, pieces):
    return pl.pallas_call(
        backward_near_kernel,
        out_shape=jax.ShapeDtypeStruct((65, RANK, SIDE), F32),
        in_specs=scalars(2) + whole(1) + anywhere(8),
        out_specs=whole(1)[0],
        scratch_shapes=[
            pltpu.VMEM((33, RANK, SIDE), BF16),
            pltpu.SemaphoreType.DMA((8,)),
        ],
        compiler_params=limits(6),
        cost_estimate=product_cost(0.75),
        name="backward_near",
    )(counts, near, tiles, *pieces)


def core_sum(keep, came, d):
    def kernel(keep, came, out):
        total = keep[pl.ds(4 * d, 4)] + came[...]
        largest = jnp.max(jnp.abs(total), axis=0)
        largest = jnp.max(jnp.max(largest, axis=0, keepdims=True), axis=1, keepdims=True)
        power = jnp.floor(jnp.log2(jnp.maximum(largest, 1e-30))) - 13.0
        scale = jnp.exp2(-power)
        for i in range(4):
            out[pl.ds(SIDE * i, SIDE), :] = total[i] * scale
        out[pl.ds(4 * SIDE, EXTRA), :] = jnp.broadcast_to(power, (EXTRA, RANK))

    return pl.pallas_call(
        kernel,
        out_shape=jax.ShapeDtypeStruct((4 * SIDE + EXTRA, RANK), F32),
        in_specs=whole(2),
        out_specs=whole(1)[0],
        compiler_params=limits(6),
        name="core_sum",
    )(keep, came)


def inner_kernel(keep, came, a, b, c, out):
    scales = [jnp.exp2(one[pl.ds(4 * SIDE, 1), :]) for one in (a, b, c)]
    for i in range(out.shape[0]):
        summed = keep[i] + came[i]
        for one, scale in zip((a, b, c), scales):
            summed += one[pl.ds(SIDE * i, SIDE), :] * scale
        out[i] = summed.T.astype(BF16)


def inner_sum(keep, came, parts):
    return pl.pallas_call(
        inner_kernel,
        out_shape=jax.ShapeDtypeStruct((4, RANK, SIDE), BF16),
        in_specs=whole(5),
        out_specs=whole(1)[0],
        compiler_params=limits(6),
        name="inner_sum",
    )(keep, came, *parts)


def relay_kernel(total, a, b, right, left):
    low, high = pl.ds(0, 8), pl.ds(8, 8)
    right[low] = (total[pl.ds(16, 8)] + a[...].astype(F32)).astype(BF16)
    right[high] = total[pl.ds(24, 8)].astype(BF16)
    left[low] = total[pl.ds(48, 8)].astype(BF16)
    left[high] = (total[pl.ds(56, 8)] + b[...].astype(F32)).astype(BF16)


def relay_sum(total, came):
    part = jax.ShapeDtypeStruct((16, RANK, SIDE), BF16)
    return pl.pallas_call(
        relay_kernel,
        out_shape=(part, part),
        in_specs=whole(3),
        out_specs=tuple(whole(2)),
        compiler_params=limits(6),
        name="relay_sum",
    )(total, *came)


def middle_kernel(total, a, b, keep, *aways):
    for d in range(4):
        at = pl.ds(4 * d, 4)
        one = total[at] + (a[at].astype(F32) + b[at].astype(F32))
        if d == 0:
            keep[...] = one
        else:
            aways[d - 1][...] = one.astype(BF16)


def middle_sum(total, came):
    part = jax.ShapeDtypeStruct((4, RANK, SIDE), BF16)
    keep, *aways = pl.pallas_call(
        middle_kernel,
        out_shape=(jax.ShapeDtypeStruct((4, RANK, SIDE), F32),) + (part,) * 3,
        in_specs=whole(3),
        out_specs=tuple(whole(4)),
        compiler_params=limits(6),
        name="middle_sum",
    )(total, *came)
    return keep, aways


def exact_dot(a, b, dims):
    return lax.dot_general(
        a, b, (dims, ((), ())), precision=lax.Precision.HIGHEST, preferred_element_type=F32
    )


def outer_kernel(keep, a, b, c, outer, gram):
    gram_total = jnp.zeros((RANK, RANK), F32)
    for i in range(outer.shape[0]):
        total = (keep[i] + a[i].astype(F32)) + (b[i].astype(F32) + c[i].astype(F32))
        outer[i] = total
        gram_total += exact_dot(total, total, ((1,), (1,)))
    gram[...] = gram_total


def outer_sum(keep, came):
    return pl.pallas_call(
        outer_kernel,
        out_shape=(
            jax.ShapeDtypeStruct((4, RANK, SIDE), F32),
            jax.ShapeDtypeStruct((RANK, RANK), F32),
        ),
        in_specs=whole(4),
        out_specs=tuple(whole(2)),
        compiler_params=limits(6),
        name="outer_sum",
    )(keep, *came)


def halved(value):
    large = value.astype(BF16)
    return large, (value - large.astype(F32)).astype(BF16)


def wide(value):
    return jnp.broadcast_to(value, (8, RANK))


def finish_kernel(scale, gram, outer, basis, factor, work):
    rows = lax.broadcasted_iota(jnp.int32, (RANK, RANK), 0)
    cols = lax.broadcasted_iota(jnp.int32, (RANK, RANK), 1)
    sub = lax.broadcasted_iota(jnp.int32, (8, RANK), 0)
    work[:, :RANK] = gram[...]
    work[:, RANK:] = jnp.where(rows == cols, 1.0, 0.0)
    for j in range(0, RANK, 8):
        halves = [work[j : j + 8, :RANK], work[j : j + 8, RANK:]]
        diag = [
            [wide(halves[0][r : r + 1, j + s : j + s + 1]) for s in range(r + 1)]
            for r in range(8)
        ]
        upper = [[wide(half[r : r + 1, :]) for half in halves] for r in range(8)]
        lower = [[None] * 8 for _ in range(8)]
        root = [None] * 8
        for i in range(8):
            root[i] = lax.rsqrt(diag[i][i])
            for r in range(i + 1, 8):
                lower[r][i] = diag[r][i] * root[i]
            for r in range(i + 1, 8):
                for s in range(i + 1, r + 1):
                    diag[r][s] = diag[r][s] - lower[r][i] * lower[s][i]
            upper[i] = [one * root[i] for one in upper[i]]
            for r in range(i + 1, 8):
                upper[r] = [a - lower[r][i] * b for a, b in zip(upper[r], upper[i])]
        for h in range(2):
            panel = upper[0][h]
            for r in range(1, 8):
                panel = jnp.where(sub == r, upper[r][h], panel)
            work[j : j + 8, h * RANK : (h + 1) * RANK] = panel
        for g in range(j + 8, RANK, 8):
            halves = [work[g : g + 8, :RANK], work[g : g + 8, RANK:]]
            column = []
            for k in range(8):
                one = wide(halves[0][:, j + k : j + k + 1])
                for i in range(k):
                    one = one - column[i] * lower[k][i]
                column.append(one * root[k])
            for h in range(2):
                block = halves[h]
                for k in range(8):
                    block = block - column[k] * upper[k][h]
                work[g : g + 8, h * RANK : (h + 1) * RANK] = block
    factor[...] = jnp.where(cols >= rows, work[:, :RANK], 0.0) * (1.0 / scale)
    inverse, rest = halved(work[:, RANK:] * scale)
    for b in range(outer.shape[0]):
        large, small = halved(outer[b])
        product = dot(inverse, large) + (dot(rest, large) + dot(inverse, small))
        basis[pl.ds(b * SIDE, SIDE), :] = product.T


def finish(gram, outer, entities):
    scale = float(entities) ** 0.5

    def kernel(*refs):
        finish_kernel(scale, *refs)

    return pl.pallas_call(
        kernel,
        out_shape=(
            jax.ShapeDtypeStruct((4 * SIDE, RANK), F32),
            jax.ShapeDtypeStruct((RANK, RANK), F32),
        ),
        in_specs=whole(2),
        out_specs=tuple(whole(2)),
        scratch_shapes=[pltpu.VMEM((RANK, 2 * RANK), F32)],
        compiler_params=limits(6),
        name="finish",
    )(gram, outer)


def shards(basis_in, tiles, tile_coords, tile_count):
    x, y, z, core = (lax.axis_index(name) for name in AXES)
    local_row = tile_coords[:, 0] - (x * 4 + y) * 32
    dz = (local_row // 8 - z) % 4
    dc = (local_row // 4 - core) % 2
    row_at = dc * 16 + dz * 4 + local_row % 4
    row_group = tile_coords[:, 1] // 32
    b = tile_coords[:, 1] % 4
    dx = (row_group // 4 - x) % 4
    dy = (row_group % 4 - y) % 4
    near_axes, far_axes = ("x", "y"), ("y", "x")
    near_at = jnp.where(core == 0, dx, dy)
    far_at = jnp.where(core == 0, dy, dx)
    col_at = far_at * 16 + near_at * 4 + b

    with jax.named_scope("gather_basis"):
        near = [basis_in] + [cross(basis_in, near_axes, -d) for d in (1, 2, 3)]
        held, counts, near_list, far_list = plan_tiles(tile_count, row_at, col_at, tiles)
        near, held = lax.optimization_barrier((near, held))
        low, high = (
            jnp.concatenate(pair, axis=0).reshape(8, SIDE, RANK) for pair in (near[:2], near[2:])
        )
        right_low, left_high = cross(low, far_axes, 1), cross(high, far_axes, -1)
        left_low, right_high = cross(low, far_axes, -1), cross(high, far_axes, 1)
        over = (cross(right_low, far_axes, 1), cross(left_high, far_axes, -1))

    keep = forward_near(
        counts, near_list, held, (low, high, left_low, left_high, right_low, right_high)
    )
    keep, *aways = forward_far(counts, far_list, held, over, keep)

    with jax.named_scope("reduce_inner"):
        parts = []
        for d in (2, 1, 3):
            one = core_sum(keep, send(aways[d], "core", 1), d)
            parts.append(send(one.astype(jnp.float16), "z", d).astype(F32))
        inner = inner_sum(keep, send(aways[0], "core", 1), parts)

    with jax.named_scope("gather_inner"):
        mine = [inner] + [send(inner, "z", -d) for d in (1, 2, 3)]
        theirs = [send(one, "core", 1) for one in mine]

    aways = backward_far(counts, far_list, held, mine + theirs)

    with jax.named_scope("reduce_outer"):
        came = (cross(aways[0], far_axes, 1), cross(aways[1], far_axes, -1))
        total = backward_near(counts, near_list, held, mine + theirs)
        right, left = relay_sum(total, came)
        came = (cross(right, far_axes, 1), cross(left, far_axes, -1))
        keep, aways = middle_sum(total, came)
        came = [cross(one, near_axes, d) for d, one in zip((1, 2, 3), aways)]
        outer, gram = outer_sum(keep, came)

    with jax.named_scope("reduce_gram"):
        gram = gram + send(gram, "core", 1)
        for axis in ("z", "y", "x"):
            parts = [send(gram, axis, d) for d in (1, 2, 3)]
            gram = (gram + parts[1]) + (parts[0] + parts[2])

    entities = basis_in.shape[0] * 128
    return finish(gram, outer, entities)


def solution(mesh):
    split = Mesh(mesh.devices.reshape(4, 4, 4, 2), AXES)
    placed = (P(AXES, None), P(AXES, None, None), P(AXES, None), P(AXES))
    return jax.shard_map(
        shards,
        mesh=split,
        in_specs=placed,
        out_specs=(P(AXES, None), P()),
        check_vma=False,
    )
```

```python
import itertools

import jax
import jax.numpy as jnp
from jax import lax
from jax.experimental import pallas as pl
from jax.experimental.pallas import tpu as pltpu
from jax.sharding import Mesh, PartitionSpec as P

AXES = ("x", "y", "z", "core")
SIZES = {"x": 4, "y": 4, "z": 4, "core": 2}
SIDE = 256
RANK = 128
CHUNK = 32
EXTRA = 16
SPARE = 32 * 256 + 64 * 65536
F32 = jnp.float32
BF16 = jnp.bfloat16


def send(array, axis, step):
    size = SIZES[axis]
    return lax.ppermute(array, axis, [(i, (i + step) % size) for i in range(size)])


def cross(array, axes, step):
    names = AXES[:3]
    pairs = []
    for place in itertools.product(*(range(SIZES[name]) for name in AXES)):
        there = list(place)
        at = names.index(axes[place[3]])
        there[at] = (there[at] + step) % SIZES[names[at]]
        pairs.append((linear(place), linear(there)))
    return lax.ppermute(array, AXES, pairs)


def linear(place):
    index = 0
    for name, one in zip(AXES, place):
        index = index * SIZES[name] + one
    return index


def limits(mib):
    return pltpu.CompilerParams(vmem_limit_bytes=mib * 1024 * 1024)


def whole(count):
    return [pl.BlockSpec(memory_space=pltpu.VMEM)] * count


def load_pieces(pieces, held, sems):
    copies = []
    at = 0
    for i, piece in enumerate(pieces):
        rows = piece.shape[0]
        copies.append(pltpu.make_async_copy(piece, held.at[pl.ds(at, rows)], sems.at[i]))
        at += rows
    for copy in copies:
        copy.start()
    return copies


def hold_copies(count, tiles, held, sems):
    chunks = (count[0] + CHUNK - 1) // CHUNK

    def copy(i):
        at = pl.ds(i * CHUNK, CHUNK)
        return pltpu.make_async_copy(tiles.at[at], held.at[at], sems.at[i])

    def start(i, _):
        copy(i).start()
        return 0

    def wait(i, _):
        copy(i).wait()
        return 0

    return (lambda: lax.fori_loop(0, chunks, start, 0)), (
        lambda: lax.fori_loop(0, chunks, wait, 0)
    )


def plan_kernel(count, row_at, col_at, tiles, held, counts, near, far, sems):
    start, wait = hold_copies(count, tiles, held, sems)
    start()

    def place(slot, ends):
        near_end, far_end = ends
        col = col_at[slot]
        entry = slot + row_at[slot] * 256 + col * 65536
        near[near_end] = entry
        far[far_end] = entry
        over = (col >> 4 == 2).astype(jnp.int32)
        return near_end + 1 - over, far_end + over

    zero = jnp.int32(0)
    near_end, far_end = lax.fori_loop(0, count[0], place, (zero, zero))
    for k in range(CHUNK):
        near[near_end + k] = SPARE
        far[far_end + k] = SPARE
    counts[0] = near_end
    counts[1] = far_end
    wait()


def hold_parameters(tiles):
    return dict(
        scratch_shapes=[pltpu.SemaphoreType.DMA((tiles.shape[0] // CHUNK,))],
        compiler_params=limits(22),
        cost_estimate=pl.CostEstimate(
            flops=0, bytes_accessed=2 * tiles.size * tiles.dtype.itemsize, transcendentals=0
        ),
    )


def scalars(count):
    return [pl.BlockSpec(memory_space=pltpu.SMEM)] * count


def anywhere(count):
    return [pl.BlockSpec(memory_space=pl.ANY)] * count


def plan_tiles(count, row_at, col_at, tiles):
    entries = jax.ShapeDtypeStruct((tiles.shape[0] + CHUNK,), jnp.int32)
    return pl.pallas_call(
        plan_kernel,
        out_shape=(
            jax.ShapeDtypeStruct(tiles.shape, tiles.dtype),
            jax.ShapeDtypeStruct((2,), jnp.int32),
            entries,
            entries,
        ),
        in_specs=scalars(3) + anywhere(1),
        out_specs=tuple(whole(1) + scalars(3)),
        name="plan_tiles",
        **hold_parameters(tiles),
    )(count, row_at, col_at, tiles)


def listed(total, entries, chunk, body):
    def step(i, _):
        for k in range(chunk):
            entry = entries[i * chunk + k]
            body(entry & 255, (entry >> 8) & 255, entry >> 16)
        return 0

    lax.fori_loop(0, (total + chunk - 1) // chunk, step, 0)


def dot(a, b):
    return jnp.dot(a, b, preferred_element_type=F32)


def product_cost(share):
    return pl.CostEstimate(
        flops=int(share * 160 * 2 * SIDE * SIDE * RANK), bytes_accessed=1 << 20, transcendentals=0
    )


def forward_near_kernel(counts, near, tiles, *rest):
    pieces, (total, held, sems) = rest[:6], rest[6:]
    copies = []
    for i, at in enumerate((0, 8, 16, 24, 48, 56)):
        copies.append(pltpu.make_async_copy(pieces[i], held.at[pl.ds(at, 8)], sems.at[i]))
    for one in copies:
        one.start()
    total[...] = jnp.zeros_like(total)
    for one in copies:
        one.wait()

    def body(slot, row, col):
        total[row] += dot(tiles[slot], held[col])

    listed(counts[0], near, 32, body)


def forward_near(counts, near, tiles, pieces):
    return pl.pallas_call(
        forward_near_kernel,
        out_shape=jax.ShapeDtypeStruct((33, SIDE, RANK), F32),
        in_specs=scalars(2) + whole(1) + anywhere(6),
        out_specs=whole(1)[0],
        scratch_shapes=[
            pltpu.VMEM((65, SIDE, RANK), BF16),
            pltpu.SemaphoreType.DMA((6,)),
        ],
        compiler_params=limits(8),
        cost_estimate=product_cost(0.75),
        name="forward_near",
    )(counts, near, tiles, *pieces)


def forward_far_kernel(counts, far, tiles, a, b, before, total, *rest):
    *aways, held, sems = rest
    copies = load_pieces([a, b], held, sems)
    for one in copies:
        one.wait()

    def body(slot, row, col):
        total[row] += dot(tiles[slot], held[jnp.minimum(col - 32, 16)])

    listed(counts[1], far, 16, body)
    for d, away in enumerate(aways):
        away[...] = total[pl.ds(16 + 4 * d, 4)]


def forward_far(counts, far, tiles, pieces, before):
    return pl.pallas_call(
        forward_far_kernel,
        out_shape=(jax.ShapeDtypeStruct((33, SIDE, RANK), F32),)
        + (jax.ShapeDtypeStruct((4, SIDE, RANK), F32),) * 4,
        in_specs=scalars(2) + whole(1) + anywhere(2) + whole(1),
        out_specs=tuple(whole(5)),
        scratch_shapes=[
            pltpu.VMEM((17, SIDE, RANK), BF16),
            pltpu.SemaphoreType.DMA((2,)),
        ],
        input_output_aliases={5: 0},
        compiler_params=limits(4),
        name="forward_far",
    )(counts, far, tiles, *pieces, before)


def backward_far_kernel(counts, far, tiles, *rest):
    pieces, (a, b, held, total, sems) = rest[:8], rest[8:]
    copies = load_pieces(pieces, held, sems)
    total[...] = jnp.zeros_like(total)
    for one in copies:
        one.wait()

    def body(slot, row, col):
        total[jnp.minimum(col - 32, 16)] += dot(held[row], tiles[slot])

    listed(counts[1], far, 16, body)
    a[...] = total[pl.ds(0, 8)].astype(BF16)
    b[...] = total[pl.ds(8, 8)].astype(BF16)


def backward_far(counts, far, tiles, pieces):
    part = jax.ShapeDtypeStruct((8, RANK, SIDE), BF16)
    return pl.pallas_call(
        backward_far_kernel,
        out_shape=(part, part),
        in_specs=scalars(2) + whole(1) + anywhere(8),
        out_specs=tuple(whole(2)),
        scratch_shapes=[
            pltpu.VMEM((33, RANK, SIDE), BF16),
            pltpu.VMEM((17, RANK, SIDE), F32),
            pltpu.SemaphoreType.DMA((8,)),
        ],
        compiler_params=limits(8),
        name="backward_far",
    )(counts, far, tiles, *pieces)


def backward_near_kernel(counts, near, tiles, *rest):
    pieces, (total, right, left, held, sems) = rest[:8], rest[8:]
    copies = load_pieces(pieces, held, sems)
    total[...] = jnp.zeros_like(total)
    for one in copies:
        one.wait()

    def body(slot, row, col):
        total[col] += dot(held[row], tiles[slot])

    listed(counts[0], near, 32, body)
    right[...] = total[pl.ds(24, 8)].astype(BF16)
    left[...] = total[pl.ds(48, 8)].astype(BF16)


def backward_near(counts, near, tiles, pieces):
    part = jax.ShapeDtypeStruct((8, RANK, SIDE), BF16)
    return pl.pallas_call(
        backward_near_kernel,
        out_shape=(jax.ShapeDtypeStruct((65, RANK, SIDE), F32), part, part),
        in_specs=scalars(2) + whole(1) + anywhere(8),
        out_specs=tuple(whole(3)),
        scratch_shapes=[
            pltpu.VMEM((33, RANK, SIDE), BF16),
            pltpu.SemaphoreType.DMA((8,)),
        ],
        compiler_params=limits(6),
        cost_estimate=product_cost(0.75),
        name="backward_near",
    )(counts, near, tiles, *pieces)


def core_sum(keep, came, d):
    def kernel(keep, came, out):
        total = keep[pl.ds(4 * d, 4)] + came[...]
        largest = jnp.max(jnp.abs(total), axis=0)
        largest = jnp.max(jnp.max(largest, axis=0, keepdims=True), axis=1, keepdims=True)
        power = jnp.floor(jnp.log2(jnp.maximum(largest, 1e-30))) - 13.0
        scale = jnp.exp2(-power)
        for i in range(4):
            out[pl.ds(SIDE * i, SIDE), :] = total[i] * scale
        out[pl.ds(4 * SIDE, EXTRA), :] = jnp.broadcast_to(power, (EXTRA, RANK))

    return pl.pallas_call(
        kernel,
        out_shape=jax.ShapeDtypeStruct((4 * SIDE + EXTRA, RANK), F32),
        in_specs=whole(2),
        out_specs=whole(1)[0],
        compiler_params=limits(6),
        name="core_sum",
    )(keep, came)


def inner_kernel(keep, came, a, b, c, out):
    scales = [jnp.exp2(one[pl.ds(4 * SIDE, 1), :]) for one in (a, b, c)]
    for i in range(out.shape[0]):
        summed = keep[i] + came[i]
        for one, scale in zip((a, b, c), scales):
            summed += one[pl.ds(SIDE * i, SIDE), :] * scale
        out[i] = summed.T.astype(BF16)


def inner_sum(keep, came, parts):
    return pl.pallas_call(
        inner_kernel,
        out_shape=jax.ShapeDtypeStruct((4, RANK, SIDE), BF16),
        in_specs=whole(5),
        out_specs=whole(1)[0],
        compiler_params=limits(6),
        name="inner_sum",
    )(keep, came, *parts)


def relay_kernel(total, a, b, right, left):
    right[...] = (total[pl.ds(16, 8)] + a[...].astype(F32)).astype(BF16)
    left[...] = (total[pl.ds(56, 8)] + b[...].astype(F32)).astype(BF16)


def relay_sum(total, came):
    part = jax.ShapeDtypeStruct((8, RANK, SIDE), BF16)
    return pl.pallas_call(
        relay_kernel,
        out_shape=(part, part),
        in_specs=whole(3),
        out_specs=tuple(whole(2)),
        compiler_params=limits(6),
        name="relay_sum",
    )(total, *came)


def middle_kernel(total, *rest):
    halves, (keep, *aways) = (rest[:2], rest[2:4]), rest[4:]
    for d in range(4):
        a, b = halves[d // 2]
        at = pl.ds(4 * (d % 2), 4)
        one = total[pl.ds(4 * d, 4)] + (a[at].astype(F32) + b[at].astype(F32))
        if d == 0:
            keep[...] = one
        else:
            aways[d - 1][...] = one.astype(BF16)


def middle_sum(total, came):
    part = jax.ShapeDtypeStruct((4, RANK, SIDE), BF16)
    keep, *aways = pl.pallas_call(
        middle_kernel,
        out_shape=(jax.ShapeDtypeStruct((4, RANK, SIDE), F32),) + (part,) * 3,
        in_specs=whole(5),
        out_specs=tuple(whole(4)),
        compiler_params=limits(6),
        name="middle_sum",
    )(total, *came)
    return keep, aways


def exact_dot(a, b, dims):
    return lax.dot_general(
        a, b, (dims, ((), ())), precision=lax.Precision.HIGHEST, preferred_element_type=F32
    )


def outer_kernel(keep, a, b, c, outer, gram):
    gram_total = jnp.zeros((RANK, RANK), F32)
    for i in range(outer.shape[0]):
        total = (keep[i] + a[i].astype(F32)) + (b[i].astype(F32) + c[i].astype(F32))
        outer[i] = total
        gram_total += exact_dot(total, total, ((1,), (1,)))
    gram[...] = gram_total


def outer_sum(keep, came):
    return pl.pallas_call(
        outer_kernel,
        out_shape=(
            jax.ShapeDtypeStruct((4, RANK, SIDE), F32),
            jax.ShapeDtypeStruct((RANK, RANK), F32),
        ),
        in_specs=whole(4),
        out_specs=tuple(whole(2)),
        compiler_params=limits(6),
        name="outer_sum",
    )(keep, *came)


def halved(value):
    large = value.astype(BF16)
    return large, (value - large.astype(F32)).astype(BF16)


def wide(value):
    return jnp.broadcast_to(value, (8, RANK))


def finish_kernel(scale, gram, outer, basis, factor, work):
    rows = lax.broadcasted_iota(jnp.int32, (RANK, RANK), 0)
    cols = lax.broadcasted_iota(jnp.int32, (RANK, RANK), 1)
    sub = lax.broadcasted_iota(jnp.int32, (8, RANK), 0)
    work[:, :RANK] = gram[...]
    work[:, RANK:] = jnp.where(rows == cols, 1.0, 0.0)
    for j in range(0, RANK, 8):
        halves = [work[j : j + 8, :RANK], work[j : j + 8, RANK:]]
        diag = [
            [wide(halves[0][r : r + 1, j + s : j + s + 1]) for s in range(r + 1)]
            for r in range(8)
        ]
        upper = [[wide(half[r : r + 1, :]) for half in halves] for r in range(8)]
        lower = [[None] * 8 for _ in range(8)]
        root = [None] * 8
        for i in range(8):
            root[i] = lax.rsqrt(diag[i][i])
            for r in range(i + 1, 8):
                lower[r][i] = diag[r][i] * root[i]
            for r in range(i + 1, 8):
                for s in range(i + 1, r + 1):
                    diag[r][s] = diag[r][s] - lower[r][i] * lower[s][i]
            upper[i] = [one * root[i] for one in upper[i]]
            for r in range(i + 1, 8):
                upper[r] = [a - lower[r][i] * b for a, b in zip(upper[r], upper[i])]
        for h in range(2):
            panel = upper[0][h]
            for r in range(1, 8):
                panel = jnp.where(sub == r, upper[r][h], panel)
            work[j : j + 8, h * RANK : (h + 1) * RANK] = panel
        for g in range(j + 8, RANK, 8):
            halves = [work[g : g + 8, :RANK], work[g : g + 8, RANK:]]
            column = []
            for k in range(8):
                one = wide(halves[0][:, j + k : j + k + 1])
                for i in range(k):
                    one = one - column[i] * lower[k][i]
                column.append(one * root[k])
            for h in range(2):
                block = halves[h]
                for k in range(8):
                    block = block - column[k] * upper[k][h]
                work[g : g + 8, h * RANK : (h + 1) * RANK] = block
    factor[...] = jnp.where(cols >= rows, work[:, :RANK], 0.0) * (1.0 / scale)
    inverse, rest = halved(work[:, RANK:] * scale)
    for b in range(outer.shape[0]):
        large, small = halved(outer[b])
        product = dot(inverse, large) + (dot(rest, large) + dot(inverse, small))
        basis[pl.ds(b * SIDE, SIDE), :] = product.T


def finish(gram, outer, entities):
    scale = float(entities) ** 0.5

    def kernel(*refs):
        finish_kernel(scale, *refs)

    return pl.pallas_call(
        kernel,
        out_shape=(
            jax.ShapeDtypeStruct((4 * SIDE, RANK), F32),
            jax.ShapeDtypeStruct((RANK, RANK), F32),
        ),
        in_specs=whole(2),
        out_specs=tuple(whole(2)),
        scratch_shapes=[pltpu.VMEM((RANK, 2 * RANK), F32)],
        compiler_params=limits(6),
        name="finish",
    )(gram, outer)


def shards(basis_in, tiles, tile_coords, tile_count):
    x, y, z, core = (lax.axis_index(name) for name in AXES)
    local_row = tile_coords[:, 0] - (x * 4 + y) * 32
    dz = (local_row // 8 - z) % 4
    dc = (local_row // 4 - core) % 2
    row_at = dc * 16 + dz * 4 + local_row % 4
    row_group = tile_coords[:, 1] // 32
    b = tile_coords[:, 1] % 4
    dx = (row_group // 4 - x) % 4
    dy = (row_group % 4 - y) % 4
    near_axes, far_axes = ("x", "y"), ("y", "x")
    near_at = jnp.where(core == 0, dx, dy)
    far_at = jnp.where(core == 0, dy, dx)
    col_at = far_at * 16 + near_at * 4 + b

    with jax.named_scope("gather_basis"):
        near = [basis_in] + [cross(basis_in, near_axes, -d) for d in (1, 2, 3)]
        held, counts, near_list, far_list = plan_tiles(tile_count, row_at, col_at, tiles)
        near, held = lax.optimization_barrier((near, held))
        low, high = (
            jnp.concatenate(pair, axis=0).reshape(8, SIDE, RANK) for pair in (near[:2], near[2:])
        )
        right_low, left_high = cross(low, far_axes, 1), cross(high, far_axes, -1)
        left_low, right_high = cross(low, far_axes, -1), cross(high, far_axes, 1)
        over = (cross(right_low, far_axes, 1), cross(left_high, far_axes, -1))

    keep = forward_near(
        counts, near_list, held, (low, high, left_low, left_high, right_low, right_high)
    )
    keep, *aways = forward_far(counts, far_list, held, over, keep)

    with jax.named_scope("reduce_inner"):
        parts = []
        for d in (2, 1, 3):
            one = core_sum(keep, send(aways[d], "core", 1), d)
            parts.append(send(one.astype(jnp.float16), "z", d).astype(F32))
        inner = inner_sum(keep, send(aways[0], "core", 1), parts)

    with jax.named_scope("gather_inner"):
        mine = [inner] + [send(inner, "z", -d) for d in (1, 2, 3)]
        theirs = [send(one, "core", 1) for one in mine]

    aways = backward_far(counts, far_list, held, mine + theirs)

    with jax.named_scope("reduce_outer"):
        over = (cross(aways[0], far_axes, 1), cross(aways[1], far_axes, -1))
        total, right_high, left_low = backward_near(counts, near_list, held, mine + theirs)
        right_high, left_low = cross(right_high, far_axes, 1), cross(left_low, far_axes, -1)
        right_low, left_high = relay_sum(total, over)
        right_low, left_high = cross(right_low, far_axes, 1), cross(left_high, far_axes, -1)
        came = (right_low, left_low, right_high, left_high)
        keep, aways = middle_sum(total, came)
        came = [cross(one, near_axes, d) for d, one in zip((1, 2, 3), aways)]
        outer, gram = outer_sum(keep, came)

    with jax.named_scope("reduce_gram"):
        gram = gram + send(gram, "core", 1)
        for axis in ("z", "y", "x"):
            parts = [send(gram, axis, d) for d in (1, 2, 3)]
            gram = (gram + parts[1]) + (parts[0] + parts[2])

    entities = basis_in.shape[0] * 128
    return finish(gram, outer, entities)


def solution(mesh):
    split = Mesh(mesh.devices.reshape(4, 4, 4, 2), AXES)
    placed = (P(AXES, None), P(AXES, None, None), P(AXES, None), P(AXES))
    return jax.shard_map(
        shards,
        mesh=split,
        in_specs=placed,
        out_specs=(P(AXES, None), P()),
        check_vma=False,
    )
```

```python
import itertools

import jax
import jax.numpy as jnp
from jax import lax
from jax.experimental import pallas as pl
from jax.experimental.pallas import tpu as pltpu
from jax.sharding import Mesh, PartitionSpec as P

AXES = ("x", "y", "z", "core")
SIZES = {"x": 4, "y": 4, "z": 4, "core": 2}
SIDE = 256
RANK = 128
CHUNK = 32
EARLY = 3
EXTRA = 16
SPARE = 32 * 256 + 64 * 65536
F32 = jnp.float32
BF16 = jnp.bfloat16


def send(array, axis, step):
    size = SIZES[axis]
    return lax.ppermute(array, axis, [(i, (i + step) % size) for i in range(size)])


def cross(array, axes, step):
    names = AXES[:3]
    pairs = []
    for place in itertools.product(*(range(SIZES[name]) for name in AXES)):
        there = list(place)
        at = names.index(axes[place[3]])
        there[at] = (there[at] + step) % SIZES[names[at]]
        pairs.append((linear(place), linear(there)))
    return lax.ppermute(array, AXES, pairs)


def linear(place):
    index = 0
    for name, one in zip(AXES, place):
        index = index * SIZES[name] + one
    return index


def limits(mib):
    return pltpu.CompilerParams(vmem_limit_bytes=mib * 1024 * 1024)


def whole(count):
    return [pl.BlockSpec(memory_space=pltpu.VMEM)] * count


def load_pieces(pieces, held, sems):
    copies = []
    at = 0
    for i, piece in enumerate(pieces):
        rows = piece.shape[0]
        copies.append(pltpu.make_async_copy(piece, held.at[pl.ds(at, rows)], sems.at[i]))
        at += rows
    for copy in copies:
        copy.start()
    return copies


def hold_copies(count, tiles, held, sems, first, last):
    end = jnp.clip((count[0] + CHUNK - 1) // CHUNK, first, last)

    def copy(i):
        at = pl.ds(i * CHUNK, CHUNK)
        return pltpu.make_async_copy(tiles.at[at], held.at[at], sems.at[i])

    def start(i, _):
        copy(i).start()
        return 0

    def wait(i, _):
        copy(i).wait()
        return 0

    return (lambda: lax.fori_loop(first, end, start, 0)), (
        lambda: lax.fori_loop(first, end, wait, 0)
    )


def rest_kernel(count, tiles, before, held, sems):
    start, wait = hold_copies(count, tiles, held, sems, EARLY, sems.shape[0])
    start()
    wait()


def plan_kernel(count, row_at, col_at, tiles, held, counts, near, far, sems):
    start, wait = hold_copies(count, tiles, held, sems, 0, EARLY)
    start()

    def place(slot, ends):
        near_end, far_end = ends
        col = col_at[slot]
        entry = slot + row_at[slot] * 256 + col * 65536
        near[near_end] = entry
        far[far_end] = entry
        over = (col >> 4 == 2).astype(jnp.int32)
        return near_end + 1 - over, far_end + over

    zero = jnp.int32(0)
    near_end, far_end = lax.fori_loop(0, count[0], place, (zero, zero))
    for k in range(CHUNK):
        near[near_end + k] = SPARE
        far[far_end + k] = SPARE
    counts[0] = near_end
    counts[1] = far_end
    wait()


def hold_parameters(tiles):
    return dict(
        scratch_shapes=[pltpu.SemaphoreType.DMA((tiles.shape[0] // CHUNK,))],
        compiler_params=limits(22),
        cost_estimate=pl.CostEstimate(
            flops=0, bytes_accessed=2 * tiles.size * tiles.dtype.itemsize, transcendentals=0
        ),
    )


def scalars(count):
    return [pl.BlockSpec(memory_space=pltpu.SMEM)] * count


def anywhere(count):
    return [pl.BlockSpec(memory_space=pl.ANY)] * count


def plan_tiles(count, row_at, col_at, tiles):
    entries = jax.ShapeDtypeStruct((tiles.shape[0] + CHUNK,), jnp.int32)
    return pl.pallas_call(
        plan_kernel,
        out_shape=(
            jax.ShapeDtypeStruct(tiles.shape, tiles.dtype),
            jax.ShapeDtypeStruct((2,), jnp.int32),
            entries,
            entries,
        ),
        in_specs=scalars(3) + anywhere(1),
        out_specs=tuple(whole(1) + scalars(3)),
        name="plan_tiles",
        **hold_parameters(tiles),
    )(count, row_at, col_at, tiles)


def hold_rest(count, tiles, held):
    return pl.pallas_call(
        rest_kernel,
        out_shape=jax.ShapeDtypeStruct(tiles.shape, tiles.dtype),
        in_specs=scalars(1) + anywhere(1) + whole(1),
        out_specs=whole(1)[0],
        input_output_aliases={2: 0},
        name="hold_rest",
        **hold_parameters(tiles),
    )(count, tiles, held)


def listed(total, entries, chunk, body):
    def step(i, _):
        for k in range(chunk):
            entry = entries[i * chunk + k]
            body(entry & 255, (entry >> 8) & 255, entry >> 16)
        return 0

    lax.fori_loop(0, (total + chunk - 1) // chunk, step, 0)


def dot(a, b):
    return jnp.dot(a, b, preferred_element_type=F32)


def product_cost(share):
    return pl.CostEstimate(
        flops=int(share * 160 * 2 * SIDE * SIDE * RANK), bytes_accessed=1 << 20, transcendentals=0
    )


def forward_near_kernel(counts, near, tiles, *rest):
    pieces, (total, held, sems) = rest[:6], rest[6:]
    copies = []
    for i, at in enumerate((0, 8, 16, 24, 48, 56)):
        copies.append(pltpu.make_async_copy(pieces[i], held.at[pl.ds(at, 8)], sems.at[i]))
    for one in copies:
        one.start()
    total[...] = jnp.zeros_like(total)
    for one in copies:
        one.wait()

    def body(slot, row, col):
        total[row] += dot(tiles[slot], held[col])

    listed(counts[0], near, 32, body)


def forward_near(counts, near, tiles, pieces):
    return pl.pallas_call(
        forward_near_kernel,
        out_shape=jax.ShapeDtypeStruct((33, SIDE, RANK), F32),
        in_specs=scalars(2) + whole(1) + anywhere(6),
        out_specs=whole(1)[0],
        scratch_shapes=[
            pltpu.VMEM((65, SIDE, RANK), BF16),
            pltpu.SemaphoreType.DMA((6,)),
        ],
        compiler_params=limits(8),
        cost_estimate=product_cost(0.75),
        name="forward_near",
    )(counts, near, tiles, *pieces)


def forward_far_kernel(counts, far, tiles, a, b, before, total, *rest):
    *aways, held, sems = rest
    copies = load_pieces([a, b], held, sems)
    for one in copies:
        one.wait()

    def body(slot, row, col):
        total[row] += dot(tiles[slot], held[jnp.minimum(col - 32, 16)])

    listed(counts[1], far, 16, body)
    for d, away in enumerate(aways):
        away[...] = total[pl.ds(16 + 4 * d, 4)]


def forward_far(counts, far, tiles, pieces, before):
    return pl.pallas_call(
        forward_far_kernel,
        out_shape=(jax.ShapeDtypeStruct((33, SIDE, RANK), F32),)
        + (jax.ShapeDtypeStruct((4, SIDE, RANK), F32),) * 4,
        in_specs=scalars(2) + whole(1) + anywhere(2) + whole(1),
        out_specs=tuple(whole(5)),
        scratch_shapes=[
            pltpu.VMEM((17, SIDE, RANK), BF16),
            pltpu.SemaphoreType.DMA((2,)),
        ],
        input_output_aliases={5: 0},
        compiler_params=limits(4),
        name="forward_far",
    )(counts, far, tiles, *pieces, before)


def backward_far_kernel(counts, far, tiles, *rest):
    pieces, (a, b, held, total, sems) = rest[:8], rest[8:]
    copies = load_pieces(pieces, held, sems)
    total[...] = jnp.zeros_like(total)
    for one in copies:
        one.wait()

    def body(slot, row, col):
        total[jnp.minimum(col - 32, 16)] += dot(held[row], tiles[slot])

    listed(counts[1], far, 16, body)
    a[...] = total[pl.ds(0, 8)].astype(BF16)
    b[...] = total[pl.ds(8, 8)].astype(BF16)


def backward_far(counts, far, tiles, pieces):
    part = jax.ShapeDtypeStruct((8, RANK, SIDE), BF16)
    return pl.pallas_call(
        backward_far_kernel,
        out_shape=(part, part),
        in_specs=scalars(2) + whole(1) + anywhere(8),
        out_specs=tuple(whole(2)),
        scratch_shapes=[
            pltpu.VMEM((33, RANK, SIDE), BF16),
            pltpu.VMEM((17, RANK, SIDE), F32),
            pltpu.SemaphoreType.DMA((8,)),
        ],
        compiler_params=limits(8),
        name="backward_far",
    )(counts, far, tiles, *pieces)


def backward_near_kernel(counts, near, tiles, *rest):
    pieces, (total, right, left, held, sems) = rest[:8], rest[8:]
    copies = load_pieces(pieces, held, sems)
    total[pl.ds(0, 32)] = jnp.zeros((32, RANK, SIDE), F32)
    total[pl.ds(48, 17)] = jnp.zeros((17, RANK, SIDE), F32)
    for one in copies:
        one.wait()

    def body(slot, row, col):
        total[col] += dot(held[row], tiles[slot])

    listed(counts[0], near, 32, body)
    right[...] = total[pl.ds(24, 8)].astype(BF16)
    left[...] = total[pl.ds(48, 8)].astype(BF16)


def backward_near(counts, near, tiles, pieces):
    part = jax.ShapeDtypeStruct((8, RANK, SIDE), BF16)
    return pl.pallas_call(
        backward_near_kernel,
        out_shape=(jax.ShapeDtypeStruct((65, RANK, SIDE), F32), part, part),
        in_specs=scalars(2) + whole(1) + anywhere(8),
        out_specs=tuple(whole(3)),
        scratch_shapes=[
            pltpu.VMEM((33, RANK, SIDE), BF16),
            pltpu.SemaphoreType.DMA((8,)),
        ],
        compiler_params=limits(6),
        cost_estimate=product_cost(0.75),
        name="backward_near",
    )(counts, near, tiles, *pieces)


def core_sum(keep, came, d):
    def kernel(keep, came, out):
        total = keep[pl.ds(4 * d, 4)] + came[...]
        largest = jnp.max(jnp.abs(total), axis=0)
        largest = jnp.max(jnp.max(largest, axis=0, keepdims=True), axis=1, keepdims=True)
        power = jnp.floor(jnp.log2(jnp.maximum(largest, 1e-30))) - 13.0
        scale = jnp.exp2(-power)
        for i in range(4):
            out[pl.ds(SIDE * i, SIDE), :] = total[i] * scale
        out[pl.ds(4 * SIDE, EXTRA), :] = jnp.broadcast_to(power, (EXTRA, RANK))

    return pl.pallas_call(
        kernel,
        out_shape=jax.ShapeDtypeStruct((4 * SIDE + EXTRA, RANK), F32),
        in_specs=whole(2),
        out_specs=whole(1)[0],
        compiler_params=limits(6),
        name="core_sum",
    )(keep, came)


def inner_kernel(keep, came, a, b, c, out):
    scales = [jnp.exp2(one[pl.ds(4 * SIDE, 1), :]) for one in (a, b, c)]
    for i in range(out.shape[0]):
        summed = keep[i] + came[i]
        for one, scale in zip((a, b, c), scales):
            summed += one[pl.ds(SIDE * i, SIDE), :] * scale
        out[i] = summed.T.astype(BF16)


def inner_sum(keep, came, parts):
    return pl.pallas_call(
        inner_kernel,
        out_shape=jax.ShapeDtypeStruct((4, RANK, SIDE), BF16),
        in_specs=whole(5),
        out_specs=whole(1)[0],
        compiler_params=limits(6),
        name="inner_sum",
    )(keep, came, *parts)


def relay_kernel(total, a, b, right, left):
    right[...] = (total[pl.ds(16, 8)] + a[...].astype(F32)).astype(BF16)
    left[...] = (total[pl.ds(56, 8)] + b[...].astype(F32)).astype(BF16)


def relay_sum(total, came):
    part = jax.ShapeDtypeStruct((8, RANK, SIDE), BF16)
    return pl.pallas_call(
        relay_kernel,
        out_shape=(part, part),
        in_specs=whole(3),
        out_specs=tuple(whole(2)),
        compiler_params=limits(6),
        name="relay_sum",
    )(total, *came)


def middle_kernel(total, *rest):
    halves, (keep, *aways) = (rest[:2], rest[2:4]), rest[4:]
    for d in range(4):
        a, b = halves[d // 2]
        at = pl.ds(4 * (d % 2), 4)
        one = total[pl.ds(4 * d, 4)] + (a[at].astype(F32) + b[at].astype(F32))
        if d == 0:
            keep[...] = one
        else:
            aways[d - 1][...] = one.astype(BF16)


def middle_sum(total, came):
    part = jax.ShapeDtypeStruct((4, RANK, SIDE), BF16)
    keep, *aways = pl.pallas_call(
        middle_kernel,
        out_shape=(jax.ShapeDtypeStruct((4, RANK, SIDE), F32),) + (part,) * 3,
        in_specs=whole(5),
        out_specs=tuple(whole(4)),
        compiler_params=limits(6),
        name="middle_sum",
    )(total, *came)
    return keep, aways


def exact_dot(a, b, dims):
    return lax.dot_general(
        a, b, (dims, ((), ())), precision=lax.Precision.HIGHEST, preferred_element_type=F32
    )


def outer_kernel(keep, a, b, c, outer, gram):
    gram_total = jnp.zeros((RANK, RANK), F32)
    for i in range(outer.shape[0]):
        total = (keep[i] + a[i].astype(F32)) + (b[i].astype(F32) + c[i].astype(F32))
        outer[i] = total
        gram_total += exact_dot(total, total, ((1,), (1,)))
    gram[...] = gram_total


def outer_sum(keep, came):
    return pl.pallas_call(
        outer_kernel,
        out_shape=(
            jax.ShapeDtypeStruct((4, RANK, SIDE), F32),
            jax.ShapeDtypeStruct((RANK, RANK), F32),
        ),
        in_specs=whole(4),
        out_specs=tuple(whole(2)),
        compiler_params=limits(6),
        name="outer_sum",
    )(keep, *came)


def halved(value):
    large = value.astype(BF16)
    return large, (value - large.astype(F32)).astype(BF16)


def wide(value):
    return jnp.broadcast_to(value, (8, RANK))


def finish_kernel(scale, gram, outer, basis, factor, work):
    rows = lax.broadcasted_iota(jnp.int32, (RANK, RANK), 0)
    cols = lax.broadcasted_iota(jnp.int32, (RANK, RANK), 1)
    sub = lax.broadcasted_iota(jnp.int32, (8, RANK), 0)
    work[:, :RANK] = gram[...]
    work[:, RANK:] = jnp.where(rows == cols, 1.0, 0.0)
    for j in range(0, RANK, 8):
        halves = [work[j : j + 8, :RANK], work[j : j + 8, RANK:]]
        diag = [
            [wide(halves[0][r : r + 1, j + s : j + s + 1]) for s in range(r + 1)]
            for r in range(8)
        ]
        upper = [[wide(half[r : r + 1, :]) for half in halves] for r in range(8)]
        lower = [[None] * 8 for _ in range(8)]
        root = [None] * 8
        for i in range(8):
            root[i] = lax.rsqrt(diag[i][i])
            for r in range(i + 1, 8):
                lower[r][i] = diag[r][i] * root[i]
            for r in range(i + 1, 8):
                for s in range(i + 1, r + 1):
                    diag[r][s] = diag[r][s] - lower[r][i] * lower[s][i]
            upper[i] = [one * root[i] for one in upper[i]]
            for r in range(i + 1, 8):
                upper[r] = [a - lower[r][i] * b for a, b in zip(upper[r], upper[i])]
        for h in range(2):
            panel = upper[0][h]
            for r in range(1, 8):
                panel = jnp.where(sub == r, upper[r][h], panel)
            work[j : j + 8, h * RANK : (h + 1) * RANK] = panel
        for g in range(j + 8, RANK, 8):
            halves = [work[g : g + 8, :RANK], work[g : g + 8, RANK:]]
            column = []
            for k in range(8):
                one = wide(halves[0][:, j + k : j + k + 1])
                for i in range(k):
                    one = one - column[i] * lower[k][i]
                column.append(one * root[k])
            for h in range(2):
                block = halves[h]
                for k in range(8):
                    block = block - column[k] * upper[k][h]
                work[g : g + 8, h * RANK : (h + 1) * RANK] = block
    factor[...] = jnp.where(cols >= rows, work[:, :RANK], 0.0) * (1.0 / scale)
    inverse, rest = halved(work[:, RANK:] * scale)
    for b in range(outer.shape[0]):
        large, small = halved(outer[b])
        product = dot(inverse, large) + (dot(rest, large) + dot(inverse, small))
        basis[pl.ds(b * SIDE, SIDE), :] = product.T


def finish(gram, outer, entities):
    scale = float(entities) ** 0.5

    def kernel(*refs):
        finish_kernel(scale, *refs)

    return pl.pallas_call(
        kernel,
        out_shape=(
            jax.ShapeDtypeStruct((4 * SIDE, RANK), F32),
            jax.ShapeDtypeStruct((RANK, RANK), F32),
        ),
        in_specs=whole(2),
        out_specs=tuple(whole(2)),
        scratch_shapes=[pltpu.VMEM((RANK, 2 * RANK), F32)],
        compiler_params=limits(6),
        name="finish",
    )(gram, outer)


def shards(basis_in, tiles, tile_coords, tile_count):
    x, y, z, core = (lax.axis_index(name) for name in AXES)
    local_row = tile_coords[:, 0] - (x * 4 + y) * 32
    dz = (local_row // 8 - z) % 4
    dc = (local_row // 4 - core) % 2
    row_at = dc * 16 + dz * 4 + local_row % 4
    row_group = tile_coords[:, 1] // 32
    b = tile_coords[:, 1] % 4
    dx = (row_group // 4 - x) % 4
    dy = (row_group % 4 - y) % 4
    near_axes, far_axes = ("x", "y"), ("y", "x")
    near_at = jnp.where(core == 0, dx, dy)
    far_at = jnp.where(core == 0, dy, dx)
    col_at = far_at * 16 + near_at * 4 + b

    with jax.named_scope("gather_basis"):
        near = [basis_in] + [cross(basis_in, near_axes, -d) for d in (1, 2, 3)]
        held, counts, near_list, far_list = plan_tiles(tile_count, row_at, col_at, tiles)
        near, held = lax.optimization_barrier((near, held))
        low, high = (
            jnp.concatenate(pair, axis=0).reshape(8, SIDE, RANK) for pair in (near[:2], near[2:])
        )
        right_low, left_high = cross(low, far_axes, 1), cross(high, far_axes, -1)
        left_low, right_high = cross(low, far_axes, -1), cross(high, far_axes, 1)
        over = (cross(right_low, far_axes, 1), cross(left_high, far_axes, -1))

    held = hold_rest(tile_count, tiles, held)
    keep = forward_near(
        counts, near_list, held, (low, high, left_low, left_high, right_low, right_high)
    )
    keep, *aways = forward_far(counts, far_list, held, over, keep)

    with jax.named_scope("reduce_inner"):
        parts = []
        for d in (2, 1, 3):
            one = core_sum(keep, send(aways[d], "core", 1), d)
            parts.append(send(one.astype(jnp.float16), "z", d).astype(F32))
        inner = inner_sum(keep, send(aways[0], "core", 1), parts)

    with jax.named_scope("gather_inner"):
        mine = [inner] + [send(inner, "z", -d) for d in (1, 2, 3)]
        theirs = [send(one, "core", 1) for one in mine]

    aways = backward_far(counts, far_list, held, mine + theirs)

    with jax.named_scope("reduce_outer"):
        over = (cross(aways[0], far_axes, 1), cross(aways[1], far_axes, -1))
        total, right_high, left_low = backward_near(counts, near_list, held, mine + theirs)
        right_high, left_low = cross(right_high, far_axes, 1), cross(left_low, far_axes, -1)
        right_low, left_high = relay_sum(total, over)
        right_low, left_high = cross(right_low, far_axes, 1), cross(left_high, far_axes, -1)
        came = (right_low, left_low, right_high, left_high)
        keep, aways = middle_sum(total, came)
        came = [cross(one, near_axes, d) for d, one in zip((1, 2, 3), aways)]
        outer, gram = outer_sum(keep, came)

    with jax.named_scope("reduce_gram"):
        gram = gram + send(gram, "core", 1)
        for axis in ("z", "y", "x"):
            parts = [send(gram, axis, d) for d in (1, 2, 3)]
            gram = (gram + parts[1]) + (parts[0] + parts[2])

    entities = basis_in.shape[0] * 128
    return finish(gram, outer, entities)


def solution(mesh):
    split = Mesh(mesh.devices.reshape(4, 4, 4, 2), AXES)
    placed = (P(AXES, None), P(AXES, None, None), P(AXES, None), P(AXES))
    return jax.shard_map(
        shards,
        mesh=split,
        in_specs=placed,
        out_specs=(P(AXES, None), P()),
        check_vma=False,
    )
```

```python
import itertools

import jax
import jax.numpy as jnp
from jax import lax
from jax.experimental import pallas as pl
from jax.experimental.pallas import tpu as pltpu
from jax.sharding import Mesh, PartitionSpec as P

AXES = ("x", "y", "z", "core")
SIZES = {"x": 4, "y": 4, "z": 4, "core": 2}
SIDE = 256
RANK = 128
CHUNK = 32
EARLY = 3
EXTRA = 16
SPARE = 32 * 256 + 64 * 65536
F32 = jnp.float32
BF16 = jnp.bfloat16


def send(array, axis, step):
    size = SIZES[axis]
    return lax.ppermute(array, axis, [(i, (i + step) % size) for i in range(size)])


def cross(array, axes, step):
    names = AXES[:3]
    pairs = []
    for place in itertools.product(*(range(SIZES[name]) for name in AXES)):
        there = list(place)
        at = names.index(axes[place[3]])
        there[at] = (there[at] + step) % SIZES[names[at]]
        pairs.append((linear(place), linear(there)))
    return lax.ppermute(array, AXES, pairs)


def linear(place):
    index = 0
    for name, one in zip(AXES, place):
        index = index * SIZES[name] + one
    return index


def limits(mib):
    return pltpu.CompilerParams(vmem_limit_bytes=mib * 1024 * 1024)


def whole(count):
    return [pl.BlockSpec(memory_space=pltpu.VMEM)] * count


def load_pieces(pieces, held, sems):
    copies = []
    at = 0
    for i, piece in enumerate(pieces):
        rows = piece.shape[0]
        copies.append(pltpu.make_async_copy(piece, held.at[pl.ds(at, rows)], sems.at[i]))
        at += rows
    for copy in copies:
        copy.start()
    return copies


def hold_copies(count, tiles, held, sems, first, last):
    end = jnp.clip((count[0] + CHUNK - 1) // CHUNK, first, last)

    def copy(i):
        at = pl.ds(i * CHUNK, CHUNK)
        return pltpu.make_async_copy(tiles.at[at], held.at[at], sems.at[i])

    def start(i, _):
        copy(i).start()
        return 0

    def wait(i, _):
        copy(i).wait()
        return 0

    return (lambda: lax.fori_loop(first, end, start, 0)), (
        lambda: lax.fori_loop(first, end, wait, 0)
    )


def rest_kernel(count, tiles, before, held, sems):
    start, wait = hold_copies(count, tiles, held, sems, EARLY, sems.shape[0])
    start()
    wait()


def plan_kernel(count, row_at, col_at, tiles, held, counts, near, far, sems):
    start, wait = hold_copies(count, tiles, held, sems, 0, EARLY)
    start()

    def place(slot, ends):
        near_end, far_end = ends
        col = col_at[slot]
        entry = slot + row_at[slot] * 256 + col * 65536
        near[near_end] = entry
        far[far_end] = entry
        over = (col >> 4 == 2).astype(jnp.int32)
        return near_end + 1 - over, far_end + over

    zero = jnp.int32(0)
    near_end, far_end = lax.fori_loop(0, count[0], place, (zero, zero))
    for k in range(CHUNK):
        near[near_end + k] = SPARE
        far[far_end + k] = SPARE
    counts[0] = near_end
    counts[1] = far_end
    wait()


def hold_parameters(tiles):
    return dict(
        scratch_shapes=[pltpu.SemaphoreType.DMA((tiles.shape[0] // CHUNK,))],
        compiler_params=limits(22),
        cost_estimate=pl.CostEstimate(
            flops=0, bytes_accessed=2 * tiles.size * tiles.dtype.itemsize, transcendentals=0
        ),
    )


def scalars(count):
    return [pl.BlockSpec(memory_space=pltpu.SMEM)] * count


def anywhere(count):
    return [pl.BlockSpec(memory_space=pl.ANY)] * count


def plan_tiles(count, row_at, col_at, tiles):
    entries = jax.ShapeDtypeStruct((tiles.shape[0] + CHUNK,), jnp.int32)
    return pl.pallas_call(
        plan_kernel,
        out_shape=(
            jax.ShapeDtypeStruct(tiles.shape, tiles.dtype),
            jax.ShapeDtypeStruct((2,), jnp.int32),
            entries,
            entries,
        ),
        in_specs=scalars(3) + anywhere(1),
        out_specs=tuple(whole(1) + scalars(3)),
        name="plan_tiles",
        **hold_parameters(tiles),
    )(count, row_at, col_at, tiles)


def hold_rest(count, tiles, held):
    return pl.pallas_call(
        rest_kernel,
        out_shape=jax.ShapeDtypeStruct(tiles.shape, tiles.dtype),
        in_specs=scalars(1) + anywhere(1) + whole(1),
        out_specs=whole(1)[0],
        input_output_aliases={2: 0},
        name="hold_rest",
        **hold_parameters(tiles),
    )(count, tiles, held)


def listed(total, entries, chunk, body):
    def step(i, _):
        for k in range(chunk):
            entry = entries[i * chunk + k]
            body(entry & 255, (entry >> 8) & 255, entry >> 16)
        return 0

    lax.fori_loop(0, (total + chunk - 1) // chunk, step, 0)


def dot(a, b):
    return jnp.dot(a, b, preferred_element_type=F32)


def product_cost(share):
    return pl.CostEstimate(
        flops=int(share * 160 * 2 * SIDE * SIDE * RANK), bytes_accessed=1 << 20, transcendentals=0
    )


def forward_near_kernel(counts, near, tiles, *rest):
    pieces, (total, held, sems) = rest[:6], rest[6:]
    copies = []
    for i, at in enumerate((0, 8, 16, 24, 48, 56)):
        copies.append(pltpu.make_async_copy(pieces[i], held.at[pl.ds(at, 8)], sems.at[i]))
    for one in copies:
        one.start()
    total[...] = jnp.zeros_like(total)
    for one in copies:
        one.wait()

    def body(slot, row, col):
        total[row] += dot(tiles[slot], held[col])

    listed(counts[0], near, 32, body)


def forward_near(counts, near, tiles, pieces):
    return pl.pallas_call(
        forward_near_kernel,
        out_shape=jax.ShapeDtypeStruct((33, SIDE, RANK), F32),
        in_specs=scalars(2) + whole(1) + anywhere(6),
        out_specs=whole(1)[0],
        scratch_shapes=[
            pltpu.VMEM((65, SIDE, RANK), BF16),
            pltpu.SemaphoreType.DMA((6,)),
        ],
        compiler_params=limits(8),
        cost_estimate=product_cost(0.75),
        name="forward_near",
    )(counts, near, tiles, *pieces)


def forward_far_kernel(counts, far, tiles, a, b, before, total, *rest):
    *aways, held = rest
    held[pl.ds(0, 8)] = a[...]
    held[pl.ds(8, 8)] = b[...]

    def body(slot, row, col):
        total[row] += dot(tiles[slot], held[jnp.minimum(col - 32, 16)])

    listed(counts[1], far, 16, body)
    for d, away in enumerate(aways):
        away[...] = total[pl.ds(16 + 4 * d, 4)]


def forward_far(counts, far, tiles, pieces, before):
    return pl.pallas_call(
        forward_far_kernel,
        out_shape=(jax.ShapeDtypeStruct((33, SIDE, RANK), F32),)
        + (jax.ShapeDtypeStruct((4, SIDE, RANK), F32),) * 4,
        in_specs=scalars(2) + whole(4),
        out_specs=tuple(whole(5)),
        scratch_shapes=[pltpu.VMEM((17, SIDE, RANK), BF16)],
        input_output_aliases={5: 0},
        compiler_params=limits(4),
        name="forward_far",
    )(counts, far, tiles, *pieces, before)


def backward_far_kernel(counts, far, tiles, *rest):
    pieces, (a, b, held, total) = rest[:8], rest[8:]
    total[...] = jnp.zeros_like(total)
    for i, piece in enumerate(pieces):
        held[pl.ds(4 * i, 4)] = piece[...]

    def body(slot, row, col):
        total[jnp.minimum(col - 32, 16)] += dot(held[row], tiles[slot])

    listed(counts[1], far, 16, body)
    a[...] = total[pl.ds(0, 8)].astype(BF16)
    b[...] = total[pl.ds(8, 8)].astype(BF16)


def backward_far(counts, far, tiles, pieces):
    part = jax.ShapeDtypeStruct((8, RANK, SIDE), BF16)
    return pl.pallas_call(
        backward_far_kernel,
        out_shape=(part, part),
        in_specs=scalars(2) + whole(9),
        out_specs=tuple(whole(2)),
        scratch_shapes=[
            pltpu.VMEM((33, RANK, SIDE), BF16),
            pltpu.VMEM((17, RANK, SIDE), F32),
        ],
        compiler_params=limits(8),
        name="backward_far",
    )(counts, far, tiles, *pieces)


def backward_near_kernel(counts, near, tiles, *rest):
    pieces, (total, right, left, held, sems) = rest[:8], rest[8:]
    copies = load_pieces(pieces, held, sems)
    total[pl.ds(0, 32)] = jnp.zeros((32, RANK, SIDE), F32)
    total[pl.ds(48, 17)] = jnp.zeros((17, RANK, SIDE), F32)
    for one in copies:
        one.wait()

    def body(slot, row, col):
        total[col] += dot(held[row], tiles[slot])

    listed(counts[0], near, 32, body)
    right[...] = total[pl.ds(24, 8)].astype(BF16)
    left[...] = total[pl.ds(48, 8)].astype(BF16)


def backward_near(counts, near, tiles, pieces):
    part = jax.ShapeDtypeStruct((8, RANK, SIDE), BF16)
    return pl.pallas_call(
        backward_near_kernel,
        out_shape=(jax.ShapeDtypeStruct((65, RANK, SIDE), F32), part, part),
        in_specs=scalars(2) + whole(1) + anywhere(8),
        out_specs=tuple(whole(3)),
        scratch_shapes=[
            pltpu.VMEM((33, RANK, SIDE), BF16),
            pltpu.SemaphoreType.DMA((8,)),
        ],
        compiler_params=limits(6),
        cost_estimate=product_cost(0.75),
        name="backward_near",
    )(counts, near, tiles, *pieces)


def core_sum(keep, came, d):
    def kernel(keep, came, out):
        total = keep[pl.ds(4 * d, 4)] + came[...]
        largest = jnp.max(jnp.abs(total), axis=0)
        largest = jnp.max(jnp.max(largest, axis=0, keepdims=True), axis=1, keepdims=True)
        power = jnp.floor(jnp.log2(jnp.maximum(largest, 1e-30))) - 13.0
        scale = jnp.exp2(-power)
        for i in range(4):
            out[pl.ds(SIDE * i, SIDE), :] = total[i] * scale
        out[pl.ds(4 * SIDE, EXTRA), :] = jnp.broadcast_to(power, (EXTRA, RANK))

    return pl.pallas_call(
        kernel,
        out_shape=jax.ShapeDtypeStruct((4 * SIDE + EXTRA, RANK), F32),
        in_specs=whole(2),
        out_specs=whole(1)[0],
        compiler_params=limits(6),
        name="core_sum",
    )(keep, came)


def inner_kernel(keep, came, a, b, c, out):
    scales = [jnp.exp2(one[pl.ds(4 * SIDE, 1), :]) for one in (a, b, c)]
    for i in range(out.shape[0]):
        summed = keep[i] + came[i]
        for one, scale in zip((a, b, c), scales):
            summed += one[pl.ds(SIDE * i, SIDE), :] * scale
        out[i] = summed.T.astype(BF16)


def inner_sum(keep, came, parts):
    return pl.pallas_call(
        inner_kernel,
        out_shape=jax.ShapeDtypeStruct((4, RANK, SIDE), BF16),
        in_specs=whole(5),
        out_specs=whole(1)[0],
        compiler_params=limits(6),
        name="inner_sum",
    )(keep, came, *parts)


def relay_kernel(total, a, b, right, left):
    right[...] = (total[pl.ds(16, 8)] + a[...].astype(F32)).astype(BF16)
    left[...] = (total[pl.ds(56, 8)] + b[...].astype(F32)).astype(BF16)


def relay_sum(total, came):
    part = jax.ShapeDtypeStruct((8, RANK, SIDE), BF16)
    return pl.pallas_call(
        relay_kernel,
        out_shape=(part, part),
        in_specs=whole(3),
        out_specs=tuple(whole(2)),
        compiler_params=limits(6),
        name="relay_sum",
    )(total, *came)


def middle_kernel(total, *rest):
    halves, (keep, *aways) = (rest[:2], rest[2:4]), rest[4:]
    for d in range(4):
        a, b = halves[d // 2]
        at = pl.ds(4 * (d % 2), 4)
        one = total[pl.ds(4 * d, 4)] + (a[at].astype(F32) + b[at].astype(F32))
        if d == 0:
            keep[...] = one
        else:
            aways[d - 1][...] = one.astype(BF16)


def middle_sum(total, came):
    part = jax.ShapeDtypeStruct((4, RANK, SIDE), BF16)
    keep, *aways = pl.pallas_call(
        middle_kernel,
        out_shape=(jax.ShapeDtypeStruct((4, RANK, SIDE), F32),) + (part,) * 3,
        in_specs=whole(5),
        out_specs=tuple(whole(4)),
        compiler_params=limits(6),
        name="middle_sum",
    )(total, *came)
    return keep, aways


def exact_dot(a, b, dims):
    return lax.dot_general(
        a, b, (dims, ((), ())), precision=lax.Precision.HIGHEST, preferred_element_type=F32
    )


def outer_kernel(keep, a, b, c, outer, gram):
    gram_total = jnp.zeros((RANK, RANK), F32)
    for i in range(outer.shape[0]):
        total = (keep[i] + a[i].astype(F32)) + (b[i].astype(F32) + c[i].astype(F32))
        outer[i] = total
        gram_total += exact_dot(total, total, ((1,), (1,)))
    gram[...] = gram_total


def outer_sum(keep, came):
    return pl.pallas_call(
        outer_kernel,
        out_shape=(
            jax.ShapeDtypeStruct((4, RANK, SIDE), F32),
            jax.ShapeDtypeStruct((RANK, RANK), F32),
        ),
        in_specs=whole(4),
        out_specs=tuple(whole(2)),
        compiler_params=limits(6),
        name="outer_sum",
    )(keep, *came)


def halved(value):
    large = value.astype(BF16)
    return large, (value - large.astype(F32)).astype(BF16)


def wide(value):
    return jnp.broadcast_to(value, (8, RANK))


def finish_kernel(scale, gram, outer, basis, factor, work):
    rows = lax.broadcasted_iota(jnp.int32, (RANK, RANK), 0)
    cols = lax.broadcasted_iota(jnp.int32, (RANK, RANK), 1)
    sub = lax.broadcasted_iota(jnp.int32, (8, RANK), 0)
    work[:, :RANK] = gram[...]
    work[:, RANK:] = jnp.where(rows == cols, 1.0, 0.0)
    for j in range(0, RANK, 8):
        halves = [work[j : j + 8, :RANK], work[j : j + 8, RANK:]]
        diag = [
            [wide(halves[0][r : r + 1, j + s : j + s + 1]) for s in range(r + 1)]
            for r in range(8)
        ]
        upper = [[wide(half[r : r + 1, :]) for half in halves] for r in range(8)]
        lower = [[None] * 8 for _ in range(8)]
        root = [None] * 8
        for i in range(8):
            root[i] = lax.rsqrt(diag[i][i])
            for r in range(i + 1, 8):
                lower[r][i] = diag[r][i] * root[i]
            for r in range(i + 1, 8):
                for s in range(i + 1, r + 1):
                    diag[r][s] = diag[r][s] - lower[r][i] * lower[s][i]
            upper[i] = [one * root[i] for one in upper[i]]
            for r in range(i + 1, 8):
                upper[r] = [a - lower[r][i] * b for a, b in zip(upper[r], upper[i])]
        for h in range(2):
            panel = upper[0][h]
            for r in range(1, 8):
                panel = jnp.where(sub == r, upper[r][h], panel)
            work[j : j + 8, h * RANK : (h + 1) * RANK] = panel
        for g in range(j + 8, RANK, 8):
            halves = [work[g : g + 8, :RANK], work[g : g + 8, RANK:]]
            column = []
            for k in range(8):
                one = wide(halves[0][:, j + k : j + k + 1])
                for i in range(k):
                    one = one - column[i] * lower[k][i]
                column.append(one * root[k])
            for h in range(2):
                block = halves[h]
                for k in range(8):
                    block = block - column[k] * upper[k][h]
                work[g : g + 8, h * RANK : (h + 1) * RANK] = block
    factor[...] = jnp.where(cols >= rows, work[:, :RANK], 0.0) * (1.0 / scale)
    inverse, rest = halved(work[:, RANK:] * scale)
    for b in range(outer.shape[0]):
        large, small = halved(outer[b])
        product = dot(inverse, large) + (dot(rest, large) + dot(inverse, small))
        basis[pl.ds(b * SIDE, SIDE), :] = product.T


def finish(gram, outer, entities):
    scale = float(entities) ** 0.5

    def kernel(*refs):
        finish_kernel(scale, *refs)

    return pl.pallas_call(
        kernel,
        out_shape=(
            jax.ShapeDtypeStruct((4 * SIDE, RANK), F32),
            jax.ShapeDtypeStruct((RANK, RANK), F32),
        ),
        in_specs=whole(2),
        out_specs=tuple(whole(2)),
        scratch_shapes=[pltpu.VMEM((RANK, 2 * RANK), F32)],
        compiler_params=limits(6),
        name="finish",
    )(gram, outer)


def shards(basis_in, tiles, tile_coords, tile_count):
    x, y, z, core = (lax.axis_index(name) for name in AXES)
    local_row = tile_coords[:, 0] - (x * 4 + y) * 32
    dz = (local_row // 8 - z) % 4
    dc = (local_row // 4 - core) % 2
    row_at = dc * 16 + dz * 4 + local_row % 4
    row_group = tile_coords[:, 1] // 32
    b = tile_coords[:, 1] % 4
    dx = (row_group // 4 - x) % 4
    dy = (row_group % 4 - y) % 4
    near_axes, far_axes = ("x", "y"), ("y", "x")
    near_at = jnp.where(core == 0, dx, dy)
    far_at = jnp.where(core == 0, dy, dx)
    col_at = far_at * 16 + near_at * 4 + b

    with jax.named_scope("gather_basis"):
        near = [basis_in] + [cross(basis_in, near_axes, -d) for d in (1, 2, 3)]
        held, counts, near_list, far_list = plan_tiles(tile_count, row_at, col_at, tiles)
        near, held = lax.optimization_barrier((near, held))
        low, high = (
            jnp.concatenate(pair, axis=0).reshape(8, SIDE, RANK) for pair in (near[:2], near[2:])
        )
        right_low, left_high = cross(low, far_axes, 1), cross(high, far_axes, -1)
        left_low, right_high = cross(low, far_axes, -1), cross(high, far_axes, 1)
        over = (cross(right_low, far_axes, 1), cross(left_high, far_axes, -1))

    held = hold_rest(tile_count, tiles, held)
    keep = forward_near(
        counts, near_list, held, (low, high, left_low, left_high, right_low, right_high)
    )
    keep, *aways = forward_far(counts, far_list, held, over, keep)

    with jax.named_scope("reduce_inner"):
        parts = []
        for d in (2, 1, 3):
            one = core_sum(keep, send(aways[d], "core", 1), d)
            parts.append(send(one.astype(jnp.float16), "z", d).astype(F32))
        inner = inner_sum(keep, send(aways[0], "core", 1), parts)

    with jax.named_scope("gather_inner"):
        mine = [inner] + [send(inner, "z", -d) for d in (1, 2, 3)]
        theirs = [send(one, "core", 1) for one in mine]

    aways = backward_far(counts, far_list, held, mine + theirs)

    with jax.named_scope("reduce_outer"):
        over = (cross(aways[0], far_axes, 1), cross(aways[1], far_axes, -1))
        total, right_high, left_low = backward_near(counts, near_list, held, mine + theirs)
        right_high, left_low = cross(right_high, far_axes, 1), cross(left_low, far_axes, -1)
        right_low, left_high = relay_sum(total, over)
        right_low, left_high = cross(right_low, far_axes, 1), cross(left_high, far_axes, -1)
        came = (right_low, left_low, right_high, left_high)
        keep, aways = middle_sum(total, came)
        came = [cross(one, near_axes, d) for d, one in zip((1, 2, 3), aways)]
        outer, gram = outer_sum(keep, came)

    with jax.named_scope("reduce_gram"):
        gram = gram + send(gram, "core", 1)
        for axis in ("z", "y", "x"):
            parts = [send(gram, axis, d) for d in (1, 2, 3)]
            gram = (gram + parts[1]) + (parts[0] + parts[2])

    entities = basis_in.shape[0] * 128
    return finish(gram, outer, entities)


def solution(mesh):
    split = Mesh(mesh.devices.reshape(4, 4, 4, 2), AXES)
    placed = (P(AXES, None), P(AXES, None, None), P(AXES, None), P(AXES))
    return jax.shard_map(
        shards,
        mesh=split,
        in_specs=placed,
        out_specs=(P(AXES, None), P()),
        check_vma=False,
    )
```
